32 devices in a mesh: branch: 4 (over x, core), col: 8 (over z, y).
Axes of the slice: x: 2, y: 2, z: 4, core: 2. Of those that a mesh axis runs over, the one named last changes fastest.
Arguments:
- child_fronts: float32 [4, 4096, 4096], P('branch', None, 'col'), as said below
- extend_map: int32 [4, 14], P('branch'), may hold values from 0 to 15, as said below
- parent_front: float32 [4096, 4096], P('branch', 'col'), as said below
Outputs:
- child_factor: float32 [4, 512, 4096], P('branch', None, 'col')
- parent_factor: float32 [512, 4096], P(None, 'col')
- parent_update: float32 [4096, 4096], P('branch', 'col')
The draws below stay inside these ranges and needn't reach their ends.
Inputs may be any that keep to these rules, and one draw needn't show every extreme that they name: Each row of extend_map names 14 different parent blocks; some row names block 0 and some row names block 15. `child_fronts`: each child front is symmetric and positive definite. `parent_front`: the parent front is symmetric and positive definite.
All inputs are finite; a program needn't handle non-finite values.
Results may differ from the reference program's by a relative error of at most 0.0003.
Values sent between devices are 32-bit elements; how exact they have to be, the bound alone decides.
No kernel may reach another device: no remote copies, remote signals or barrier semaphores. Data moves between devices by JAX's collectives and lax.ppermute only.
A program may use at most 128 MiB of HBM per device.

```python
import jax
import jax.numpy as jnp
from jax import lax

BS = 256
NC = 4096
P_SIZE = 512
NP = 4096
PP = 512
UB = 14
NPB = 16
CHILDREN = 4


def gram_front(key, count, order, inner, gain):
    key_factor, key_diag = jax.random.split(key, 2)
    factors = jax.random.randint(key_factor, (count, order, inner), -2, 3).astype(jnp.float32)

    def one_gram(factor):
        return jnp.dot(factor, factor.T, precision=lax.Precision.HIGHEST)
    gram = lax.map(one_gram, factors)
    diag = jax.random.uniform(key_diag, (count, order), jnp.float32, 0.1, 0.4)
    eye = (jnp.arange(order)[:, None] == jnp.arange(order)[None, :]).astype(jnp.float32)
    front = gain / (2.0 * inner) * gram + gain * eye[None] * diag[:, :, None]
    return front


def draw_child_fronts(key, part):
    return gram_front(jax.random.fold_in(key, 11), CHILDREN, NC, NC // 2, 1.0)


def draw_parent_front(key, part):
    return gram_front(jax.random.fold_in(key, 23), 1, NP, NP // 4, 4.0)[0]


def draw_extend_map(key, part):
    keys = jax.random.split(jax.random.fold_in(key, 37), CHILDREN)
    targets = jnp.where(jnp.arange(CHILDREN) % 2 == 0, NPB - 1, 0).astype(jnp.int32)

    def one_row(row_key, target):
        order = jax.random.permutation(row_key, NPB).astype(jnp.int32)
        where_target = jnp.argmax(order == target).astype(jnp.int32)
        return jnp.roll(order, -where_target)[:UB]
    return jax.vmap(one_row)(keys, targets)


def setup_inputs(seed: int = 0) -> dict:
    seeds = jax.random.split(jax.random.key(seed), 4)
    child_fronts = draw_child_fronts(jax.random.fold_in(seeds[3], 71), 0)
    extend_map = draw_extend_map(jax.random.fold_in(seeds[3], 71), 0)
    parent_front = draw_parent_front(jax.random.fold_in(seeds[3], 71), 0)
    return {"child_fronts": child_fronts, "extend_map": extend_map, "parent_front": parent_front}


def outer_rows(left, right):
    return lax.dot_general(left, right, (((0,), (0,)), ((), ())), precision=lax.Precision.HIGHEST)

def solve_lower(lower_factor, rhs):
    return lax.linalg.triangular_solve(lower_factor, rhs, left_side=True, lower=True)

def source_table(blocks):
    hit = blocks[:, None] == jnp.arange(NPB, dtype=jnp.int32)[None, :]
    present = jnp.any(hit, axis=0)
    child_block = jnp.sum(jnp.where(hit, jnp.arange(UB, dtype=jnp.int32)[:, None], 0), axis=0).astype(jnp.int32)
    positions = jnp.arange(NP, dtype=jnp.int32)
    source = (child_block[positions // BS] * BS + positions % BS).astype(jnp.int32)
    keep = present[positions // BS].astype(jnp.float32)
    return (source, keep)

def reference(child_fronts, extend_map, parent_front):

    def one_child(total, inputs):
        front, blocks = inputs
        top = front[:P_SIZE]
        lower_factor = jnp.linalg.cholesky(top[:, :P_SIZE])
        factor = solve_lower(lower_factor, top)
        tail = factor[:, P_SIZE:]
        update = front[P_SIZE:, P_SIZE:] - outer_rows(tail, tail)
        source, keep = source_table(blocks)
        spread = jnp.take(jnp.take(update, source, axis=0), source, axis=1)
        spread = spread * keep[:, None] * keep[None, :]
        return (total + spread, factor)
    summed, factors = lax.scan(one_child, jnp.zeros((NP, NP), jnp.float32), (child_fronts, extend_map))
    assembled = parent_front + summed
    ptop = assembled[:PP]
    plower = jnp.linalg.cholesky(ptop[:, :PP])
    pfactor = solve_lower(plower, ptop)
    pupdate = assembled - outer_rows(pfactor, pfactor)
    return (factors, pfactor, pupdate)
```

```python
import jax
import jax.numpy as jnp
from jax import lax
from jax.experimental import pallas as pl
from jax.experimental.pallas import tpu as pltpu
from jax.sharding import PartitionSpec as P

BS = 256
P_SIZE = 512
NP = 4096
PP = 512

SUB = 8
LANES = 128
F32 = jnp.float32


def mm(a, b, ca, cb):
    return lax.dot_general(
        a, b, (((ca,), (cb,)), ((), ())),
        precision=lax.Precision.HIGHEST, preferred_element_type=F32,
    )


def factor_tile(rows):
    sub = lax.broadcasted_iota(jnp.int32, (SUB, LANES), 0)
    lane = lax.broadcasted_iota(jnp.int32, (SUB, LANES), 1)
    rows = list(rows)
    count = len(rows)
    spread = lambda column: jnp.broadcast_to(column, (SUB, LANES))
    for g in range(count):
        base = g * SUB
        inside = (lane >= base) & (lane < base + SUB)
        cols = [spread(rows[g][:, base + j:base + j + 1]) for j in range(SUB)]
        panel = jnp.where(inside, jnp.where(lane - base == sub, 1.0, 0.0), rows[g])
        kept = panel
        pivots = cols[0]
        for j in range(SUB):
            here = sub == j
            pivot = spread(cols[j][j:j + 1, :])
            inverse = 1.0 / pivot
            scaled = cols[j] * inverse
            row = spread(panel[j:j + 1, :])
            kept = jnp.where(here, panel, kept)
            pivots = jnp.where(here, pivot, pivots)
            panel = jnp.where(here, row * inverse, panel - scaled * row)
            for m in range(j + 1, SUB):
                across = spread(cols[m][j:j + 1, :])
                cols[m] = jnp.where(here, across * inverse, cols[m] - scaled * across)
        rows[g] = kept * lax.rsqrt(pivots)
        panel_rows = [spread(panel[j:j + 1, :]) for j in range(SUB)]
        for i in range(g + 1, count):
            terms = [spread(rows[i][:, base + j:base + j + 1]) * panel_rows[j] for j in range(SUB)]
            while len(terms) > 1:
                terms = [terms[t] + terms[t + 1] for t in range(0, len(terms), 2)]
            rows[i] = jnp.where(inside, 0.0, rows[i]) - terms[0]
    return rows


def inverse_factor_kernel(a_ref, w_ref):
    n = a_ref.shape[0]
    steps = n // LANES
    tri = (lax.broadcasted_iota(jnp.int32, (LANES, LANES), 0)
           >= lax.broadcasted_iota(jnp.int32, (LANES, LANES), 1))
    work = [[a_ref[i * LANES:(i + 1) * LANES, j * LANES:(j + 1) * LANES]
             for j in range(steps)] for i in range(steps)]
    for k in range(steps):
        tile = work[k][k]
        done = factor_tile([tile[g * SUB:(g + 1) * SUB, :] for g in range(LANES // SUB)])
        inv = jnp.where(tri, jnp.concatenate(done, axis=0), 0.0)
        work[k] = [inv if j == k else mm(inv, work[k][j], 1, 0) for j in range(steps)]
        for i in range(k + 1, steps):
            left = work[k][i]
            for j in range(steps):
                product = mm(left, work[k][j], 0, 0)
                work[i][j] = -product if j == k else work[i][j] - product
    for i in range(steps):
        for j in range(steps):
            value = work[i][j] if j <= i else jnp.zeros((LANES, LANES), F32)
            w_ref[i * LANES:(i + 1) * LANES, j * LANES:(j + 1) * LANES] = value


def inverse_factor(a):
    n = a.shape[0]
    return pl.pallas_call(
        inverse_factor_kernel,
        out_shape=jax.ShapeDtypeStruct((n, n), F32),
        in_specs=[pl.BlockSpec(memory_space=pltpu.VMEM)],
        out_specs=pl.BlockSpec(memory_space=pltpu.VMEM),
        compiler_params=pltpu.CompilerParams(vmem_limit_bytes=32 * 1024 * 1024),
        cost_estimate=pl.CostEstimate(flops=n * n * n, bytes_accessed=8 * n * n, transcendentals=0),
    )(a)


def split(x):
    high = x.astype(jnp.bfloat16)
    return high, (x - high.astype(F32)).astype(jnp.bfloat16)


def spread_kernel(unit_ref, slot_ref, part_ref, keep_ref, high_ref, low_ref, factor_ref, piece_ref, out_ref):
    t = pl.program_id(0)
    high, low = split(factor_ref[...])
    dims = (((1,), (0,)), ((), ()))
    dot = lambda a, b: lax.dot_general(a, b, dims, preferred_element_type=F32)
    product = dot(high_ref[...], high) + dot(high_ref[...], low) + dot(low_ref[...], high)
    value = piece_ref[0] - product
    out_ref[0] = jnp.where(keep_ref[t] > 0, value, 0.0)


def spread_update(units, slots, parts, keeps, mine_t, factor, pieces, width):
    high, low = split(mine_t)
    count = units.shape[0]
    q, depth = mine_t.shape
    whole = lambda t, *refs: (0, 0)
    return pl.pallas_call(
        spread_kernel,
        grid_spec=pltpu.PrefetchScalarGridSpec(
            num_scalar_prefetch=4,
            grid=(count,),
            in_specs=[
                pl.BlockSpec((q, depth), whole),
                pl.BlockSpec((q, depth), whole),
                pl.BlockSpec((depth, width), lambda t, u, s, h, k: (0, u[t])),
                pl.BlockSpec((1, q, width), lambda t, u, s, h, k: (s[t], 0, h[t])),
            ],
            out_specs=pl.BlockSpec((1, q, width), lambda t, u, s, h, k: (t, 0, 0)),
        ),
        out_shape=jax.ShapeDtypeStruct((count, q, width), F32),
        compiler_params=pltpu.CompilerParams(vmem_limit_bytes=32 * 1024 * 1024),
        cost_estimate=pl.CostEstimate(
            flops=6 * count * q * depth * width,
            bytes_accessed=4 * count * width * (2 * q + depth), transcendentals=0),
    )(units, slots, parts, keeps, high, low, factor, pieces)


def product(a, b, ca, cb, precision=lax.Precision.HIGH):
    return lax.dot_general(a, b, (((ca,), (cb,)), ((), ())), precision=precision)


def on_device(child_fronts, extend_map, parent_front):
    front = child_fronts[0]
    order, ncols = front.shape
    nrows, pcols = parent_front.shape
    groups = lax.axis_size("col")
    width = min(BS, ncols)
    per = ncols // width
    ratio = BS // width
    units_total = NP // width
    col = lax.axis_index("col")
    branch = lax.axis_index("branch")
    pivot_devices = P_SIZE // ncols

    blocks = extend_map[0]
    hit = blocks[:, None] == jnp.arange(NP // BS, dtype=jnp.int32)[None, :]
    present = jnp.any(hit, axis=0).astype(jnp.int32)
    child_block = jnp.sum(
        jnp.where(hit, jnp.arange(blocks.shape[0], dtype=jnp.int32)[:, None], 0), axis=0
    ).astype(jnp.int32)
    t = jnp.arange(units_total, dtype=jnp.int32)
    units = P_SIZE // width + child_block[t // ratio] * ratio + t % ratio
    keeps = present[t // ratio]

    def rows_of(target):
        parts = [
            lax.dynamic_slice_in_dim(front, units[target * per + a] * width, width, 0)
            for a in range(per)
        ]
        return jnp.concatenate(parts, axis=0) if per > 1 else parts[0]

    def placed(x):
        if pivot_devices == 1:
            return jnp.where(col == 0, x, 0.0)
        wide = jnp.zeros((x.shape[0], P_SIZE), F32)
        wide = lax.dynamic_update_slice_in_dim(wide, x, jnp.minimum(col, pivot_devices - 1) * ncols, 1)
        return jnp.where(col < pivot_devices, wide, 0.0)

    pivots = lax.psum(placed(front[:P_SIZE]), "col")

    pivot_units = PP // width

    def pivot_column(b):
        local = units[b] - col * per
        ok = (local >= 0) & (local < per) & (keeps[b] > 0)
        column = lax.dynamic_slice_in_dim(front, jnp.clip(local, 0, per - 1) * width, width, 1)
        head = column[:P_SIZE]
        body = [
            jnp.where(keeps[a] > 0, lax.dynamic_slice_in_dim(column, units[a] * width, width, 0), 0.0)
            for a in range(pivot_units)
        ]
        return jnp.where(ok, jnp.concatenate([head] + body, axis=0), 0.0)

    corner = jnp.concatenate([pivot_column(b) for b in range(pivot_units)], axis=1)
    own = jnp.where(branch == 0, placed(parent_front[:PP]), 0.0)
    corner = corner + jnp.concatenate([jnp.zeros((P_SIZE, PP), F32), own], axis=0)
    corner = lax.psum(corner, "col")

    received = [rows_of(col)]
    for shift in range(1, groups):
        pairs = [(c, (c + shift) % groups) for c in range(groups) if c >= pivot_devices]
        received.append(lax.ppermute(rows_of((col + shift) % groups), "col", pairs))
    pieces = jnp.stack(received)

    top = lax.all_gather(front[:P_SIZE], "col", axis=1, tiled=True)

    inverse = inverse_factor(pivots)
    child_mine = product(inverse, front[:P_SIZE], 1, 0)

    gpiv = product(inverse, corner[:P_SIZE], 1, 0)
    pblock = corner[P_SIZE:] - product(gpiv, gpiv, 0, 0)
    pblock = lax.psum(pblock, "branch")

    factor = product(inverse, top, 1, 0)
    mine = [
        jnp.where(
            keeps[col * per + a] > 0,
            lax.dynamic_slice_in_dim(factor, units[col * per + a] * width, width, 1), 0.0)
        for a in range(per)
    ]
    mine_t = jnp.concatenate(mine, axis=1).T
    mine_keep = jnp.repeat(lax.dynamic_slice_in_dim(keeps, col * per, per), width)
    pieces = jnp.where((mine_keep > 0)[None, :, None], pieces, 0.0)
    source = units // per
    slots = (col - source + groups) % groups
    spread = spread_update(units, slots, units % per, keeps, mine_t, factor, pieces, width)
    summed = lax.psum_scatter(spread, "branch", scatter_dimension=0, tiled=True)
    summed, _ = lax.optimization_barrier((summed, pblock))
    assembled = parent_front + jnp.transpose(summed, (0, 2, 1)).reshape(nrows, pcols)

    top_mine = lax.psum(jnp.where(branch == 0, assembled[:PP], 0.0), "branch")
    side = lax.psum(placed(assembled), "col")

    pinverse = inverse_factor(pblock)
    parent_mine = product(pinverse, top_mine, 1, 0)
    row_factor = product(side, pinverse, 1, 1)
    result = assembled - product(row_factor, parent_mine, 1, 0)
    return (child_mine[None], parent_mine, result)


def solution(mesh):
    in_specs = (P("branch", None, "col"), P("branch", None), P("branch", "col"))
    out_specs = (P("branch", None, "col"), P(None, "col"), P("branch", "col"))
    return jax.shard_map(
        on_device, mesh=mesh, in_specs=in_specs, out_specs=out_specs, check_vma=False
    )
```

```python
import jax
import jax.numpy as jnp
from jax import lax
from jax.experimental import pallas as pl
from jax.experimental.pallas import tpu as pltpu
from jax.sharding import PartitionSpec as P

BS = 256
P_SIZE = 512
NP = 4096
PP = 512

SUB = 8
LANES = 128
F32 = jnp.float32


def mm(a, b, ca, cb):
    return lax.dot_general(
        a, b, (((ca,), (cb,)), ((), ())),
        precision=lax.Precision.HIGHEST, preferred_element_type=F32,
    )


def factor_tile(rows):
    sub = lax.broadcasted_iota(jnp.int32, (SUB, LANES), 0)
    lane = lax.broadcasted_iota(jnp.int32, (SUB, LANES), 1)
    rows = list(rows)
    count = len(rows)
    spread = lambda column: jnp.broadcast_to(column, (SUB, LANES))
    for g in range(count):
        base = g * SUB
        inside = (lane >= base) & (lane < base + SUB)
        cols = [spread(rows[g][:, base + j:base + j + 1]) for j in range(SUB)]
        panel = jnp.where(inside, jnp.where(lane - base == sub, 1.0, 0.0), rows[g])
        kept = panel
        pivots = cols[0]
        for j in range(SUB):
            here = sub == j
            pivot = spread(cols[j][j:j + 1, :])
            inverse = 1.0 / pivot
            scaled = cols[j] * inverse
            row = spread(panel[j:j + 1, :])
            kept = jnp.where(here, panel, kept)
            pivots = jnp.where(here, pivot, pivots)
            panel = jnp.where(here, row * inverse, panel - scaled * row)
            for m in range(j + 1, SUB):
                across = spread(cols[m][j:j + 1, :])
                cols[m] = jnp.where(here, across * inverse, cols[m] - scaled * across)
        rows[g] = kept * lax.rsqrt(pivots)
        panel_rows = [spread(panel[j:j + 1, :]) for j in range(SUB)]
        for i in range(g + 1, count):
            terms = [spread(rows[i][:, base + j:base + j + 1]) * panel_rows[j] for j in range(SUB)]
            while len(terms) > 1:
                terms = [terms[t] + terms[t + 1] for t in range(0, len(terms), 2)]
            rows[i] = jnp.where(inside, 0.0, rows[i]) - terms[0]
    return rows


def inverse_factor_kernel(a_ref, w_ref):
    n = a_ref.shape[0]
    steps = n // LANES
    tri = (lax.broadcasted_iota(jnp.int32, (LANES, LANES), 0)
           >= lax.broadcasted_iota(jnp.int32, (LANES, LANES), 1))
    work = [[a_ref[i * LANES:(i + 1) * LANES, j * LANES:(j + 1) * LANES]
             for j in range(steps)] for i in range(steps)]
    for k in range(steps):
        tile = work[k][k]
        done = factor_tile([tile[g * SUB:(g + 1) * SUB, :] for g in range(LANES // SUB)])
        inv = jnp.where(tri, jnp.concatenate(done, axis=0), 0.0)
        work[k] = [inv if j == k else mm(inv, work[k][j], 1, 0) for j in range(steps)]
        for i in range(k + 1, steps):
            left = work[k][i]
            for j in range(steps):
                product = mm(left, work[k][j], 0, 0)
                work[i][j] = -product if j == k else work[i][j] - product
    for i in range(steps):
        for j in range(steps):
            value = work[i][j] if j <= i else jnp.zeros((LANES, LANES), F32)
            w_ref[i * LANES:(i + 1) * LANES, j * LANES:(j + 1) * LANES] = value


def inverse_factor(a):
    n = a.shape[0]
    return pl.pallas_call(
        inverse_factor_kernel,
        out_shape=jax.ShapeDtypeStruct((n, n), F32),
        in_specs=[pl.BlockSpec(memory_space=pltpu.VMEM)],
        out_specs=pl.BlockSpec(memory_space=pltpu.VMEM),
        compiler_params=pltpu.CompilerParams(vmem_limit_bytes=32 * 1024 * 1024),
        cost_estimate=pl.CostEstimate(flops=n * n * n, bytes_accessed=8 * n * n, transcendentals=0),
    )(a)


def split(x):
    high = x.astype(jnp.bfloat16)
    return high, (x - high.astype(F32)).astype(jnp.bfloat16)


def spread_kernel(slot_ref, place_ref, part_ref, keep_ref, start_ref, high_ref, low_ref, factor_ref, piece_ref, *rest):
    t = pl.program_id(0)
    high, low = split(factor_ref[0])
    dims = (((1,), (0,)), ((), ()))
    dot = lambda a, b: lax.dot_general(a, b, dims, preferred_element_type=F32)
    value = dot(high_ref[...], high) + dot(high_ref[...], low) + dot(low_ref[...], high)
    out_ref = rest[-1]
    out_ref[0] = jnp.where(keep_ref[t] > 0, piece_ref[0] - value, 0.0)
    if len(rest) == 2:
        extra = rest[0][0]
        rows = pl.ds(pl.multiple_of(start_ref[0], 8), extra.shape[0])
        out_ref[0, rows, :] += extra


def spread_update(slots, places, parts, keeps, mine, factor, pieces, width, start, extra=None):
    high, low = split(mine.T)
    count = slots.shape[0]
    q, depth = high.shape
    whole = lambda t, *refs: (0, 0)
    block = lambda t, s, p, h, *refs: (s[t], 0, h[t])
    piece = lambda t, s, p, h, *refs: (p[t], 0, h[t])
    more = []
    if extra is not None:
        per = extra.shape[2] // width
        more = [pl.BlockSpec((1, extra.shape[1], width), lambda t, *refs: (t // per, 0, t % per))]
    return pl.pallas_call(
        spread_kernel,
        grid_spec=pltpu.PrefetchScalarGridSpec(
            num_scalar_prefetch=5,
            grid=(count,),
            in_specs=[
                pl.BlockSpec((q, depth), whole),
                pl.BlockSpec((q, depth), whole),
                pl.BlockSpec((1, depth, width), block),
                pl.BlockSpec((1, q, width), piece),
            ] + more,
            out_specs=pl.BlockSpec((1, q, width), lambda t, *refs: (t, 0, 0)),
        ),
        out_shape=jax.ShapeDtypeStruct((count, q, width), F32),
        compiler_params=pltpu.CompilerParams(vmem_limit_bytes=32 * 1024 * 1024),
        cost_estimate=pl.CostEstimate(
            flops=6 * count * q * depth * width,
            bytes_accessed=4 * count * width * (2 * q + depth), transcendentals=0),
    )(slots, places, parts, keeps, start, high, low, factor, pieces, *([] if extra is None else [extra]))


def product(a, b, ca, cb, precision=lax.Precision.HIGHEST):
    return lax.dot_general(a, b, (((ca,), (cb,)), ((), ())), precision=precision)


def flip(x, axis, bit):
    n = lax.axis_size(axis)
    return lax.ppermute(x, axis, [(i, i ^ bit) for i in range(n)])


def sum_scatter(x, axis):
    n = lax.axis_size(axis)
    me = lax.axis_index(axis)
    bit = 1
    while bit < n:
        pairs = x.reshape((x.shape[0] // 2, 2) + x.shape[1:])
        mine = (me // bit) % 2
        away = lax.dynamic_index_in_dim(pairs, 1 - mine, 1, keepdims=False)
        home = lax.dynamic_index_in_dim(pairs, mine, 1, keepdims=False)
        x = home + flip(away, axis, bit)
        bit *= 2
    return x[0]


def sum_all(x, axis):
    n = lax.axis_size(axis)
    low = lax.axis_index(axis) % 2
    half = x.shape[0] // 2
    away = lax.dynamic_slice_in_dim(x, (1 - low) * half, half, 0)
    part = lax.dynamic_slice_in_dim(x, low * half, half, 0) + flip(away, axis, 1)
    bit = 2
    while bit < n:
        part = part + flip(part, axis, bit)
        bit *= 2
    other = flip(part, axis, 1)
    return jnp.concatenate([jnp.where(low == 0, part, other), jnp.where(low == 0, other, part)], axis=0)


def line_gather(x, axis, ny):
    n = lax.axis_size(axis)
    nz = n // ny
    z = lax.axis_index(axis) // ny
    slots = [x]
    up, down = [x], [x]
    for step in range(1, nz):
        up.append(lax.ppermute(up[-1], axis, [(c, c + ny) for c in range(n) if step - 1 <= c // ny < nz - 1]))
        down.append(lax.ppermute(down[-1], axis, [(c, c - ny) for c in range(n) if 0 < c // ny <= nz - step]))
    for k in range(1, nz):
        slots.append(jnp.where(z >= k, up[k], down[nz - k]))
    beside = []
    for k in range(nz):
        for j in range(1, ny):
            pairs = [(c, c // ny * ny + (c % ny - j) % ny) for c in range(n)]
            beside.append(lax.ppermute(slots[k], axis, pairs))
    return slots + beside


def on_device(child_fronts, extend_map, parent_front):
    front = child_fronts[0]
    order, ncols = front.shape
    nrows, pcols = parent_front.shape
    groups = lax.axis_size("col")
    branches = lax.axis_size("branch")
    ny = 1
    while 4 * ny * ny <= groups:
        ny *= 2
    nz = groups // ny
    width = min(BS, ncols)
    per = ncols // width
    ratio = BS // width
    units_total = NP // width
    col = lax.axis_index("col")
    branch = lax.axis_index("branch")
    pivot_devices = P_SIZE // ncols

    blocks = extend_map[0]
    hit = blocks[:, None] == jnp.arange(NP // BS, dtype=jnp.int32)[None, :]
    present = jnp.any(hit, axis=0).astype(jnp.int32)
    child_block = jnp.sum(
        jnp.where(hit, jnp.arange(blocks.shape[0], dtype=jnp.int32)[:, None], 0), axis=0
    ).astype(jnp.int32)
    t = jnp.arange(units_total, dtype=jnp.int32)
    units = P_SIZE // width + child_block[t // ratio] * ratio + t % ratio
    keeps = present[t // ratio]
    source = units // per
    parts = units % per

    def unit_rows(u):
        return lax.dynamic_slice_in_dim(front, units[u] * width, width, 0)

    def placed(x):
        if pivot_devices == 1:
            return jnp.where(col == 0, x, 0.0)
        wide = jnp.zeros((x.shape[0], P_SIZE), F32)
        wide = lax.dynamic_update_slice_in_dim(wide, x, jnp.minimum(col, pivot_devices - 1) * ncols, 1)
        return jnp.where(col < pivot_devices, wide, 0.0)

    pivots = lax.psum(placed(front[:P_SIZE]), "col")

    pivot_units = PP // width
    lead = jnp.concatenate(
        [front[:P_SIZE]] + [jnp.where(keeps[u] > 0, unit_rows(u), 0.0) for u in range(pivot_units)], axis=0)
    gathered = line_gather(lead, "col", ny)
    back = (col // ny - source // ny) % nz
    aside = (source % ny - col % ny) % ny
    slots = jnp.where(aside == 0, back, nz + back * (ny - 1) + aside - 1)

    share = PP // branches
    ours = jnp.where(branch == 0, parent_front[:PP], 0.0).reshape(branches, share, pcols)
    ours = lax.all_gather(sum_scatter(ours, "branch"), "col")
    start = jnp.reshape(branch * share, (1,)).astype(jnp.int32)

    moved = []
    for a in range(per):
        received = [unit_rows(col * per + a)]
        for shift in range(1, groups):
            pairs = [(c, (c + shift) % groups) for c in range(groups) if c >= pivot_devices]
            received.append(lax.ppermute(unit_rows((col + shift) % groups * per + a), "col", pairs))
        moved.append(jnp.stack(received))
    shifts = (col - source) % groups

    inverse = inverse_factor(pivots)
    child_mine = product(inverse, front[:P_SIZE], 1, 0)
    factor = jnp.stack([product(inverse, x[:P_SIZE], 1, 0) for x in gathered])

    def factor_columns(u):
        block = lax.dynamic_slice(factor, (slots[u], 0, parts[u] * width), (1, P_SIZE, width))
        return jnp.where(keeps[u] > 0, block[0], 0.0)

    head = jnp.concatenate([factor_columns(u) for u in range(pivot_units)], axis=1)
    head_rows = jnp.stack([x[P_SIZE:] for x in gathered])
    first = spread_update(slots, slots, parts, keeps, head, factor, head_rows, width, start, ours)

    def first_columns(begin, count):
        wide = lax.dynamic_slice_in_dim(first, begin, count, 0)
        return jnp.transpose(wide, (1, 0, 2)).reshape(PP, count * width)

    corner = sum_all(first_columns(0, pivot_units), "branch")
    top_mine = sum_all(first_columns(col * per, per), "branch")
    side = sum_scatter(first.reshape((branches, units_total // branches) + first.shape[1:]), "branch")
    side = jnp.transpose(side, (1, 0, 2)).reshape(PP, nrows)

    parent_inverse = inverse_factor(corner)
    parent_mine = product(parent_inverse, top_mine, 1, 0)
    row_factor = product(parent_inverse, side, 1, 0)

    results = []
    for a in range(per):
        unit = col * per + a
        spread = spread_update(
            slots, shifts, parts, keeps * keeps[unit], factor_columns(unit), factor, moved[a], width, start)
        spread = spread.reshape((branches, units_total // branches) + spread.shape[1:])
        added = jnp.transpose(sum_scatter(spread, "branch"), (0, 2, 1)).reshape(nrows, width)
        columns = slice(a * width, (a + 1) * width)
        results.append(
            parent_front[:, columns] + added
            - product(row_factor, parent_mine[:, columns], 0, 0, lax.Precision.HIGH))
    return (child_mine[None], parent_mine, jnp.concatenate(results, axis=1))


def solution(mesh):
    in_specs = (P("branch", None, "col"), P("branch", None), P("branch", "col"))
    out_specs = (P("branch", None, "col"), P(None, "col"), P("branch", "col"))
    return jax.shard_map(
        on_device, mesh=mesh, in_specs=in_specs, out_specs=out_specs, check_vma=False
    )
```

```python
import jax
import jax.numpy as jnp
from jax import lax
from jax.experimental import pallas as pl
from jax.experimental.pallas import tpu as pltpu
from jax.sharding import PartitionSpec as P

BS = 256
P_SIZE = 512
NP = 4096
PP = 512

SUB = 8
LANES = 128
F32 = jnp.float32


def mm(a, b, ca, cb):
    return lax.dot_general(
        a, b, (((ca,), (cb,)), ((), ())),
        precision=lax.Precision.HIGHEST, preferred_element_type=F32,
    )


def factor_tile(rows):
    sub = lax.broadcasted_iota(jnp.int32, (SUB, LANES), 0)
    lane = lax.broadcasted_iota(jnp.int32, (SUB, LANES), 1)
    rows = list(rows)
    count = len(rows)
    spread = lambda column: jnp.broadcast_to(column, (SUB, LANES))
    for g in range(count):
        base = g * SUB
        inside = (lane >= base) & (lane < base + SUB)
        cols = [spread(rows[g][:, base + j:base + j + 1]) for j in range(SUB)]
        panel = jnp.where(inside, jnp.where(lane - base == sub, 1.0, 0.0), rows[g])
        kept = panel
        pivots = cols[0]
        for j in range(SUB):
            here = sub == j
            pivot = spread(cols[j][j:j + 1, :])
            inverse = 1.0 / pivot
            scaled = cols[j] * inverse
            row = spread(panel[j:j + 1, :])
            kept = jnp.where(here, panel, kept)
            pivots = jnp.where(here, pivot, pivots)
            panel = jnp.where(here, row * inverse, panel - scaled * row)
            for m in range(j + 1, SUB):
                across = spread(cols[m][j:j + 1, :])
                cols[m] = jnp.where(here, across * inverse, cols[m] - scaled * across)
        rows[g] = kept * lax.rsqrt(pivots)
        panel_rows = [spread(panel[j:j + 1, :]) for j in range(SUB)]
        for i in range(g + 1, count):
            terms = [spread(rows[i][:, base + j:base + j + 1]) * panel_rows[j] for j in range(SUB)]
            while len(terms) > 1:
                terms = [terms[t] + terms[t + 1] for t in range(0, len(terms), 2)]
            rows[i] = jnp.where(inside, 0.0, rows[i]) - terms[0]
    return rows


def inverse_factor_kernel(a_ref, w_ref):
    n = a_ref.shape[0]
    steps = n // LANES
    tri = (lax.broadcasted_iota(jnp.int32, (LANES, LANES), 0)
           >= lax.broadcasted_iota(jnp.int32, (LANES, LANES), 1))
    work = [[a_ref[i * LANES:(i + 1) * LANES, j * LANES:(j + 1) * LANES]
             for j in range(steps)] for i in range(steps)]
    for k in range(steps):
        tile = work[k][k]
        done = factor_tile([tile[g * SUB:(g + 1) * SUB, :] for g in range(LANES // SUB)])
        inv = jnp.where(tri, jnp.concatenate(done, axis=0), 0.0)
        work[k] = [inv if j == k else mm(inv, work[k][j], 1, 0) for j in range(steps)]
        for i in range(k + 1, steps):
            left = work[k][i]
            for j in range(steps):
                product = mm(left, work[k][j], 0, 0)
                work[i][j] = -product if j == k else work[i][j] - product
    for i in range(steps):
        for j in range(steps):
            value = work[i][j] if j <= i else jnp.zeros((LANES, LANES), F32)
            w_ref[i * LANES:(i + 1) * LANES, j * LANES:(j + 1) * LANES] = value


def inverse_factor(a):
    n = a.shape[0]
    return pl.pallas_call(
        inverse_factor_kernel,
        out_shape=jax.ShapeDtypeStruct((n, n), F32),
        in_specs=[pl.BlockSpec(memory_space=pltpu.VMEM)],
        out_specs=pl.BlockSpec(memory_space=pltpu.VMEM),
        compiler_params=pltpu.CompilerParams(vmem_limit_bytes=32 * 1024 * 1024),
        cost_estimate=pl.CostEstimate(flops=n * n * n, bytes_accessed=8 * n * n, transcendentals=0),
    )(a)


def spread_kernel(slot_ref, place_ref, part_ref, keep_ref, left_ref, factor_ref, piece_ref, out_ref):
    t = pl.program_id(0)
    whole = factor_ref[0]
    high = whole.astype(jnp.bfloat16)
    low = (whole - high.astype(F32)).astype(jnp.bfloat16)
    right = jnp.concatenate([high, low, high], axis=0)
    value = lax.dot_general(left_ref[...], right, (((1,), (0,)), ((), ())), preferred_element_type=F32)
    out_ref[0] = jnp.where(keep_ref[t] > 0, piece_ref[0] - value, 0.0)


def spread_update(slots, places, parts, keeps, mine, factor, pieces, width):
    turned = mine.T
    rounded = lax.reduce_precision(turned, 8, 7)
    high = rounded.astype(jnp.bfloat16)
    low = (turned - rounded).astype(jnp.bfloat16)
    left = jnp.concatenate([high, high, low], axis=1)
    count = slots.shape[0]
    q, depth = turned.shape
    return pl.pallas_call(
        spread_kernel,
        grid_spec=pltpu.PrefetchScalarGridSpec(
            num_scalar_prefetch=4,
            grid=(count,),
            in_specs=[
                pl.BlockSpec((q, 3 * depth), lambda t, *refs: (0, 0)),
                pl.BlockSpec((1, depth, width), lambda t, s, p, h, k: (s[t], 0, h[t])),
                pl.BlockSpec((1, q, width), lambda t, s, p, h, k: (p[t], 0, h[t])),
            ],
            out_specs=pl.BlockSpec((1, q, width), lambda t, *refs: (t, 0, 0)),
        ),
        out_shape=jax.ShapeDtypeStruct((count, q, width), F32),
        compiler_params=pltpu.CompilerParams(vmem_limit_bytes=32 * 1024 * 1024),
        cost_estimate=pl.CostEstimate(
            flops=6 * count * q * depth * width,
            bytes_accessed=4 * count * width * (2 * q + depth), transcendentals=0),
    )(slots, places, parts, keeps, left, factor, pieces)


def product(a, b, ca, cb, precision=lax.Precision.HIGH):
    return lax.dot_general(a, b, (((ca,), (cb,)), ((), ())), precision=precision)


def flip(x, axis, bit):
    n = lax.axis_size(axis)
    return lax.ppermute(x, axis, [(i, i ^ bit) for i in range(n)])


def sum_scatter(x, axis):
    n = lax.axis_size(axis)
    me = lax.axis_index(axis)
    bit = 1
    while bit < n:
        pairs = x.reshape((x.shape[0] // 2, 2) + x.shape[1:])
        mine = (me // bit) % 2
        away = lax.dynamic_index_in_dim(pairs, 1 - mine, 1, keepdims=False)
        home = lax.dynamic_index_in_dim(pairs, mine, 1, keepdims=False)
        x = home + flip(away, axis, bit)
        bit *= 2
    return x[0]


def sum_all(x, axis):
    n = lax.axis_size(axis)
    low = lax.axis_index(axis) % 2
    half = x.shape[0] // 2
    away = lax.dynamic_slice_in_dim(x, (1 - low) * half, half, 0)
    part = lax.dynamic_slice_in_dim(x, low * half, half, 0) + flip(away, axis, 1)
    bit = 2
    while bit < n:
        part = part + flip(part, axis, bit)
        bit *= 2
    other = flip(part, axis, 1)
    return jnp.concatenate([jnp.where(low == 0, part, other), jnp.where(low == 0, other, part)], axis=0)


def share_rows(x, ny):
    branches = lax.axis_size("branch")
    groups = lax.axis_size("col")
    nz = groups // ny
    col = lax.axis_index("col")
    branch = lax.axis_index("branch")
    if nz != branches:
        return lax.dynamic_slice_in_dim(lax.all_gather(x, "col"), branch * groups // branches, groups // branches, 0)
    place = lambda b, z, y: b * groups + z * ny + y
    got = jnp.where(col // ny == branch, x, 0.0)
    for off in range(1, nz):
        pairs = [(place(b, b, y), place(b, (b + off) % nz, y)) for b in range(branches) for y in range(ny)]
        got = got + lax.ppermute(x, ("branch", "col"), pairs)
    shares = [got]
    for j in range(1, ny):
        pairs = [(c, c // ny * ny + (c % ny - j) % ny) for c in range(groups)]
        shares.append(lax.ppermute(got, "col", pairs))
    order = (jnp.arange(ny) - col % ny) % ny
    return jnp.take(jnp.stack(shares), order, axis=0)


def on_device(child_fronts, extend_map, parent_front):
    front = child_fronts[0]
    order, ncols = front.shape
    nrows, pcols = parent_front.shape
    groups = lax.axis_size("col")
    branches = lax.axis_size("branch")
    ny = 1
    while 4 * ny * ny <= groups:
        ny *= 2
    nz = groups // ny
    width = min(BS, ncols)
    per = ncols // width
    ratio = BS // width
    units_total = NP // width
    col = lax.axis_index("col")
    branch = lax.axis_index("branch")
    pivot_devices = P_SIZE // ncols

    blocks = extend_map[0]
    hit = blocks[:, None] == jnp.arange(NP // BS, dtype=jnp.int32)[None, :]
    present = jnp.any(hit, axis=0).astype(jnp.int32)
    child_block = jnp.sum(
        jnp.where(hit, jnp.arange(blocks.shape[0], dtype=jnp.int32)[:, None], 0), axis=0
    ).astype(jnp.int32)
    t = jnp.arange(units_total, dtype=jnp.int32)
    units = P_SIZE // width + child_block[t // ratio] * ratio + t % ratio
    keeps = present[t // ratio]
    source = units // per
    parts = units % per

    def unit_rows(u):
        return lax.dynamic_slice_in_dim(front, units[u] * width, width, 0)

    def placed(x):
        if pivot_devices == 1:
            return jnp.where(col == 0, x, 0.0)
        wide = jnp.zeros((x.shape[0], P_SIZE), F32)
        wide = lax.dynamic_update_slice_in_dim(wide, x, jnp.minimum(col, pivot_devices - 1) * ncols, 1)
        return jnp.where(col < pivot_devices, wide, 0.0)

    pivots = lax.psum(placed(front[:P_SIZE]), "col")

    def rows_for(target):
        return jnp.concatenate([unit_rows(target * per + a) for a in range(per)], axis=0)

    def moved(shift, rows):
        pairs = [(c, (c + shift) % groups) for c in range(groups) if c >= pivot_devices]
        return lax.ppermute(rows, "col", pairs)

    far = sorted(range(1, groups), key=lambda shift: abs(2 * shift - groups))
    received = {0: rows_for(col)}
    for shift in far[:5]:
        received[shift] = moved(shift, rows_for((col + shift) % groups))

    top = lax.all_gather(front[:P_SIZE], "col")
    inverse = inverse_factor(pivots)
    child_mine = product(inverse, front[:P_SIZE], 1, 0)
    for shift in far[5:]:
        rows, _ = lax.optimization_barrier((rows_for((col + shift) % groups), inverse))
        received[shift] = moved(shift, rows)
    places = (col - source) % groups

    factor = jnp.stack([product(inverse, top[c], 1, 0) for c in range(groups)])

    def factor_columns(u):
        block = lax.dynamic_slice(factor, (source[u], 0, parts[u] * width), (1, P_SIZE, width))
        return jnp.where(keeps[u] > 0, block[0], 0.0)

    mine = jnp.concatenate([factor_columns(col * per + a) for a in range(per)], axis=1)
    mine_keep = jnp.repeat(lax.dynamic_slice_in_dim(keeps, col * per, per), width)[:, None] > 0
    pieces = jnp.stack([jnp.where(mine_keep, received[shift], 0.0) for shift in range(groups)])

    spread = spread_update(source, places, parts, keeps, mine, factor, pieces, width)
    pivot_units = PP // width
    first = jnp.where(branch == 0, parent_front[:PP].T, 0.0)
    first = first + jnp.concatenate([spread[u] for u in range(pivot_units)], axis=1)
    first = sum_all(first, "branch")
    corner = lax.psum(placed(first.T) if pivot_devices > 1 else placed(first), "col")
    side = share_rows(first, ny).reshape(nrows, PP)

    added = sum_scatter(spread.reshape((branches, units_total // branches) + spread.shape[1:]), "branch")
    assembled = parent_front + jnp.transpose(added, (0, 2, 1)).reshape(nrows, pcols)

    parent_inverse = inverse_factor(corner)
    parent_mine = product(parent_inverse, first, 1, 1)
    row_factor = product(side, parent_inverse, 1, 1)
    result = assembled - product(row_factor, parent_mine, 1, 0)
    return (child_mine[None], parent_mine, result)


def solution(mesh):
    in_specs = (P("branch", None, "col"), P("branch", None), P("branch", "col"))
    out_specs = (P("branch", None, "col"), P(None, "col"), P("branch", "col"))
    return jax.shard_map(
        on_device, mesh=mesh, in_specs=in_specs, out_specs=out_specs, check_vma=False
    )
```

```python
import jax
import jax.numpy as jnp
from jax import lax
from jax.experimental import pallas as pl
from jax.experimental.pallas import tpu as pltpu
from jax.sharding import PartitionSpec as P

BS = 256
P_SIZE = 512
NP = 4096
PP = 512
EARLY = 4
LATE = 5

SUB = 8
LANES = 128
F32 = jnp.float32


def mm(a, b, ca, cb):
    return lax.dot_general(
        a, b, (((ca,), (cb,)), ((), ())),
        precision=lax.Precision.HIGHEST, preferred_element_type=F32,
    )


def factor_tile(rows):
    sub = lax.broadcasted_iota(jnp.int32, (SUB, LANES), 0)
    lane = lax.broadcasted_iota(jnp.int32, (SUB, LANES), 1)
    rows = list(rows)
    count = len(rows)
    spread = lambda column: jnp.broadcast_to(column, (SUB, LANES))
    for g in range(count):
        base = g * SUB
        inside = (lane >= base) & (lane < base + SUB)
        cols = [spread(rows[g][:, base + j:base + j + 1]) for j in range(SUB)]
        panel = jnp.where(inside, jnp.where(lane - base == sub, 1.0, 0.0), rows[g])
        kept = panel
        pivots = cols[0]
        for j in range(SUB):
            here = sub == j
            pivot = spread(cols[j][j:j + 1, :])
            inverse = 1.0 / pivot
            scaled = cols[j] * inverse
            row = spread(panel[j:j + 1, :])
            kept = jnp.where(here, panel, kept)
            pivots = jnp.where(here, pivot, pivots)
            panel = jnp.where(here, row * inverse, panel - scaled * row)
            for m in range(j + 1, SUB):
                across = spread(cols[m][j:j + 1, :])
                cols[m] = jnp.where(here, across * inverse, cols[m] - scaled * across)
        rows[g] = kept * lax.rsqrt(pivots)
        panel_rows = [spread(panel[j:j + 1, :]) for j in range(SUB)]
        for i in range(g + 1, count):
            terms = [spread(rows[i][:, base + j:base + j + 1]) * panel_rows[j] for j in range(SUB)]
            while len(terms) > 1:
                terms = [terms[t] + terms[t + 1] for t in range(0, len(terms), 2)]
            rows[i] = jnp.where(inside, 0.0, rows[i]) - terms[0]
    return rows


def inverse_factor_kernel(a_ref, w_ref):
    n = a_ref.shape[0]
    steps = n // LANES
    tri = (lax.broadcasted_iota(jnp.int32, (LANES, LANES), 0)
           >= lax.broadcasted_iota(jnp.int32, (LANES, LANES), 1))
    work = [[a_ref[i * LANES:(i + 1) * LANES, j * LANES:(j + 1) * LANES]
             for j in range(steps)] for i in range(steps)]
    for k in range(steps):
        tile = work[k][k]
        done = factor_tile([tile[g * SUB:(g + 1) * SUB, :] for g in range(LANES // SUB)])
        inv = jnp.where(tri, jnp.concatenate(done, axis=0), 0.0)
        work[k] = [inv if j == k else mm(inv, work[k][j], 1, 0) for j in range(steps)]
        for i in range(k + 1, steps):
            left = work[k][i]
            for j in range(steps):
                product = mm(left, work[k][j], 0, 0)
                work[i][j] = -product if j == k else work[i][j] - product
    for i in range(steps):
        for j in range(steps):
            value = work[i][j] if j <= i else jnp.zeros((LANES, LANES), F32)
            w_ref[i * LANES:(i + 1) * LANES, j * LANES:(j + 1) * LANES] = value


def inverse_factor(a):
    n = a.shape[0]
    return pl.pallas_call(
        inverse_factor_kernel,
        out_shape=jax.ShapeDtypeStruct((n, n), F32),
        in_specs=[pl.BlockSpec(memory_space=pltpu.VMEM)],
        out_specs=pl.BlockSpec(memory_space=pltpu.VMEM),
        compiler_params=pltpu.CompilerParams(vmem_limit_bytes=32 * 1024 * 1024),
        cost_estimate=pl.CostEstimate(flops=n * n * n, bytes_accessed=8 * n * n, transcendentals=0),
    )(a)


def spread_kernel(slot_ref, place_ref, part_ref, keep_ref, left_ref, factor_ref, piece_ref, out_ref):
    t = pl.program_id(0)
    whole = factor_ref[0]
    high = whole.astype(jnp.bfloat16)
    low = (whole - high.astype(F32)).astype(jnp.bfloat16)
    right = jnp.concatenate([high, low, high], axis=0)
    value = lax.dot_general(left_ref[...], right, (((1,), (0,)), ((), ())), preferred_element_type=F32)
    out_ref[0] = jnp.where(keep_ref[t] > 0, piece_ref[0] - value, 0.0)


def three_part(x):
    turned = x.T
    rounded = lax.reduce_precision(turned, 8, 7)
    high = rounded.astype(jnp.bfloat16)
    low = (turned - rounded).astype(jnp.bfloat16)
    return jnp.concatenate([high, high, low], axis=1)


def spread_update(slots, places, parts, keeps, left, factor, pieces, width):
    count = slots.shape[0]
    q, depth = left.shape[0], left.shape[1] // 3
    return pl.pallas_call(
        spread_kernel,
        grid_spec=pltpu.PrefetchScalarGridSpec(
            num_scalar_prefetch=4,
            grid=(count,),
            in_specs=[
                pl.BlockSpec((q, 3 * depth), lambda t, *refs: (0, 0)),
                pl.BlockSpec((1, depth, width), lambda t, s, p, h, k: (s[t], 0, h[t])),
                pl.BlockSpec((1, q, width), lambda t, s, p, h, k: (p[t], 0, h[t])),
            ],
            out_specs=pl.BlockSpec((1, q, width), lambda t, *refs: (t, 0, 0)),
        ),
        out_shape=jax.ShapeDtypeStruct((count, q, width), F32),
        compiler_params=pltpu.CompilerParams(vmem_limit_bytes=32 * 1024 * 1024),
        cost_estimate=pl.CostEstimate(
            flops=6 * count * q * depth * width,
            bytes_accessed=4 * count * width * (2 * q + depth), transcendentals=0),
    )(slots, places, parts, keeps, left, factor, pieces)


def product(a, b, ca, cb, precision=lax.Precision.HIGH):
    return lax.dot_general(a, b, (((ca,), (cb,)), ((), ())), precision=precision)


def flip(x, axis, bit):
    n = lax.axis_size(axis)
    return lax.ppermute(x, axis, [(i, i ^ bit) for i in range(n)])


def sum_scatter(x, axis):
    n = lax.axis_size(axis)
    me = lax.axis_index(axis)
    bit = 1
    while bit < n:
        pairs = x.reshape((x.shape[0] // 2, 2) + x.shape[1:])
        mine = (me // bit) % 2
        away = lax.dynamic_index_in_dim(pairs, 1 - mine, 1, keepdims=False)
        home = lax.dynamic_index_in_dim(pairs, mine, 1, keepdims=False)
        x = home + flip(away, axis, bit)
        bit *= 2
    return x[0]


def sum_all(x, axis):
    n = lax.axis_size(axis)
    me = lax.axis_index(axis)
    bits = []
    while 1 << len(bits) < n:
        bits.append(1 << len(bits))
    for bit in bits:
        high = (me // bit) % 2
        half = x.shape[0] // 2
        away = lax.dynamic_slice_in_dim(x, (1 - high) * half, half, 0)
        x = lax.dynamic_slice_in_dim(x, high * half, half, 0) + flip(away, axis, bit)
    for bit in reversed(bits):
        high = (me // bit) % 2
        other = flip(x, axis, bit)
        x = jnp.concatenate([jnp.where(high == 0, x, other), jnp.where(high == 0, other, x)], axis=0)
    return x


def share_rows(x, ny):
    branches = lax.axis_size("branch")
    groups = lax.axis_size("col")
    nz = groups // ny
    col = lax.axis_index("col")
    branch = lax.axis_index("branch")
    if nz != branches:
        return lax.dynamic_slice_in_dim(lax.all_gather(x, "col"), branch * groups // branches, groups // branches, 0)
    place = lambda b, z, y: b * groups + z * ny + y
    got = jnp.where(col // ny == branch, x, 0.0)
    for off in range(1, nz):
        pairs = [(place(b, b, y), place(b, (b + off) % nz, y)) for b in range(branches) for y in range(ny)]
        got = got + lax.ppermute(x, ("branch", "col"), pairs)
    shares = [got]
    for j in range(1, ny):
        pairs = [(c, c // ny * ny + (c % ny - j) % ny) for c in range(groups)]
        shares.append(lax.ppermute(got, "col", pairs))
    order = (jnp.arange(ny) - col % ny) % ny
    return jnp.take(jnp.stack(shares), order, axis=0)


def on_device(child_fronts, extend_map, parent_front):
    front = child_fronts[0]
    order, ncols = front.shape
    nrows, pcols = parent_front.shape
    groups = lax.axis_size("col")
    branches = lax.axis_size("branch")
    ny = 1
    while 4 * ny * ny <= groups:
        ny *= 2
    nz = groups // ny
    width = min(BS, ncols)
    per = ncols // width
    ratio = BS // width
    units_total = NP // width
    col = lax.axis_index("col")
    branch = lax.axis_index("branch")
    pivot_devices = P_SIZE // ncols

    blocks = extend_map[0]
    hit = blocks[:, None] == jnp.arange(NP // BS, dtype=jnp.int32)[None, :]
    present = jnp.any(hit, axis=0).astype(jnp.int32)
    child_block = jnp.sum(
        jnp.where(hit, jnp.arange(blocks.shape[0], dtype=jnp.int32)[:, None], 0), axis=0
    ).astype(jnp.int32)
    t = jnp.arange(units_total, dtype=jnp.int32)
    units = P_SIZE // width + child_block[t // ratio] * ratio + t % ratio
    keeps = present[t // ratio]
    source = units // per
    parts = units % per

    def unit_rows(u):
        return lax.dynamic_slice_in_dim(front, units[u] * width, width, 0)

    def placed(x):
        if pivot_devices == 1:
            return jnp.where(col == 0, x, 0.0)
        wide = jnp.zeros((x.shape[0], P_SIZE), F32)
        wide = lax.dynamic_update_slice_in_dim(wide, x, jnp.minimum(col, pivot_devices - 1) * ncols, 1)
        return jnp.where(col < pivot_devices, wide, 0.0)

    top = lax.all_gather(front[:P_SIZE], "col")
    pivots = jnp.concatenate([top[c] for c in range(pivot_devices)], axis=1) if pivot_devices > 1 else top[0]

    pivot_units = PP // width

    def pivot_column(b):
        local = units[b] - col * per
        ok = (local >= 0) & (local < per) & (keeps[b] > 0)
        column = lax.dynamic_slice_in_dim(front, jnp.clip(local, 0, per - 1) * width, width, 1)
        body = [
            jnp.where(ok & (keeps[a] > 0), lax.dynamic_slice_in_dim(column, units[a] * width, width, 0), 0.0)
            for a in range(pivot_units)
        ]
        return jnp.concatenate(body, axis=0)

    corner = jnp.concatenate([pivot_column(b) for b in range(pivot_units)], axis=1)
    corner = corner + jnp.where(branch == 0, placed(parent_front[:PP]), 0.0)
    corner = sum_all(corner, "col")

    def rows_for(target):
        return jnp.concatenate([unit_rows(target * per + a) for a in range(per)], axis=0)

    def moved(shift, rows):
        pairs = [(c, (c + shift) % groups) for c in range(groups) if c >= pivot_devices]
        return lax.ppermute(rows, "col", pairs)

    far = sorted(range(1, groups), key=lambda shift: abs(2 * shift - groups))
    received = {0: rows_for(col)}
    for shift in far[:EARLY]:
        received[shift] = moved(shift, rows_for((col + shift) % groups))
    for shift in far[EARLY:LATE]:
        rows, _ = lax.optimization_barrier((rows_for((col + shift) % groups), corner))
        received[shift] = moved(shift, rows)
    pivots, received, corner = lax.optimization_barrier((pivots, received, corner))
    for shift in far[LATE:]:
        rows, _ = lax.optimization_barrier((rows_for((col + shift) % groups), pivots))
        received[shift] = moved(shift, rows)

    inverse = inverse_factor(pivots)
    child_mine = product(inverse, front[:P_SIZE], 1, 0)
    places = (col - source) % groups

    factor = jnp.stack([product(inverse, top[c], 1, 0) for c in range(groups)])

    def factor_columns(u):
        block = lax.dynamic_slice(factor, (source[u], 0, parts[u] * width), (1, P_SIZE, width))
        return jnp.where(keeps[u] > 0, block[0], 0.0)

    head = jnp.concatenate([factor_columns(u) for u in range(pivot_units)], axis=1)
    corner = sum_all(corner - product(head, head, 0, 0), "branch")
    parent_inverse = inverse_factor(corner)

    mine = jnp.concatenate([factor_columns(col * per + a) for a in range(per)], axis=1)
    mine_keep = jnp.repeat(lax.dynamic_slice_in_dim(keeps, col * per, per), width)[:, None] > 0
    pieces = jnp.stack([jnp.where(mine_keep, received[shift], 0.0) for shift in range(groups)])
    left = three_part(mine)
    n = pivot_units
    first = spread_update(source[:n], places[:n], parts[:n], keeps[:n], left, factor, pieces, width)
    left, first = lax.optimization_barrier((left, first))
    first = jnp.concatenate([first[u] for u in range(n)], axis=1)
    first = sum_all(first + jnp.where(branch == 0, parent_front[:PP].T, 0.0), "branch")
    side = share_rows(first, ny).reshape(nrows, PP)

    spread = spread_update(source, places, parts, keeps, left, factor, pieces, width)
    added = sum_scatter(spread.reshape((branches, units_total // branches) + spread.shape[1:]), "branch")
    assembled = parent_front + jnp.transpose(added, (0, 2, 1)).reshape(nrows, pcols)

    parent_mine = product(parent_inverse, first, 1, 1)
    row_factor = product(side, parent_inverse, 1, 1)
    result = assembled - product(row_factor, parent_mine, 1, 0)
    return (child_mine[None], parent_mine, result)


def solution(mesh):
    in_specs = (P("branch", None, "col"), P("branch", None), P("branch", "col"))
    out_specs = (P("branch", None, "col"), P(None, "col"), P("branch", "col"))
    return jax.shard_map(
        on_device, mesh=mesh, in_specs=in_specs, out_specs=out_specs, check_vma=False
    )
```

```python
import jax
import jax.numpy as jnp
from jax import lax
from jax.experimental import pallas as pl
from jax.experimental.pallas import tpu as pltpu
from jax.sharding import PartitionSpec as P

BS = 256
P_SIZE = 512
NP = 4096
PP = 512
EARLY = 4

SUB = 8
LANES = 128
F32 = jnp.float32


def mm(a, b, ca, cb):
    return lax.dot_general(
        a, b, (((ca,), (cb,)), ((), ())),
        precision=lax.Precision.HIGHEST, preferred_element_type=F32,
    )


def factor_tile(rows):
    sub = lax.broadcasted_iota(jnp.int32, (SUB, LANES), 0)
    lane = lax.broadcasted_iota(jnp.int32, (SUB, LANES), 1)
    rows = list(rows)
    count = len(rows)
    spread = lambda column: jnp.broadcast_to(column, (SUB, LANES))
    for g in range(count):
        base = g * SUB
        inside = (lane >= base) & (lane < base + SUB)
        cols = [spread(rows[g][:, base + j:base + j + 1]) for j in range(SUB)]
        panel = jnp.where(inside, jnp.where(lane - base == sub, 1.0, 0.0), rows[g])
        kept = panel
        pivots = cols[0]
        for j in range(SUB):
            here = sub == j
            pivot = spread(cols[j][j:j + 1, :])
            inverse = 1.0 / pivot
            scaled = cols[j] * inverse
            row = spread(panel[j:j + 1, :])
            kept = jnp.where(here, panel, kept)
            pivots = jnp.where(here, pivot, pivots)
            panel = jnp.where(here, row * inverse, panel - scaled * row)
            for m in range(j + 1, SUB):
                across = spread(cols[m][j:j + 1, :])
                cols[m] = jnp.where(here, across * inverse, cols[m] - scaled * across)
        rows[g] = kept * lax.rsqrt(pivots)
        panel_rows = [spread(panel[j:j + 1, :]) for j in range(SUB)]
        for i in range(g + 1, count):
            terms = [spread(rows[i][:, base + j:base + j + 1]) * panel_rows[j] for j in range(SUB)]
            while len(terms) > 1:
                terms = [terms[t] + terms[t + 1] for t in range(0, len(terms), 2)]
            rows[i] = jnp.where(inside, 0.0, rows[i]) - terms[0]
    return rows


def inverse_factor_kernel(a_ref, w_ref):
    n = a_ref.shape[0]
    steps = n // LANES
    tri = (lax.broadcasted_iota(jnp.int32, (LANES, LANES), 0)
           >= lax.broadcasted_iota(jnp.int32, (LANES, LANES), 1))
    work = [[a_ref[i * LANES:(i + 1) * LANES, j * LANES:(j + 1) * LANES]
             for j in range(steps)] for i in range(steps)]
    for k in range(steps):
        tile = work[k][k]
        done = factor_tile([tile[g * SUB:(g + 1) * SUB, :] for g in range(LANES // SUB)])
        inv = jnp.where(tri, jnp.concatenate(done, axis=0), 0.0)
        work[k] = [inv if j == k else mm(inv, work[k][j], 1, 0) for j in range(steps)]
        for i in range(k + 1, steps):
            left = work[k][i]
            for j in range(steps):
                product = mm(left, work[k][j], 0, 0)
                work[i][j] = -product if j == k else work[i][j] - product
    for i in range(steps):
        for j in range(steps):
            value = work[i][j] if j <= i else jnp.zeros((LANES, LANES), F32)
            w_ref[i * LANES:(i + 1) * LANES, j * LANES:(j + 1) * LANES] = value


def inverse_factor(a):
    n = a.shape[0]
    return pl.pallas_call(
        inverse_factor_kernel,
        out_shape=jax.ShapeDtypeStruct((n, n), F32),
        in_specs=[pl.BlockSpec(memory_space=pltpu.VMEM)],
        out_specs=pl.BlockSpec(memory_space=pltpu.VMEM),
        compiler_params=pltpu.CompilerParams(vmem_limit_bytes=32 * 1024 * 1024),
        cost_estimate=pl.CostEstimate(flops=n * n * n, bytes_accessed=8 * n * n, transcendentals=0),
    )(a)


def spread_kernel(slot_ref, place_ref, part_ref, keep_ref, left_ref, factor_ref, piece_ref, out_ref):
    t = pl.program_id(0)
    whole = factor_ref[0]
    high = whole.astype(jnp.bfloat16)
    low = (whole - high.astype(F32)).astype(jnp.bfloat16)
    right = jnp.concatenate([high, low, high], axis=0)
    value = lax.dot_general(left_ref[...], right, (((1,), (0,)), ((), ())), preferred_element_type=F32)
    out_ref[0] = jnp.where(keep_ref[t] > 0, piece_ref[0] - value, 0.0)


def three_part(x):
    turned = x.T
    rounded = lax.reduce_precision(turned, 8, 7)
    high = rounded.astype(jnp.bfloat16)
    low = (turned - rounded).astype(jnp.bfloat16)
    return jnp.concatenate([high, high, low], axis=1)


def spread_update(slots, places, parts, keeps, left, factor, pieces, width):
    count = slots.shape[0]
    q, depth = left.shape[0], left.shape[1] // 3
    return pl.pallas_call(
        spread_kernel,
        grid_spec=pltpu.PrefetchScalarGridSpec(
            num_scalar_prefetch=4,
            grid=(count,),
            in_specs=[
                pl.BlockSpec((q, 3 * depth), lambda t, *refs: (0, 0)),
                pl.BlockSpec((1, depth, width), lambda t, s, p, h, k: (s[t], 0, h[t])),
                pl.BlockSpec((1, q, width), lambda t, s, p, h, k: (p[t], 0, h[t])),
            ],
            out_specs=pl.BlockSpec((1, q, width), lambda t, *refs: (t, 0, 0)),
        ),
        out_shape=jax.ShapeDtypeStruct((count, q, width), F32),
        compiler_params=pltpu.CompilerParams(vmem_limit_bytes=32 * 1024 * 1024),
        cost_estimate=pl.CostEstimate(
            flops=6 * count * q * depth * width,
            bytes_accessed=4 * count * width * (2 * q + depth), transcendentals=0),
    )(slots, places, parts, keeps, left, factor, pieces)


def product(a, b, ca, cb, precision=lax.Precision.HIGH):
    return lax.dot_general(a, b, (((ca,), (cb,)), ((), ())), precision=precision)


def flip(x, axis, bit):
    n = lax.axis_size(axis)
    return lax.ppermute(x, axis, [(i, i ^ bit) for i in range(n)])


def sum_scatter(x, axis):
    n = lax.axis_size(axis)
    me = lax.axis_index(axis)
    bit = 1
    while bit < n:
        pairs = x.reshape((x.shape[0] // 2, 2) + x.shape[1:])
        mine = (me // bit) % 2
        away = lax.dynamic_index_in_dim(pairs, 1 - mine, 1, keepdims=False)
        home = lax.dynamic_index_in_dim(pairs, mine, 1, keepdims=False)
        x = home + flip(away, axis, bit)
        bit *= 2
    return x[0]


def sum_all(x, axis, gates=()):
    n = lax.axis_size(axis)
    me = lax.axis_index(axis)
    bits = []
    while 1 << len(bits) < n:
        bits.append(1 << len(bits))
    for step, bit in enumerate(bits):
        if step < len(gates):
            x, _ = lax.optimization_barrier((x, gates[step]))
        high = (me // bit) % 2
        half = x.shape[0] // 2
        away = lax.dynamic_slice_in_dim(x, (1 - high) * half, half, 0)
        x = lax.dynamic_slice_in_dim(x, high * half, half, 0) + flip(away, axis, bit)
    for bit in reversed(bits):
        high = (me // bit) % 2
        other = flip(x, axis, bit)
        x = jnp.concatenate([jnp.where(high == 0, x, other), jnp.where(high == 0, other, x)], axis=0)
    return x


def line_gather(x, axis, ny):
    n = lax.axis_size(axis)
    nz = n // ny
    up, down = [x], [x]
    for step in range(1, nz):
        up.append(lax.ppermute(up[-1], axis, [(c, c + ny) for c in range(n) if step - 1 <= c // ny < nz - 1]))
        down.append(lax.ppermute(down[-1], axis, [(c, c - ny) for c in range(n) if 0 < c // ny <= nz - step]))

    def beside(y, j, rows):
        pairs = [(c, c // ny * ny + (c % ny - j) % ny) for c in range(n) if c // ny in rows]
        return lax.ppermute(y, axis, pairs)

    got = [[x] + [beside(x, j, range(nz)) for j in range(1, ny)]]
    for k in range(1, nz):
        above, below = range(k, nz), range(k)
        got.append([up[k] + down[nz - k]] + [
            beside(up[k], j, above) + beside(down[nz - k], j, below) for j in range(1, ny)])
    return got, list(zip(up[1:], down[1:]))


def share_rows(x, ny):
    branches = lax.axis_size("branch")
    groups = lax.axis_size("col")
    nz = groups // ny
    col = lax.axis_index("col")
    branch = lax.axis_index("branch")
    if nz != branches:
        return lax.dynamic_slice_in_dim(lax.all_gather(x, "col"), branch * groups // branches, groups // branches, 0)
    place = lambda b, z, y: b * groups + z * ny + y
    got = jnp.where(col // ny == branch, x, 0.0)
    for off in range(1, nz):
        pairs = [(place(b, b, y), place(b, (b + off) % nz, y)) for b in range(branches) for y in range(ny)]
        got = got + lax.ppermute(x, ("branch", "col"), pairs)
    shares = [got]
    for j in range(1, ny):
        pairs = [(c, c // ny * ny + (c % ny - j) % ny) for c in range(groups)]
        shares.append(lax.ppermute(got, "col", pairs))
    order = (jnp.arange(ny) - col % ny) % ny
    return jnp.take(jnp.stack(shares), order, axis=0)


def on_device(child_fronts, extend_map, parent_front):
    front = child_fronts[0]
    order, ncols = front.shape
    nrows, pcols = parent_front.shape
    groups = lax.axis_size("col")
    branches = lax.axis_size("branch")
    ny = 1
    while 4 * ny * ny <= groups:
        ny *= 2
    nz = groups // ny
    width = min(BS, ncols)
    per = ncols // width
    ratio = BS // width
    units_total = NP // width
    col = lax.axis_index("col")
    branch = lax.axis_index("branch")
    pivot_devices = P_SIZE // ncols

    blocks = extend_map[0]
    hit = blocks[:, None] == jnp.arange(NP // BS, dtype=jnp.int32)[None, :]
    present = jnp.any(hit, axis=0).astype(jnp.int32)
    child_block = jnp.sum(
        jnp.where(hit, jnp.arange(blocks.shape[0], dtype=jnp.int32)[:, None], 0), axis=0
    ).astype(jnp.int32)
    t = jnp.arange(units_total, dtype=jnp.int32)
    units = P_SIZE // width + child_block[t // ratio] * ratio + t % ratio
    keeps = present[t // ratio]
    source = units // per
    parts = units % per

    def unit_rows(u):
        return lax.dynamic_slice_in_dim(front, units[u] * width, width, 0)

    def placed(x):
        if pivot_devices == 1:
            return jnp.where(col == 0, x, 0.0)
        wide = jnp.zeros((x.shape[0], P_SIZE), F32)
        wide = lax.dynamic_update_slice_in_dim(wide, x, jnp.minimum(col, pivot_devices - 1) * ncols, 1)
        return jnp.where(col < pivot_devices, wide, 0.0)

    gathered, ends = line_gather(front[:P_SIZE], "col", ny)
    nz = groups // ny
    z, y = col // ny, col % ny
    back = (z - source // ny) % nz
    aside = (source % ny - y) % ny
    slots = back * ny + aside

    def top_of(c):
        return sum(
            jnp.where((z == (c // ny + k) % nz) & (y == (c % ny - j) % ny), gathered[k][j], 0.0)
            for k in range(nz) for j in range(ny))

    pivots = [top_of(c) for c in range(pivot_devices)]
    pivots = jnp.concatenate(pivots, axis=1) if pivot_devices > 1 else pivots[0]

    pivot_units = PP // width

    def pivot_column(b):
        local = units[b] - col * per
        ok = (local >= 0) & (local < per) & (keeps[b] > 0)
        column = lax.dynamic_slice_in_dim(front, jnp.clip(local, 0, per - 1) * width, width, 1)
        body = [
            jnp.where(ok & (keeps[a] > 0), lax.dynamic_slice_in_dim(column, units[a] * width, width, 0), 0.0)
            for a in range(pivot_units)
        ]
        return jnp.concatenate(body, axis=0)

    corner = jnp.concatenate([pivot_column(b) for b in range(pivot_units)], axis=1)
    corner = corner + jnp.where(branch == 0, placed(parent_front[:PP]), 0.0)
    corner = sum_all(corner, "col", [front[:8], *ends])

    def rows_for(target):
        return jnp.concatenate([unit_rows(target * per + a) for a in range(per)], axis=0)

    def moved(shift, rows):
        pairs = [(c, (c + shift) % groups) for c in range(groups) if c >= pivot_devices]
        return lax.ppermute(rows, "col", pairs)

    far = sorted(range(1, groups), key=lambda shift: abs(2 * shift - groups))
    received = {0: rows_for(col)}
    for shift in far[:EARLY]:
        rows, _ = lax.optimization_barrier((rows_for((col + shift) % groups), ends[-1]))
        received[shift] = moved(shift, rows)

    inverse = inverse_factor(pivots)
    for shift in far[EARLY:]:
        rows, _ = lax.optimization_barrier((rows_for((col + shift) % groups), inverse))
        received[shift] = moved(shift, rows)
    places = (col - source) % groups
    child_mine = product(inverse, front[:P_SIZE], 1, 0)

    early = [received[shift] for shift in far[:EARLY]]
    inverse, early, corner = lax.optimization_barrier((inverse, early, corner))
    received.update(zip(far[:EARLY], early))
    factor = jnp.stack([product(inverse, x, 1, 0) for line in gathered for x in line])

    def factor_columns(u):
        block = lax.dynamic_slice(factor, (slots[u], 0, parts[u] * width), (1, P_SIZE, width))
        return jnp.where(keeps[u] > 0, block[0], 0.0)

    head = jnp.concatenate([factor_columns(u) for u in range(pivot_units)], axis=1)
    corner = sum_all(corner - product(head, head, 0, 0), "branch")
    parent_inverse = inverse_factor(corner)

    mine = jnp.concatenate([factor_columns(col * per + a) for a in range(per)], axis=1)
    mine_keep = jnp.repeat(lax.dynamic_slice_in_dim(keeps, col * per, per), width)[:, None] > 0
    pieces = jnp.stack([jnp.where(mine_keep, received[shift], 0.0) for shift in range(groups)])
    left = three_part(mine)
    n = pivot_units
    first = spread_update(slots[:n], places[:n], parts[:n], keeps[:n], left, factor, pieces, width)
    left, first = lax.optimization_barrier((left, first))
    first = jnp.concatenate([first[u] for u in range(n)], axis=1)
    first = sum_all(first + jnp.where(branch == 0, parent_front[:PP].T, 0.0), "branch")
    side = share_rows(first, ny).reshape(nrows, PP)

    spread = spread_update(slots, places, parts, keeps, left, factor, pieces, width)
    added = sum_scatter(spread.reshape((branches, units_total // branches) + spread.shape[1:]), "branch")
    assembled = parent_front + jnp.transpose(added, (0, 2, 1)).reshape(nrows, pcols)

    parent_mine = product(parent_inverse, first, 1, 1)
    row_factor = product(side, parent_inverse, 1, 1)
    result = assembled - product(row_factor, parent_mine, 1, 0)
    return (child_mine[None], parent_mine, result)


def solution(mesh):
    in_specs = (P("branch", None, "col"), P("branch", None), P("branch", "col"))
    out_specs = (P("branch", None, "col"), P(None, "col"), P("branch", "col"))
    return jax.shard_map(
        on_device, mesh=mesh, in_specs=in_specs, out_specs=out_specs, check_vma=False
    )
```

```python
import jax
import jax.numpy as jnp
from jax import lax
from jax.experimental import pallas as pl
from jax.experimental.pallas import tpu as pltpu
from jax.sharding import PartitionSpec as P

BS = 256
P_SIZE = 512
NP = 4096
PP = 512
EARLY = 5

SUB = 8
LANES = 128
F32 = jnp.float32


def mm(a, b, ca, cb):
    return lax.dot_general(
        a, b, (((ca,), (cb,)), ((), ())),
        precision=lax.Precision.HIGHEST, preferred_element_type=F32,
    )


def factor_tile(rows):
    sub = lax.broadcasted_iota(jnp.int32, (SUB, LANES), 0)
    lane = lax.broadcasted_iota(jnp.int32, (SUB, LANES), 1)
    rows = list(rows)
    count = len(rows)
    spread = lambda column: jnp.broadcast_to(column, (SUB, LANES))
    for g in range(count):
        base = g * SUB
        inside = (lane >= base) & (lane < base + SUB)
        cols = [spread(rows[g][:, base + j:base + j + 1]) for j in range(SUB)]
        panel = jnp.where(inside, jnp.where(lane - base == sub, 1.0, 0.0), rows[g])
        kept = panel
        pivots = cols[0]
        for j in range(SUB):
            here = sub == j
            pivot = spread(cols[j][j:j + 1, :])
            inverse = 1.0 / pivot
            scaled = cols[j] * inverse
            row = spread(panel[j:j + 1, :])
            kept = jnp.where(here, panel, kept)
            pivots = jnp.where(here, pivot, pivots)
            panel = jnp.where(here, row * inverse, panel - scaled * row)
            for m in range(j + 1, SUB):
                across = spread(cols[m][j:j + 1, :])
                cols[m] = jnp.where(here, across * inverse, cols[m] - scaled * across)
        rows[g] = kept * lax.rsqrt(pivots)
        panel_rows = [spread(panel[j:j + 1, :]) for j in range(SUB)]
        for i in range(g + 1, count):
            terms = [spread(rows[i][:, base + j:base + j + 1]) * panel_rows[j] for j in range(SUB)]
            while len(terms) > 1:
                terms = [terms[t] + terms[t + 1] for t in range(0, len(terms), 2)]
            rows[i] = jnp.where(inside, 0.0, rows[i]) - terms[0]
    return rows


def inverse_factor_kernel(a_ref, w_ref):
    n = a_ref.shape[0]
    steps = n // LANES
    tri = (lax.broadcasted_iota(jnp.int32, (LANES, LANES), 0)
           >= lax.broadcasted_iota(jnp.int32, (LANES, LANES), 1))
    work = [[a_ref[i * LANES:(i + 1) * LANES, j * LANES:(j + 1) * LANES]
             for j in range(steps)] for i in range(steps)]
    for k in range(steps):
        tile = work[k][k]
        done = factor_tile([tile[g * SUB:(g + 1) * SUB, :] for g in range(LANES // SUB)])
        inv = jnp.where(tri, jnp.concatenate(done, axis=0), 0.0)
        work[k] = [inv if j == k else mm(inv, work[k][j], 1, 0) for j in range(steps)]
        for i in range(k + 1, steps):
            left = work[k][i]
            for j in range(steps):
                product = mm(left, work[k][j], 0, 0)
                work[i][j] = -product if j == k else work[i][j] - product
    for i in range(steps):
        for j in range(steps):
            value = work[i][j] if j <= i else jnp.zeros((LANES, LANES), F32)
            w_ref[i * LANES:(i + 1) * LANES, j * LANES:(j + 1) * LANES] = value


def inverse_factor(a):
    n = a.shape[0]
    return pl.pallas_call(
        inverse_factor_kernel,
        out_shape=jax.ShapeDtypeStruct((n, n), F32),
        in_specs=[pl.BlockSpec(memory_space=pltpu.VMEM)],
        out_specs=pl.BlockSpec(memory_space=pltpu.VMEM),
        compiler_params=pltpu.CompilerParams(vmem_limit_bytes=32 * 1024 * 1024),
        cost_estimate=pl.CostEstimate(flops=n * n * n, bytes_accessed=8 * n * n, transcendentals=0),
    )(a)


def spread_kernel(slot_ref, place_ref, part_ref, keep_ref, left_ref, factor_ref, piece_ref, out_ref):
    t = pl.program_id(0)
    whole = factor_ref[0]
    high = whole.astype(jnp.bfloat16)
    low = (whole - high.astype(F32)).astype(jnp.bfloat16)
    right = jnp.concatenate([high, low, high], axis=0)
    value = lax.dot_general(left_ref[...], right, (((1,), (0,)), ((), ())), preferred_element_type=F32)
    out_ref[0] = jnp.where(keep_ref[t] > 0, piece_ref[0] - value, 0.0)


def three_part(x):
    turned = x.T
    rounded = lax.reduce_precision(turned, 8, 7)
    high = rounded.astype(jnp.bfloat16)
    low = (turned - rounded).astype(jnp.bfloat16)
    return jnp.concatenate([high, high, low], axis=1)


def spread_update(slots, places, parts, keeps, left, factor, pieces, width):
    count = slots.shape[0]
    q, depth = left.shape[0], left.shape[1] // 3
    return pl.pallas_call(
        spread_kernel,
        grid_spec=pltpu.PrefetchScalarGridSpec(
            num_scalar_prefetch=4,
            grid=(count,),
            in_specs=[
                pl.BlockSpec((q, 3 * depth), lambda t, *refs: (0, 0)),
                pl.BlockSpec((1, depth, width), lambda t, s, p, h, k: (s[t], 0, h[t])),
                pl.BlockSpec((1, q, width), lambda t, s, p, h, k: (p[t], 0, h[t])),
            ],
            out_specs=pl.BlockSpec((1, q, width), lambda t, *refs: (t, 0, 0)),
        ),
        out_shape=jax.ShapeDtypeStruct((count, q, width), F32),
        compiler_params=pltpu.CompilerParams(vmem_limit_bytes=32 * 1024 * 1024),
        cost_estimate=pl.CostEstimate(
            flops=6 * count * q * depth * width,
            bytes_accessed=4 * count * width * (2 * q + depth), transcendentals=0),
    )(slots, places, parts, keeps, left, factor, pieces)


def product(a, b, ca, cb, precision=lax.Precision.HIGH):
    return lax.dot_general(a, b, (((ca,), (cb,)), ((), ())), precision=precision)


def flip(x, axis, bit):
    n = lax.axis_size(axis)
    return lax.ppermute(x, axis, [(i, i ^ bit) for i in range(n)])


def axis_bits(axis):
    return [1 << i for i in range(lax.axis_size(axis).bit_length() - 1)]


def halve(x, axis, steps=None):
    me = lax.axis_index(axis)
    for bit in axis_bits(axis):
        high = (me // bit) % 2
        half = x.shape[0] // 2
        away = lax.dynamic_slice_in_dim(x, (1 - high) * half, half, 0)
        x = lax.dynamic_slice_in_dim(x, high * half, half, 0) + flip(away, axis, bit)
        if steps is not None:
            steps.append(x)
    return x


def join(x, axis, steps=None):
    me = lax.axis_index(axis)
    for bit in reversed(axis_bits(axis)):
        high = (me // bit) % 2
        other = flip(x, axis, bit)
        x = jnp.concatenate([jnp.where(high == 0, x, other), jnp.where(high == 0, other, x)], axis=0)
        if steps is not None:
            steps.append(x)
    return x


def scatter_sum(parts, axis):
    parts = list(parts)
    for bit in axis_bits(axis):
        for m in reversed(range(len(parts))):
            if m & bit and not m & (bit - 1):
                parts[m ^ bit] = parts[m ^ bit] + flip(parts[m], axis, bit)
    return parts[0]


def line_gather(x, axis, ny):
    n = lax.axis_size(axis)
    nz = n // ny
    up, down = [x], [x]
    for step in range(1, nz):
        up.append(lax.ppermute(up[-1], axis, [(c, c + ny) for c in range(n) if step - 1 <= c // ny < nz - 1]))
        down.append(lax.ppermute(down[-1], axis, [(c, c - ny) for c in range(n) if 0 < c // ny <= nz - step]))

    def beside(y, j, rows):
        pairs = [(c, c // ny * ny + (c % ny - j) % ny) for c in range(n) if c // ny in rows]
        return lax.ppermute(y, axis, pairs)

    got = [[x] + [beside(x, j, range(nz)) for j in range(1, ny)]]
    for k in range(1, nz):
        above, below = range(k, nz), range(k)
        got.append([up[k] + down[nz - k]] + [
            beside(up[k], j, above) + beside(down[nz - k], j, below) for j in range(1, ny)])
    return got, list(zip(up[1:], down[1:]))


def share_line(x, ny):
    branches = lax.axis_size("branch")
    groups = lax.axis_size("col")
    nz = groups // ny
    place = lambda b, z, y: b * groups + z * ny + y
    got = jnp.where(lax.axis_index("col") // ny == lax.axis_index("branch"), x, 0.0)
    for off in range(1, nz):
        pairs = [(place(b, b, y), place(b, (b + off) % nz, y)) for b in range(branches) for y in range(ny)]
        got = got + lax.ppermute(x, ("branch", "col"), pairs)
    return got


def share_beside(got, ny):
    groups = lax.axis_size("col")
    y = lax.axis_index("col") % ny
    shares = [got]
    for j in range(1, ny):
        pairs = [(c, c // ny * ny + (c % ny - j) % ny) for c in range(groups)]
        shares.append(lax.ppermute(got, "col", pairs))
    return [sum(jnp.where(y == (i - j) % ny, shares[j], 0.0) for j in range(ny)) for i in range(ny)]


def on_device(child_fronts, extend_map, parent_front):
    front = child_fronts[0]
    order, ncols = front.shape
    nrows, pcols = parent_front.shape
    groups = lax.axis_size("col")
    branches = lax.axis_size("branch")
    ny = 1
    while 4 * ny * ny <= groups:
        ny *= 2
    nz = groups // ny
    width = min(BS, ncols)
    per = ncols // width
    ratio = BS // width
    units_total = NP // width
    col = lax.axis_index("col")
    branch = lax.axis_index("branch")
    pivot_devices = P_SIZE // ncols

    blocks = extend_map[0]
    hit = blocks[:, None] == jnp.arange(NP // BS, dtype=jnp.int32)[None, :]
    present = jnp.any(hit, axis=0).astype(jnp.int32)
    child_block = jnp.sum(
        jnp.where(hit, jnp.arange(blocks.shape[0], dtype=jnp.int32)[:, None], 0), axis=0
    ).astype(jnp.int32)
    t = jnp.arange(units_total, dtype=jnp.int32)
    units = P_SIZE // width + child_block[t // ratio] * ratio + t % ratio
    keeps = present[t // ratio]
    source = units // per
    parts = units % per

    def unit_rows(u):
        return lax.dynamic_slice_in_dim(front, units[u] * width, width, 0)

    def placed(x):
        if pivot_devices == 1:
            return jnp.where(col == 0, x, 0.0)
        wide = jnp.zeros((x.shape[0], P_SIZE), F32)
        wide = lax.dynamic_update_slice_in_dim(wide, x, jnp.minimum(col, pivot_devices - 1) * ncols, 1)
        return jnp.where(col < pivot_devices, wide, 0.0)

    gathered, ends = line_gather(front[:P_SIZE], "col", ny)
    nz = groups // ny
    z, y = col // ny, col % ny
    back = (z - source // ny) % nz
    aside = (source % ny - y) % ny
    slots = back * ny + aside

    def top_of(c):
        return sum(
            jnp.where((z == (c // ny + k) % nz) & (y == (c % ny - j) % ny), gathered[k][j], 0.0)
            for k in range(nz) for j in range(ny))

    pivots = [top_of(c) for c in range(pivot_devices)]
    pivots = jnp.concatenate(pivots, axis=1) if pivot_devices > 1 else pivots[0]

    pivot_units = PP // width

    def pivot_column(b):
        local = units[b] - col * per
        ok = (local >= 0) & (local < per) & (keeps[b] > 0)
        column = lax.dynamic_slice_in_dim(front, jnp.clip(local, 0, per - 1) * width, width, 1)
        body = [
            jnp.where(ok & (keeps[a] > 0), lax.dynamic_slice_in_dim(column, units[a] * width, width, 0), 0.0)
            for a in range(pivot_units)
        ]
        return jnp.concatenate(body, axis=0)

    corner = jnp.concatenate([pivot_column(b) for b in range(pivot_units)], axis=1)
    corner = corner + jnp.where(branch == 0, placed(parent_front[:PP]), 0.0)
    corner = lax.psum(halve(corner, "branch"), "col")

    def rows_for(target):
        return jnp.concatenate([unit_rows(target * per + a) for a in range(per)], axis=0)

    def moved(shift, rows):
        pairs = [(c, (c + shift) % groups) for c in range(groups) if c >= pivot_devices]
        return lax.ppermute(rows, "col", pairs)

    far = sorted(range(1, groups), key=lambda shift: abs(2 * shift - groups))
    received = {0: rows_for(col)}
    for shift in far[:EARLY]:
        rows, _ = lax.optimization_barrier((rows_for((col + shift) % groups), ends[-1]))
        received[shift] = moved(shift, rows)

    inverse = inverse_factor(pivots)
    for shift in far[EARLY:]:
        rows, _ = lax.optimization_barrier((rows_for((col + shift) % groups), inverse))
        received[shift] = moved(shift, rows)
    places = (col - source) % groups
    child_mine = product(inverse, front[:P_SIZE], 1, 0)

    early = [received[shift] for shift in far[:EARLY]]
    inverse, early, corner = lax.optimization_barrier((inverse, early, corner))
    received.update(zip(far[:EARLY], early))
    factor = jnp.stack([product(inverse, x, 1, 0) for line in gathered for x in line])

    def factor_columns(u):
        block = lax.dynamic_slice(factor, (slots[u], 0, parts[u] * width), (1, P_SIZE, width))
        return jnp.where(keeps[u] > 0, block[0], 0.0)

    mine = jnp.concatenate([factor_columns(col * per + a) for a in range(per)], axis=1)
    mine_keep = jnp.repeat(lax.dynamic_slice_in_dim(keeps, col * per, per), width)[:, None] > 0
    pieces = jnp.stack([jnp.where(mine_keep, received[shift], 0.0) for shift in range(groups)])
    left = three_part(mine)
    n = pivot_units
    first = spread_update(slots[:n], places[:n], parts[:n], keeps[:n], left, factor, pieces, width)
    first = jnp.concatenate([first[u] for u in range(n)], axis=1)
    steps = []
    first = first + jnp.where(branch == 0, parent_front[:PP].T, 0.0)
    first = join(halve(first, "branch", steps), "branch", steps)

    head = jnp.concatenate([factor_columns(u) for u in range(pivot_units)], axis=1)
    head, _ = lax.optimization_barrier((head, received[far[EARLY]]))
    corner = corner - halve(product(head, head, 0, 0), "branch")
    corner, _ = lax.optimization_barrier((corner, received[far[-1]]))
    parent_inverse = inverse_factor(join(corner, "branch"))

    owned = units_total // branches
    order = list(reversed(range(branches)))
    spread = [None] * branches
    for i, m in enumerate(order):
        gated, _ = lax.optimization_barrier((left, steps[min(i, len(steps) - 1)]))
        at = lambda table: lax.dynamic_slice_in_dim(table, (branch ^ m) * owned, owned)
        spread[m] = spread_update(at(slots), at(places), at(parts), at(keeps), gated, factor, pieces, width)
    added = scatter_sum(spread, "branch")
    assembled = parent_front + jnp.transpose(added, (0, 2, 1)).reshape(nrows, pcols)

    parent_mine = product(parent_inverse, first, 1, 1)
    if nz == branches:
        line, parent_inverse = lax.optimization_barrier((share_line(first, ny), parent_inverse))
        sides = share_beside(line, ny)
    else:
        sides = lax.dynamic_slice_in_dim(
            lax.all_gather(first, "col"), branch * groups // branches, groups // branches, 0)
        sides = [sides[i] for i in range(groups // branches)]
    results = []
    for i, side in enumerate(sides):
        rows = assembled[i * pcols:(i + 1) * pcols]
        results.append(rows - product(product(side, parent_inverse, 1, 1), parent_mine, 1, 0))
    return (child_mine[None], parent_mine, jnp.concatenate(results, axis=0))


def solution(mesh):
    in_specs = (P("branch", None, "col"), P("branch", None), P("branch", "col"))
    out_specs = (P("branch", None, "col"), P(None, "col"), P("branch", "col"))
    return jax.shard_map(
        on_device, mesh=mesh, in_specs=in_specs, out_specs=out_specs, check_vma=False
    )
```

```python
import jax
import jax.numpy as jnp
from jax import lax
from jax.experimental import pallas as pl
from jax.experimental.pallas import tpu as pltpu
from jax.sharding import PartitionSpec as P

BS = 256
P_SIZE = 512
NP = 4096
PP = 512
EARLY = 5

SUB = 8
LANES = 128
F32 = jnp.float32


def mm(a, b, ca, cb):
    return lax.dot_general(
        a, b, (((ca,), (cb,)), ((), ())),
        precision=lax.Precision.HIGHEST, preferred_element_type=F32,
    )


def factor_tile(rows):
    sub = lax.broadcasted_iota(jnp.int32, (SUB, LANES), 0)
    lane = lax.broadcasted_iota(jnp.int32, (SUB, LANES), 1)
    rows = list(rows)
    count = len(rows)
    spread = lambda column: jnp.broadcast_to(column, (SUB, LANES))
    for g in range(count):
        base = g * SUB
        inside = (lane >= base) & (lane < base + SUB)
        cols = [spread(rows[g][:, base + j:base + j + 1]) for j in range(SUB)]
        panel = jnp.where(inside, jnp.where(lane - base == sub, 1.0, 0.0), rows[g])
        kept = panel
        pivots = cols[0]
        for j in range(SUB):
            here = sub == j
            pivot = spread(cols[j][j:j + 1, :])
            inverse = 1.0 / pivot
            scaled = cols[j] * inverse
            row = spread(panel[j:j + 1, :])
            kept = jnp.where(here, panel, kept)
            pivots = jnp.where(here, pivot, pivots)
            panel = jnp.where(here, row * inverse, panel - scaled * row)
            for m in range(j + 1, SUB):
                across = spread(cols[m][j:j + 1, :])
                cols[m] = jnp.where(here, across * inverse, cols[m] - scaled * across)
        rows[g] = kept * lax.rsqrt(pivots)
        panel_rows = [spread(panel[j:j + 1, :]) for j in range(SUB)]
        for i in range(g + 1, count):
            terms = [spread(rows[i][:, base + j:base + j + 1]) * panel_rows[j] for j in range(SUB)]
            while len(terms) > 1:
                terms = [terms[t] + terms[t + 1] for t in range(0, len(terms), 2)]
            rows[i] = jnp.where(inside, 0.0, rows[i]) - terms[0]
    return rows


def inverse_factor_kernel(a_ref, w_ref):
    n = a_ref.shape[0]
    steps = n // LANES
    tri = (lax.broadcasted_iota(jnp.int32, (LANES, LANES), 0)
           >= lax.broadcasted_iota(jnp.int32, (LANES, LANES), 1))
    work = [[a_ref[i * LANES:(i + 1) * LANES, j * LANES:(j + 1) * LANES]
             for j in range(steps)] for i in range(steps)]
    for k in range(steps):
        tile = work[k][k]
        done = factor_tile([tile[g * SUB:(g + 1) * SUB, :] for g in range(LANES // SUB)])
        inv = jnp.where(tri, jnp.concatenate(done, axis=0), 0.0)
        work[k] = [inv if j == k else mm(inv, work[k][j], 1, 0) for j in range(steps)]
        for i in range(k + 1, steps):
            left = work[k][i]
            for j in range(steps):
                product = mm(left, work[k][j], 0, 0)
                work[i][j] = -product if j == k else work[i][j] - product
    for i in range(steps):
        for j in range(steps):
            value = work[i][j] if j <= i else jnp.zeros((LANES, LANES), F32)
            w_ref[i * LANES:(i + 1) * LANES, j * LANES:(j + 1) * LANES] = value


def inverse_factor(a):
    n = a.shape[0]
    return pl.pallas_call(
        inverse_factor_kernel,
        out_shape=jax.ShapeDtypeStruct((n, n), F32),
        in_specs=[pl.BlockSpec(memory_space=pltpu.VMEM)],
        out_specs=pl.BlockSpec(memory_space=pltpu.VMEM),
        compiler_params=pltpu.CompilerParams(vmem_limit_bytes=32 * 1024 * 1024),
        cost_estimate=pl.CostEstimate(flops=n * n * n, bytes_accessed=8 * n * n, transcendentals=0),
    )(a)


def spread_kernel(slot_ref, place_ref, part_ref, keep_ref, left_ref, factor_ref, piece_ref, out_ref):
    t = pl.program_id(0)
    whole = factor_ref[0]
    high = whole.astype(jnp.bfloat16)
    low = (whole - high.astype(F32)).astype(jnp.bfloat16)
    right = jnp.concatenate([high, low, high], axis=0)
    value = lax.dot_general(left_ref[...], right, (((1,), (0,)), ((), ())), preferred_element_type=F32)
    out_ref[0] = jnp.where(keep_ref[t] > 0, piece_ref[0] - value, 0.0)


def three_part(x):
    turned = x.T
    rounded = lax.reduce_precision(turned, 8, 7)
    high = rounded.astype(jnp.bfloat16)
    low = (turned - rounded).astype(jnp.bfloat16)
    return jnp.concatenate([high, high, low], axis=1)


def spread_update(slots, places, parts, keeps, left, factor, pieces, width):
    count = slots.shape[0]
    q, depth = left.shape[0], left.shape[1] // 3
    return pl.pallas_call(
        spread_kernel,
        grid_spec=pltpu.PrefetchScalarGridSpec(
            num_scalar_prefetch=4,
            grid=(count,),
            in_specs=[
                pl.BlockSpec((q, 3 * depth), lambda t, *refs: (0, 0)),
                pl.BlockSpec((1, depth, width), lambda t, s, p, h, k: (s[t], 0, h[t])),
                pl.BlockSpec((1, q, width), lambda t, s, p, h, k: (p[t], 0, h[t])),
            ],
            out_specs=pl.BlockSpec((1, q, width), lambda t, *refs: (t, 0, 0)),
        ),
        out_shape=jax.ShapeDtypeStruct((count, q, width), F32),
        compiler_params=pltpu.CompilerParams(vmem_limit_bytes=56 * 1024 * 1024),
        cost_estimate=pl.CostEstimate(
            flops=6 * count * q * depth * width,
            bytes_accessed=4 * count * width * (2 * q + depth), transcendentals=0),
    )(slots, places, parts, keeps, left, factor, pieces)


def product(a, b, ca, cb, precision=lax.Precision.HIGH):
    return lax.dot_general(a, b, (((ca,), (cb,)), ((), ())), precision=precision)


def flip(x, axis, bit):
    n = lax.axis_size(axis)
    return lax.ppermute(x, axis, [(i, i ^ bit) for i in range(n)])


def axis_bits(axis):
    return [1 << i for i in range(lax.axis_size(axis).bit_length() - 1)]


def halve(x, axis, steps=None):
    me = lax.axis_index(axis)
    for bit in axis_bits(axis):
        high = (me // bit) % 2
        half = x.shape[0] // 2
        away = lax.dynamic_slice_in_dim(x, (1 - high) * half, half, 0)
        x = lax.dynamic_slice_in_dim(x, high * half, half, 0) + flip(away, axis, bit)
        if steps is not None:
            steps.append(x)
    return x


def join(x, axis, steps=None):
    me = lax.axis_index(axis)
    for bit in reversed(axis_bits(axis)):
        high = (me // bit) % 2
        other = flip(x, axis, bit)
        x = jnp.concatenate([jnp.where(high == 0, x, other), jnp.where(high == 0, other, x)], axis=0)
        if steps is not None:
            steps.append(x)
    return x


def scatter_sum(parts, axis):
    parts = list(parts)
    terms = [parts[0]]
    for bit in axis_bits(axis):
        for m in reversed(range(len(parts))):
            if m & bit and not m & (bit - 1):
                sent = parts[m]
                other = flip(sent, axis, bit)
                if m == bit:
                    terms.append(other)
                else:
                    parts[m ^ bit] = parts[m ^ bit] + other
    return terms, sent


def three_rows(x):
    high = x.astype(jnp.bfloat16)
    return high, (x - high.astype(F32)).astype(jnp.bfloat16)


def finish_kernel(parent_ref, side_ref, inverse_ref, mine_ref, *rest):
    terms, out_ref = rest[:-1], rest[-1]
    total = terms[0][0]
    for term in terms[1:]:
        total = total + term[0]
    dot = lambda a, b, cb: lax.dot_general(a, b, (((1,), (cb,)), ((), ())), preferred_element_type=F32)
    high, low = three_rows(side_ref[0])
    ihigh, ilow = three_rows(inverse_ref[...])
    factor = dot(jnp.concatenate([high, high, low], axis=1), jnp.concatenate([ihigh, ilow, ihigh], axis=1), 1)
    high, low = three_rows(factor)
    mhigh, mlow = three_rows(mine_ref[...])
    outer = dot(jnp.concatenate([high, high, low], axis=1), jnp.concatenate([mhigh, mlow, mhigh], axis=0), 0)
    out_ref[...] = parent_ref[...] + total.T - outer


def finish(parent, terms, sides, inverse, mine):
    count, q, width = terms[0].shape
    depth = inverse.shape[0]
    sides = sides.reshape(count, width, depth)
    whole = lambda t: (0, 0)
    block = lambda t: (t, 0, 0)
    return pl.pallas_call(
        finish_kernel,
        grid=(count,),
        in_specs=[
            pl.BlockSpec((width, q), lambda t: (t, 0)),
            pl.BlockSpec((1, width, depth), block),
            pl.BlockSpec((depth, depth), whole),
            pl.BlockSpec((depth, q), whole),
        ] + [pl.BlockSpec((1, q, width), block)] * len(terms),
        out_specs=pl.BlockSpec((width, q), lambda t: (t, 0)),
        out_shape=jax.ShapeDtypeStruct(parent.shape, F32),
        compiler_params=pltpu.CompilerParams(vmem_limit_bytes=48 * 1024 * 1024),
        cost_estimate=pl.CostEstimate(
            flops=6 * count * width * depth * (q + depth), bytes_accessed=8 * parent.size * 4, transcendentals=0),
    )(parent, sides, inverse, mine, *terms)


def line_gather(x, axis, ny, gates):
    n = lax.axis_size(axis)
    nz = n // ny

    def beside(y, j, rows):
        pairs = [(c, c // ny * ny + (c % ny - j) % ny) for c in range(n) if c // ny in rows]
        return lax.ppermute(y, axis, pairs)

    own = [beside(x, j, range(nz)) for j in range(1, ny)]
    up, down = [x], [x]
    for step in range(1, nz):
        ends = (up[-1], down[-1])
        if 1 < step < len(gates) + 2:
            ends, _ = lax.optimization_barrier((ends, gates[step - 2](own)))
        up.append(lax.ppermute(ends[0], axis, [(c, c + ny) for c in range(n) if step - 1 <= c // ny < nz - 1]))
        down.append(lax.ppermute(ends[1], axis, [(c, c - ny) for c in range(n) if 0 < c // ny <= nz - step]))
    got = [[x] + own]
    for k in range(1, nz):
        above, below = range(k, nz), range(k)
        got.append([up[k] + down[nz - k]] + [
            beside(up[k], j, above) + beside(down[nz - k], j, below) for j in range(1, ny)])
    return got, (up[-1], down[-1])


def share_line(x, ny):
    branches = lax.axis_size("branch")
    groups = lax.axis_size("col")
    nz = groups // ny
    place = lambda b, z, y: b * groups + z * ny + y
    got = jnp.where(lax.axis_index("col") // ny == lax.axis_index("branch"), x, 0.0)
    for off in range(1, nz):
        pairs = [(place(b, b, y), place(b, (b + off) % nz, y)) for b in range(branches) for y in range(ny)]
        got = got + lax.ppermute(x, ("branch", "col"), pairs)
    return got


def share_beside(got, ny):
    groups = lax.axis_size("col")
    y = lax.axis_index("col") % ny
    shares = [got]
    for j in range(1, ny):
        pairs = [(c, c // ny * ny + (c % ny - j) % ny) for c in range(groups)]
        shares.append(lax.ppermute(got, "col", pairs))
    return [sum(jnp.where(y == (i - j) % ny, shares[j], 0.0) for j in range(ny)) for i in range(ny)]


def on_device(child_fronts, extend_map, parent_front):
    front = child_fronts[0]
    order, ncols = front.shape
    nrows, pcols = parent_front.shape
    groups = lax.axis_size("col")
    branches = lax.axis_size("branch")
    ny = 1
    while 4 * ny * ny <= groups:
        ny *= 2
    nz = groups // ny
    width = min(BS, ncols)
    per = ncols // width
    ratio = BS // width
    units_total = NP // width
    col = lax.axis_index("col")
    branch = lax.axis_index("branch")
    pivot_devices = P_SIZE // ncols

    blocks = extend_map[0]
    hit = blocks[:, None] == jnp.arange(NP // BS, dtype=jnp.int32)[None, :]
    present = jnp.any(hit, axis=0).astype(jnp.int32)
    child_block = jnp.sum(
        jnp.where(hit, jnp.arange(blocks.shape[0], dtype=jnp.int32)[:, None], 0), axis=0
    ).astype(jnp.int32)
    t = jnp.arange(units_total, dtype=jnp.int32)
    units = P_SIZE // width + child_block[t // ratio] * ratio + t % ratio
    keeps = present[t // ratio]
    source = units // per
    parts = units % per

    def unit_rows(u):
        return lax.dynamic_slice_in_dim(front, units[u] * width, width, 0)

    def placed(x):
        if pivot_devices == 1:
            return jnp.where(col == 0, x, 0.0)
        wide = jnp.zeros((x.shape[0], P_SIZE), F32)
        wide = lax.dynamic_update_slice_in_dim(wide, x, jnp.minimum(col, pivot_devices - 1) * ncols, 1)
        return jnp.where(col < pivot_devices, wide, 0.0)

    pivot_units = PP // width

    def pivot_column(b):
        local = units[b] - col * per
        ok = (local >= 0) & (local < per) & (keeps[b] > 0)
        column = lax.dynamic_slice_in_dim(front, jnp.clip(local, 0, per - 1) * width, width, 1)
        body = [
            jnp.where(ok & (keeps[a] > 0), lax.dynamic_slice_in_dim(column, units[a] * width, width, 0), 0.0)
            for a in range(pivot_units)
        ]
        return jnp.concatenate(body, axis=0)

    corner = jnp.concatenate([pivot_column(b) for b in range(pivot_units)], axis=1)
    corner = corner + jnp.where(branch == 0, placed(parent_front[:PP]), 0.0)
    corner_steps = []
    corner = halve(corner, "branch", corner_steps)
    corner = halve(corner, "col", corner_steps)
    corner = join(corner, "col", corner_steps)

    def rows_for(target):
        return jnp.concatenate([unit_rows(target * per + a) for a in range(per)], axis=0)

    def moved(shift, rows):
        pairs = [(c, (c + shift) % groups) for c in range(groups) if c >= pivot_devices]
        return lax.ppermute(rows, "col", pairs)

    far = sorted(range(1, groups), key=lambda shift: abs(2 * shift - groups))
    rows = [rows_for((col + shift) % groups) for shift in far]

    in_branch, in_col = len(axis_bits("branch")), len(axis_bits("col"))
    gathered, ends = line_gather(front[:P_SIZE], "col", ny, [
        lambda own: (own, rows, corner_steps[in_branch - 1]), lambda own: corner_steps[in_branch + in_col - 1]])
    nz = groups // ny
    z, y = col // ny, col % ny
    back = (z - source // ny) % nz
    aside = (source % ny - y) % ny
    slots = back * ny + aside

    def top_of(c):
        return sum(
            jnp.where((z == (c // ny + k) % nz) & (y == (c % ny - j) % ny), gathered[k][j], 0.0)
            for k in range(nz) for j in range(ny))

    pivots = [top_of(c) for c in range(pivot_devices)]
    pivots = jnp.concatenate(pivots, axis=1) if pivot_devices > 1 else pivots[0]

    received = {0: rows_for(col)}
    for shift, row in zip(far[:EARLY], rows):
        row, _ = lax.optimization_barrier((row, (ends, corner)))
        received[shift] = moved(shift, row)

    inverse = inverse_factor(pivots)
    for shift, row in zip(far[EARLY:], rows[EARLY:]):
        row, _ = lax.optimization_barrier((row, inverse))
        received[shift] = moved(shift, row)
    places = (col - source) % groups
    child_mine = product(inverse, front[:P_SIZE], 1, 0)

    early = [received[shift] for shift in far[:EARLY]]
    inverse, early = lax.optimization_barrier((inverse, early))
    received.update(zip(far[:EARLY], early))
    factor = jnp.stack([product(inverse, x, 1, 0) for line in gathered for x in line])

    def factor_columns(u):
        block = lax.dynamic_slice(factor, (slots[u], 0, parts[u] * width), (1, P_SIZE, width))
        return jnp.where(keeps[u] > 0, block[0], 0.0)

    mine = jnp.concatenate([factor_columns(col * per + a) for a in range(per)], axis=1)
    mine_keep = jnp.repeat(lax.dynamic_slice_in_dim(keeps, col * per, per), width)[:, None] > 0
    pieces = jnp.stack([jnp.where(mine_keep, received[shift], 0.0) for shift in range(groups)])
    left = three_part(mine)
    n = pivot_units
    first = spread_update(slots[:n], places[:n], parts[:n], keeps[:n], left, factor, pieces, width)
    first = jnp.concatenate([first[u] for u in range(n)], axis=1)
    steps = []
    first = first + jnp.where(branch == 0, parent_front[:PP].T, 0.0)
    first = join(halve(first, "branch", steps), "branch", steps)

    head = jnp.concatenate([factor_columns(u) for u in range(pivot_units)], axis=1)
    head, _ = lax.optimization_barrier((head, received[far[EARLY]]))
    corner = corner - halve(product(head, head, 0, 0), "branch")
    corner, _ = lax.optimization_barrier((corner, received[far[-1]]))
    corner = join(corner, "branch")

    owned = units_total // branches
    spread = [None] * branches
    for i, m in enumerate(reversed(range(branches))):
        table, _ = lax.optimization_barrier((slots, steps[min(i, len(steps) - 1)]))
        at = lambda table: lax.dynamic_slice_in_dim(table, (branch ^ m) * owned, owned)
        spread[m] = spread_update(at(table), at(places), at(parts), at(keeps), left, factor, pieces, width)
    terms, sent = scatter_sum(spread, "branch")
    corner, _ = lax.optimization_barrier((corner, sent))
    parent_inverse = inverse_factor(corner)

    parent_mine = product(parent_inverse, first, 1, 1)
    if nz == branches:
        line, parent_inverse = lax.optimization_barrier((share_line(first, ny), parent_inverse))
        sides = jnp.concatenate(share_beside(line, ny), axis=0)
    else:
        sides = lax.dynamic_slice_in_dim(
            lax.all_gather(first, "col"), branch * groups // branches, groups // branches, 0).reshape(nrows, PP)
    result = finish(parent_front, terms, sides, parent_inverse, parent_mine)
    return (child_mine[None], parent_mine, result)


def solution(mesh):
    in_specs = (P("branch", None, "col"), P("branch", None), P("branch", "col"))
    out_specs = (P("branch", None, "col"), P(None, "col"), P("branch", "col"))
    return jax.shard_map(
        on_device, mesh=mesh, in_specs=in_specs, out_specs=out_specs, check_vma=False
    )
```

```python
import jax
import jax.numpy as jnp
from jax import lax
from jax.experimental import pallas as pl
from jax.experimental.pallas import tpu as pltpu
from jax.sharding import PartitionSpec as P

BS = 256
P_SIZE = 512
NP = 4096
PP = 512
EARLY = 5

SUB = 8
LANES = 128
F32 = jnp.float32


def mm(a, b, ca, cb):
    return lax.dot_general(
        a, b, (((ca,), (cb,)), ((), ())),
        precision=lax.Precision.HIGHEST, preferred_element_type=F32,
    )


def factor_tile(rows):
    sub = lax.broadcasted_iota(jnp.int32, (SUB, LANES), 0)
    lane = lax.broadcasted_iota(jnp.int32, (SUB, LANES), 1)
    rows = list(rows)
    count = len(rows)
    spread = lambda column: jnp.broadcast_to(column, (SUB, LANES))
    for g in range(count):
        base = g * SUB
        inside = (lane >= base) & (lane < base + SUB)
        cols = [spread(rows[g][:, base + j:base + j + 1]) for j in range(SUB)]
        panel = jnp.where(inside, jnp.where(lane - base == sub, 1.0, 0.0), rows[g])
        kept = panel
        pivots = cols[0]
        for j in range(SUB):
            here = sub == j
            pivot = spread(cols[j][j:j + 1, :])
            inverse = 1.0 / pivot
            scaled = cols[j] * inverse
            row = spread(panel[j:j + 1, :])
            kept = jnp.where(here, panel, kept)
            pivots = jnp.where(here, pivot, pivots)
            panel = jnp.where(here, row * inverse, panel - scaled * row)
            for m in range(j + 1, SUB):
                across = spread(cols[m][j:j + 1, :])
                cols[m] = jnp.where(here, across * inverse, cols[m] - scaled * across)
        rows[g] = kept * lax.rsqrt(pivots)
        panel_rows = [spread(panel[j:j + 1, :]) for j in range(SUB)]
        for i in range(g + 1, count):
            terms = [spread(rows[i][:, base + j:base + j + 1]) * panel_rows[j] for j in range(SUB)]
            while len(terms) > 1:
                terms = [terms[t] + terms[t + 1] for t in range(0, len(terms), 2)]
            rows[i] = jnp.where(inside, 0.0, rows[i]) - terms[0]
    return rows


def inverse_factor_kernel(a_ref, w_ref):
    n = a_ref.shape[0]
    steps = n // LANES
    tri = (lax.broadcasted_iota(jnp.int32, (LANES, LANES), 0)
           >= lax.broadcasted_iota(jnp.int32, (LANES, LANES), 1))
    work = [[a_ref[i * LANES:(i + 1) * LANES, j * LANES:(j + 1) * LANES]
             for j in range(steps)] for i in range(steps)]
    for k in range(steps):
        tile = work[k][k]
        done = factor_tile([tile[g * SUB:(g + 1) * SUB, :] for g in range(LANES // SUB)])
        inv = jnp.where(tri, jnp.concatenate(done, axis=0), 0.0)
        work[k] = [inv if j == k else mm(inv, work[k][j], 1, 0) for j in range(steps)]
        for i in range(k + 1, steps):
            left = work[k][i]
            for j in range(steps):
                product = mm(left, work[k][j], 0, 0)
                work[i][j] = -product if j == k else work[i][j] - product
    for i in range(steps):
        for j in range(steps):
            value = work[i][j] if j <= i else jnp.zeros((LANES, LANES), F32)
            w_ref[i * LANES:(i + 1) * LANES, j * LANES:(j + 1) * LANES] = value


def inverse_factor(a):
    n = a.shape[0]
    return pl.pallas_call(
        inverse_factor_kernel,
        out_shape=jax.ShapeDtypeStruct((n, n), F32),
        in_specs=[pl.BlockSpec(memory_space=pltpu.VMEM)],
        out_specs=pl.BlockSpec(memory_space=pltpu.VMEM),
        compiler_params=pltpu.CompilerParams(vmem_limit_bytes=32 * 1024 * 1024),
        cost_estimate=pl.CostEstimate(flops=n * n * n, bytes_accessed=8 * n * n, transcendentals=0),
    )(a)


def spread_kernel(slot_ref, place_ref, part_ref, keep_ref, left_ref, factor_ref, piece_ref, out_ref):
    t = pl.program_id(0)
    whole = factor_ref[0]
    high = whole.astype(jnp.bfloat16)
    low = (whole - high.astype(F32)).astype(jnp.bfloat16)
    right = jnp.concatenate([high, low, high], axis=0)
    value = lax.dot_general(left_ref[...], right, (((1,), (0,)), ((), ())), preferred_element_type=F32)
    out_ref[0] = jnp.where(keep_ref[t] > 0, piece_ref[0] - value, 0.0)


def three_part(x):
    turned = x.T
    rounded = lax.reduce_precision(turned, 8, 7)
    high = rounded.astype(jnp.bfloat16)
    low = (turned - rounded).astype(jnp.bfloat16)
    return jnp.concatenate([high, high, low], axis=1)


def spread_update(slots, places, parts, keeps, left, factor, pieces, width):
    count = slots.shape[0]
    q, depth = left.shape[0], left.shape[1] // 3
    return pl.pallas_call(
        spread_kernel,
        grid_spec=pltpu.PrefetchScalarGridSpec(
            num_scalar_prefetch=4,
            grid=(count,),
            in_specs=[
                pl.BlockSpec((q, 3 * depth), lambda t, *refs: (0, 0)),
                pl.BlockSpec((1, depth, width), lambda t, s, p, h, k: (s[t], 0, h[t])),
                pl.BlockSpec((1, q, width), lambda t, s, p, h, k: (p[t], 0, h[t])),
            ],
            out_specs=pl.BlockSpec((1, q, width), lambda t, *refs: (t, 0, 0)),
        ),
        out_shape=jax.ShapeDtypeStruct((count, q, width), F32),
        compiler_params=pltpu.CompilerParams(vmem_limit_bytes=56 * 1024 * 1024),
        cost_estimate=pl.CostEstimate(
            flops=6 * count * q * depth * width,
            bytes_accessed=4 * count * width * (2 * q + depth), transcendentals=0),
    )(slots, places, parts, keeps, left, factor, pieces)


def product(a, b, ca, cb, precision=lax.Precision.HIGH):
    return lax.dot_general(a, b, (((ca,), (cb,)), ((), ())), precision=precision)


def flip(x, axis, bit):
    n = lax.axis_size(axis)
    return lax.ppermute(x, axis, [(i, i ^ bit) for i in range(n)])


def axis_bits(axis):
    return [1 << i for i in range(lax.axis_size(axis).bit_length() - 1)]


def halve(x, axis, steps=None):
    me = lax.axis_index(axis)
    for bit in axis_bits(axis):
        high = (me // bit) % 2
        half = x.shape[0] // 2
        away = lax.dynamic_slice_in_dim(x, (1 - high) * half, half, 0)
        x = lax.dynamic_slice_in_dim(x, high * half, half, 0) + flip(away, axis, bit)
        if steps is not None:
            steps.append(x)
    return x


def join(x, axis, steps=None):
    me = lax.axis_index(axis)
    for bit in reversed(axis_bits(axis)):
        high = (me // bit) % 2
        other = flip(x, axis, bit)
        x = jnp.concatenate([jnp.where(high == 0, x, other), jnp.where(high == 0, other, x)], axis=0)
        if steps is not None:
            steps.append(x)
    return x


def scatter_sum(parts, axis):
    parts = list(parts)
    terms = [parts[0]]
    for bit in axis_bits(axis):
        for m in reversed(range(len(parts))):
            if m & bit and not m & (bit - 1):
                sent = parts[m]
                other = flip(sent, axis, bit)
                if m == bit:
                    terms.append(other)
                else:
                    parts[m ^ bit] = parts[m ^ bit] + other
    return terms, sent


def three_rows(x):
    high = x.astype(jnp.bfloat16)
    return high, (x - high.astype(F32)).astype(jnp.bfloat16)


def finish_kernel(parent_ref, side_ref, inverse_ref, mine_ref, *rest):
    terms, out_ref = rest[:-1], rest[-1]
    total = terms[0][0]
    for term in terms[1:]:
        total = total + term[0]
    dot = lambda a, b, cb: lax.dot_general(a, b, (((1,), (cb,)), ((), ())), preferred_element_type=F32)
    high, low = three_rows(side_ref[0])
    ihigh, ilow = three_rows(inverse_ref[...])
    factor = dot(jnp.concatenate([high, high, low], axis=1), jnp.concatenate([ihigh, ilow, ihigh], axis=1), 1)
    high, low = three_rows(factor)
    mhigh, mlow = three_rows(mine_ref[...])
    outer = dot(jnp.concatenate([high, high, low], axis=1), jnp.concatenate([mhigh, mlow, mhigh], axis=0), 0)
    out_ref[...] = parent_ref[...] + total.T - outer


def finish(parent, terms, sides, inverse, mine):
    count, q, width = terms[0].shape
    depth = inverse.shape[0]
    sides = sides.reshape(count, width, depth)
    whole = lambda t: (0, 0)
    block = lambda t: (t, 0, 0)
    return pl.pallas_call(
        finish_kernel,
        grid=(count,),
        in_specs=[
            pl.BlockSpec((width, q), lambda t: (t, 0)),
            pl.BlockSpec((1, width, depth), block),
            pl.BlockSpec((depth, depth), whole),
            pl.BlockSpec((depth, q), whole),
        ] + [pl.BlockSpec((1, q, width), block)] * len(terms),
        out_specs=pl.BlockSpec((width, q), lambda t: (t, 0)),
        out_shape=jax.ShapeDtypeStruct(parent.shape, F32),
        compiler_params=pltpu.CompilerParams(vmem_limit_bytes=48 * 1024 * 1024),
        cost_estimate=pl.CostEstimate(
            flops=6 * count * width * depth * (q + depth), bytes_accessed=8 * parent.size * 4, transcendentals=0),
    )(parent, sides, inverse, mine, *terms)


def share_line(x, ny):
    branches = lax.axis_size("branch")
    groups = lax.axis_size("col")
    nz = groups // ny
    place = lambda b, z, y: b * groups + z * ny + y
    got = jnp.where(lax.axis_index("col") // ny == lax.axis_index("branch"), x, 0.0)
    for off in range(1, nz):
        pairs = [(place(b, b, y), place(b, (b + off) % nz, y)) for b in range(branches) for y in range(ny)]
        got = got + lax.ppermute(x, ("branch", "col"), pairs)
    return got


def share_beside(got, ny):
    groups = lax.axis_size("col")
    y = lax.axis_index("col") % ny
    shares = [got]
    for j in range(1, ny):
        pairs = [(c, c // ny * ny + (c % ny - j) % ny) for c in range(groups)]
        shares.append(lax.ppermute(got, "col", pairs))
    return [sum(jnp.where(y == (i - j) % ny, shares[j], 0.0) for j in range(ny)) for i in range(ny)]


def on_device(child_fronts, extend_map, parent_front):
    front = child_fronts[0]
    order, ncols = front.shape
    nrows, pcols = parent_front.shape
    groups = lax.axis_size("col")
    branches = lax.axis_size("branch")
    ny = 1
    while 4 * ny * ny <= groups:
        ny *= 2
    nz = groups // ny
    width = min(BS, ncols)
    per = ncols // width
    ratio = BS // width
    units_total = NP // width
    col = lax.axis_index("col")
    branch = lax.axis_index("branch")
    pivot_devices = P_SIZE // ncols

    blocks = extend_map[0]
    hit = blocks[:, None] == jnp.arange(NP // BS, dtype=jnp.int32)[None, :]
    present = jnp.any(hit, axis=0).astype(jnp.int32)
    child_block = jnp.sum(
        jnp.where(hit, jnp.arange(blocks.shape[0], dtype=jnp.int32)[:, None], 0), axis=0
    ).astype(jnp.int32)
    t = jnp.arange(units_total, dtype=jnp.int32)
    units = P_SIZE // width + child_block[t // ratio] * ratio + t % ratio
    keeps = present[t // ratio]
    source = units // per
    parts = units % per

    def unit_rows(u):
        return lax.dynamic_slice_in_dim(front, units[u] * width, width, 0)

    def placed(x):
        if pivot_devices == 1:
            return jnp.where(col == 0, x, 0.0)
        wide = jnp.zeros((x.shape[0], P_SIZE), F32)
        wide = lax.dynamic_update_slice_in_dim(wide, x, jnp.minimum(col, pivot_devices - 1) * ncols, 1)
        return jnp.where(col < pivot_devices, wide, 0.0)

    pivot_units = PP // width

    def pivot_column(b):
        local = units[b] - col * per
        ok = (local >= 0) & (local < per) & (keeps[b] > 0)
        column = lax.dynamic_slice_in_dim(front, jnp.clip(local, 0, per - 1) * width, width, 1)
        body = [
            jnp.where(ok & (keeps[a] > 0), lax.dynamic_slice_in_dim(column, units[a] * width, width, 0), 0.0)
            for a in range(pivot_units)
        ]
        return jnp.concatenate(body, axis=0)

    corner = jnp.concatenate([pivot_column(b) for b in range(pivot_units)], axis=1)
    corner = corner + jnp.where(branch == 0, placed(parent_front[:PP]), 0.0)
    corner = join(halve(halve(corner, "branch"), "col"), "col")

    def rows_for(target):
        return jnp.concatenate([unit_rows(target * per + a) for a in range(per)], axis=0)

    def moved(shift, rows):
        pairs = [(c, (c + shift) % groups) for c in range(groups) if c >= pivot_devices]
        return lax.ppermute(rows, "col", pairs)

    far = sorted(range(1, groups), key=lambda shift: abs(2 * shift - groups))
    rows = [rows_for((col + shift) % groups) for shift in far]

    top = lax.all_gather(front[:P_SIZE], "col")
    pivots = jnp.concatenate([top[c] for c in range(pivot_devices)], axis=1) if pivot_devices > 1 else top[0]

    received = {0: rows_for(col)}
    for shift, row in zip(far[:EARLY], rows):
        row, _ = lax.optimization_barrier((row, (pivots, corner)))
        received[shift] = moved(shift, row)

    inverse = inverse_factor(pivots)
    for shift, row in zip(far[EARLY:], rows[EARLY:]):
        row, _ = lax.optimization_barrier((row, inverse))
        received[shift] = moved(shift, row)
    places = (col - source) % groups
    child_mine = product(inverse, front[:P_SIZE], 1, 0)

    early = [received[shift] for shift in far[:EARLY]]
    inverse, early = lax.optimization_barrier((inverse, early))
    received.update(zip(far[:EARLY], early))
    factor = jnp.stack([product(inverse, top[c], 1, 0) for c in range(groups)])

    def factor_columns(u):
        block = lax.dynamic_slice(factor, (source[u], 0, parts[u] * width), (1, P_SIZE, width))
        return jnp.where(keeps[u] > 0, block[0], 0.0)

    mine = jnp.concatenate([factor_columns(col * per + a) for a in range(per)], axis=1)
    mine_keep = jnp.repeat(lax.dynamic_slice_in_dim(keeps, col * per, per), width)[:, None] > 0
    pieces = jnp.stack([jnp.where(mine_keep, received[shift], 0.0) for shift in range(groups)])
    left = three_part(mine)
    n = pivot_units
    first = spread_update(source[:n], places[:n], parts[:n], keeps[:n], left, factor, pieces, width)
    first = jnp.concatenate([first[u] for u in range(n)], axis=1)
    steps = []
    first = first + jnp.where(branch == 0, parent_front[:PP].T, 0.0)
    first = join(halve(first, "branch", steps), "branch", steps)

    head = jnp.concatenate([factor_columns(u) for u in range(pivot_units)], axis=1)
    head, _ = lax.optimization_barrier((head, received[far[EARLY]]))
    corner = corner - halve(product(head, head, 0, 0), "branch")
    corner, _ = lax.optimization_barrier((corner, received[far[-1]]))
    corner = join(corner, "branch")

    owned = units_total // branches
    spread = [None] * branches
    for i, m in enumerate(reversed(range(branches))):
        table, _ = lax.optimization_barrier((source, steps[min(i, len(steps) - 1)]))
        at = lambda table: lax.dynamic_slice_in_dim(table, (branch ^ m) * owned, owned)
        spread[m] = spread_update(at(table), at(places), at(parts), at(keeps), left, factor, pieces, width)
    terms, sent = scatter_sum(spread, "branch")
    corner, _ = lax.optimization_barrier((corner, sent))
    parent_inverse = inverse_factor(corner)

    parent_mine = product(parent_inverse, first, 1, 1)
    if groups // ny == branches:
        line, parent_inverse = lax.optimization_barrier((share_line(first, ny), parent_inverse))
        sides = jnp.concatenate(share_beside(line, ny), axis=0)
    else:
        sides = lax.dynamic_slice_in_dim(
            lax.all_gather(first, "col"), branch * groups // branches, groups // branches, 0).reshape(nrows, PP)
    result = finish(parent_front, terms, sides, parent_inverse, parent_mine)
    return (child_mine[None], parent_mine, result)


def solution(mesh):
    in_specs = (P("branch", None, "col"), P("branch", None), P("branch", "col"))
    out_specs = (P("branch", None, "col"), P(None, "col"), P("branch", "col"))
    return jax.shard_map(
        on_device, mesh=mesh, in_specs=in_specs, out_specs=out_specs, check_vma=False
    )
```

```python
import jax
import jax.numpy as jnp
from jax import lax
from jax.experimental import pallas as pl
from jax.experimental.pallas import tpu as pltpu
from jax.sharding import PartitionSpec as P

BS = 256
P_SIZE = 512
NP = 4096
PP = 512
EARLY = 3

SUB = 8
LANES = 128
F32 = jnp.float32


def mm(a, b, ca, cb):
    return lax.dot_general(
        a, b, (((ca,), (cb,)), ((), ())),
        precision=lax.Precision.HIGHEST, preferred_element_type=F32,
    )


def factor_tile(rows):
    sub = lax.broadcasted_iota(jnp.int32, (SUB, LANES), 0)
    lane = lax.broadcasted_iota(jnp.int32, (SUB, LANES), 1)
    rows = list(rows)
    count = len(rows)
    spread = lambda column: jnp.broadcast_to(column, (SUB, LANES))
    for g in range(count):
        base = g * SUB
        inside = (lane >= base) & (lane < base + SUB)
        cols = [spread(rows[g][:, base + j:base + j + 1]) for j in range(SUB)]
        panel = jnp.where(inside, jnp.where(lane - base == sub, 1.0, 0.0), rows[g])
        kept = panel
        pivots = cols[0]
        for j in range(SUB):
            here = sub == j
            pivot = spread(cols[j][j:j + 1, :])
            inverse = 1.0 / pivot
            scaled = cols[j] * inverse
            row = spread(panel[j:j + 1, :])
            kept = jnp.where(here, panel, kept)
            pivots = jnp.where(here, pivot, pivots)
            panel = jnp.where(here, row * inverse, panel - scaled * row)
            for m in range(j + 1, SUB):
                across = spread(cols[m][j:j + 1, :])
                cols[m] = jnp.where(here, across * inverse, cols[m] - scaled * across)
        rows[g] = kept * lax.rsqrt(pivots)
        panel_rows = [spread(panel[j:j + 1, :]) for j in range(SUB)]
        for i in range(g + 1, count):
            terms = [spread(rows[i][:, base + j:base + j + 1]) * panel_rows[j] for j in range(SUB)]
            while len(terms) > 1:
                terms = [terms[t] + terms[t + 1] for t in range(0, len(terms), 2)]
            rows[i] = jnp.where(inside, 0.0, rows[i]) - terms[0]
    return rows


def inverse_factor_kernel(a_ref, w_ref):
    n = a_ref.shape[0]
    steps = n // LANES
    tri = (lax.broadcasted_iota(jnp.int32, (LANES, LANES), 0)
           >= lax.broadcasted_iota(jnp.int32, (LANES, LANES), 1))
    work = [[a_ref[i * LANES:(i + 1) * LANES, j * LANES:(j + 1) * LANES]
             for j in range(steps)] for i in range(steps)]
    for k in range(steps):
        tile = work[k][k]
        done = factor_tile([tile[g * SUB:(g + 1) * SUB, :] for g in range(LANES // SUB)])
        inv = jnp.where(tri, jnp.concatenate(done, axis=0), 0.0)
        work[k] = [inv if j == k else mm(inv, work[k][j], 1, 0) for j in range(steps)]
        for i in range(k + 1, steps):
            left = work[k][i]
            for j in range(steps):
                product = mm(left, work[k][j], 0, 0)
                work[i][j] = -product if j == k else work[i][j] - product
    for i in range(steps):
        for j in range(steps):
            value = work[i][j] if j <= i else jnp.zeros((LANES, LANES), F32)
            w_ref[i * LANES:(i + 1) * LANES, j * LANES:(j + 1) * LANES] = value


def inverse_factor(a):
    n = a.shape[0]
    return pl.pallas_call(
        inverse_factor_kernel,
        out_shape=jax.ShapeDtypeStruct((n, n), F32),
        in_specs=[pl.BlockSpec(memory_space=pltpu.VMEM)],
        out_specs=pl.BlockSpec(memory_space=pltpu.VMEM),
        compiler_params=pltpu.CompilerParams(vmem_limit_bytes=32 * 1024 * 1024),
        cost_estimate=pl.CostEstimate(flops=n * n * n, bytes_accessed=8 * n * n, transcendentals=0),
    )(a)


def spread_kernel(slot_ref, place_ref, part_ref, keep_ref, left_ref, factor_ref, piece_ref, out_ref):
    t = pl.program_id(0)
    whole = factor_ref[0]
    high = whole.astype(jnp.bfloat16)
    low = (whole - high.astype(F32)).astype(jnp.bfloat16)
    right = jnp.concatenate([high, low, high], axis=0)
    value = lax.dot_general(left_ref[...], right, (((1,), (0,)), ((), ())), preferred_element_type=F32)
    out_ref[0] = jnp.where(keep_ref[t] > 0, piece_ref[0] - value, 0.0)


def three_part(x):
    turned = x.T
    rounded = lax.reduce_precision(turned, 8, 7)
    high = rounded.astype(jnp.bfloat16)
    low = (turned - rounded).astype(jnp.bfloat16)
    return jnp.concatenate([high, high, low], axis=1)


def spread_update(slots, places, parts, keeps, left, factor, pieces, width):
    count = slots.shape[0]
    q, depth = left.shape[0], left.shape[1] // 3
    return pl.pallas_call(
        spread_kernel,
        grid_spec=pltpu.PrefetchScalarGridSpec(
            num_scalar_prefetch=4,
            grid=(count,),
            in_specs=[
                pl.BlockSpec((q, 3 * depth), lambda t, *refs: (0, 0)),
                pl.BlockSpec((1, depth, width), lambda t, s, p, h, k: (s[t], 0, h[t])),
                pl.BlockSpec((1, q, width), lambda t, s, p, h, k: (p[t], 0, h[t])),
            ],
            out_specs=pl.BlockSpec((1, q, width), lambda t, *refs: (t, 0, 0)),
        ),
        out_shape=jax.ShapeDtypeStruct((count, q, width), F32),
        compiler_params=pltpu.CompilerParams(vmem_limit_bytes=56 * 1024 * 1024),
        cost_estimate=pl.CostEstimate(
            flops=6 * count * q * depth * width,
            bytes_accessed=4 * count * width * (2 * q + depth), transcendentals=0),
    )(slots, places, parts, keeps, left, factor, pieces)


def product(a, b, ca, cb, precision=lax.Precision.HIGH):
    return lax.dot_general(a, b, (((ca,), (cb,)), ((), ())), precision=precision)


def flip(x, axis, bit):
    n = lax.axis_size(axis)
    return lax.ppermute(x, axis, [(i, i ^ bit) for i in range(n)])


def axis_bits(axis):
    return [1 << i for i in range(lax.axis_size(axis).bit_length() - 1)]


def halve(x, axis, steps=None, gates=()):
    me = lax.axis_index(axis)
    for step, bit in enumerate(axis_bits(axis)):
        if step < len(gates):
            x, _ = lax.optimization_barrier((x, gates[step]))
        high = (me // bit) % 2
        half = x.shape[0] // 2
        away = lax.dynamic_slice_in_dim(x, (1 - high) * half, half, 0)
        x = lax.dynamic_slice_in_dim(x, high * half, half, 0) + flip(away, axis, bit)
        if steps is not None:
            steps.append(x)
    return x


def join(x, axis, steps=None):
    me = lax.axis_index(axis)
    for bit in reversed(axis_bits(axis)):
        high = (me // bit) % 2
        other = flip(x, axis, bit)
        x = jnp.concatenate([jnp.where(high == 0, x, other), jnp.where(high == 0, other, x)], axis=0)
        if steps is not None:
            steps.append(x)
    return x


def scatter_sum(parts, axis):
    parts = list(parts)
    terms = [parts[0]]
    for bit in axis_bits(axis):
        for m in reversed(range(len(parts))):
            if m & bit and not m & (bit - 1):
                sent = parts[m]
                other = flip(sent, axis, bit)
                if m == bit:
                    terms.append(other)
                else:
                    parts[m ^ bit] = parts[m ^ bit] + other
    return terms, sent


def three_rows(x):
    high = x.astype(jnp.bfloat16)
    return high, (x - high.astype(F32)).astype(jnp.bfloat16)


def finish_kernel(parent_ref, side_ref, inverse_ref, mine_ref, *rest):
    terms, out_ref = rest[:-1], rest[-1]
    total = terms[0][0]
    for term in terms[1:]:
        total = total + term[0]
    dot = lambda a, b, cb: lax.dot_general(a, b, (((1,), (cb,)), ((), ())), preferred_element_type=F32)
    high, low = three_rows(side_ref[0])
    ihigh, ilow = three_rows(inverse_ref[...])
    factor = dot(jnp.concatenate([high, high, low], axis=1), jnp.concatenate([ihigh, ilow, ihigh], axis=1), 1)
    high, low = three_rows(factor)
    mhigh, mlow = three_rows(mine_ref[...])
    outer = dot(jnp.concatenate([high, high, low], axis=1), jnp.concatenate([mhigh, mlow, mhigh], axis=0), 0)
    out_ref[...] = parent_ref[...] + total.T - outer


def finish(parent, terms, sides, inverse, mine):
    count, q, width = terms[0].shape
    depth = inverse.shape[0]
    sides = sides.reshape(count, width, depth)
    whole = lambda t: (0, 0)
    block = lambda t: (t, 0, 0)
    return pl.pallas_call(
        finish_kernel,
        grid=(count,),
        in_specs=[
            pl.BlockSpec((width, q), lambda t: (t, 0)),
            pl.BlockSpec((1, width, depth), block),
            pl.BlockSpec((depth, depth), whole),
            pl.BlockSpec((depth, q), whole),
        ] + [pl.BlockSpec((1, q, width), block)] * len(terms),
        out_specs=pl.BlockSpec((width, q), lambda t: (t, 0)),
        out_shape=jax.ShapeDtypeStruct(parent.shape, F32),
        compiler_params=pltpu.CompilerParams(vmem_limit_bytes=48 * 1024 * 1024),
        cost_estimate=pl.CostEstimate(
            flops=6 * count * width * depth * (q + depth), bytes_accessed=8 * parent.size * 4, transcendentals=0),
    )(parent, sides, inverse, mine, *terms)


def line_gather(x, axis, ny, gates):
    n = lax.axis_size(axis)
    nz = n // ny
    up, down = [x], [x]
    for step in range(1, nz):
        ends = (up[-1], down[-1])
        if 1 < step < len(gates) + 2:
            ends, _ = lax.optimization_barrier((ends, gates[step - 2]))
        up.append(lax.ppermute(ends[0], axis, [(c, c + ny) for c in range(n) if step - 1 <= c // ny < nz - 1]))
        down.append(lax.ppermute(ends[1], axis, [(c, c - ny) for c in range(n) if 0 < c // ny <= nz - step]))
    return [x] + [up[k] + down[nz - k] for k in range(1, nz)], list(zip(up, down))


def from_beside(x, axis, ny, j):
    n = lax.axis_size(axis)
    return lax.ppermute(x, axis, [(c, c // ny * ny + (c % ny - j) % ny) for c in range(n)])


def share_line(x, ny):
    branches = lax.axis_size("branch")
    groups = lax.axis_size("col")
    nz = groups // ny
    place = lambda b, z, y: b * groups + z * ny + y
    got = jnp.where(lax.axis_index("col") // ny == lax.axis_index("branch"), x, 0.0)
    for off in range(1, nz):
        pairs = [(place(b, b, y), place(b, (b + off) % nz, y)) for b in range(branches) for y in range(ny)]
        got = got + lax.ppermute(x, ("branch", "col"), pairs)
    return got


def share_beside(got, ny):
    groups = lax.axis_size("col")
    y = lax.axis_index("col") % ny
    shares = [got]
    for j in range(1, ny):
        pairs = [(c, c // ny * ny + (c % ny - j) % ny) for c in range(groups)]
        shares.append(lax.ppermute(got, "col", pairs))
    return [sum(jnp.where(y == (i - j) % ny, shares[j], 0.0) for j in range(ny)) for i in range(ny)]


def on_device(child_fronts, extend_map, parent_front):
    front = child_fronts[0]
    order, ncols = front.shape
    nrows, pcols = parent_front.shape
    groups = lax.axis_size("col")
    branches = lax.axis_size("branch")
    ny = 1
    while 4 * ny * ny <= groups:
        ny *= 2
    nz = groups // ny
    width = min(BS, ncols)
    per = ncols // width
    ratio = BS // width
    units_total = NP // width
    col = lax.axis_index("col")
    branch = lax.axis_index("branch")
    pivot_devices = P_SIZE // ncols

    blocks = extend_map[0]
    hit = blocks[:, None] == jnp.arange(NP // BS, dtype=jnp.int32)[None, :]
    present = jnp.any(hit, axis=0).astype(jnp.int32)
    child_block = jnp.sum(
        jnp.where(hit, jnp.arange(blocks.shape[0], dtype=jnp.int32)[:, None], 0), axis=0
    ).astype(jnp.int32)
    t = jnp.arange(units_total, dtype=jnp.int32)
    units = P_SIZE // width + child_block[t // ratio] * ratio + t % ratio
    keeps = present[t // ratio]
    source = units // per
    parts = units % per

    def unit_rows(u):
        return lax.dynamic_slice_in_dim(front, units[u] * width, width, 0)

    def placed(x):
        if pivot_devices == 1:
            return jnp.where(col == 0, x, 0.0)
        wide = jnp.zeros((x.shape[0], P_SIZE), F32)
        wide = lax.dynamic_update_slice_in_dim(wide, x, jnp.minimum(col, pivot_devices - 1) * ncols, 1)
        return jnp.where(col < pivot_devices, wide, 0.0)

    pivot_units = PP // width

    def pivot_column(b):
        local = units[b] - col * per
        ok = (local >= 0) & (local < per) & (keeps[b] > 0)
        column = lax.dynamic_slice_in_dim(front, jnp.clip(local, 0, per - 1) * width, width, 1)
        body = [
            jnp.where(ok & (keeps[a] > 0), lax.dynamic_slice_in_dim(column, units[a] * width, width, 0), 0.0)
            for a in range(pivot_units)
        ]
        return jnp.concatenate(body, axis=0)

    corner = jnp.concatenate([pivot_column(b) for b in range(pivot_units)], axis=1)
    corner = corner + jnp.where(branch == 0, placed(parent_front[:PP]), 0.0)
    corner = halve(corner, "branch")

    def rows_for(target):
        return jnp.concatenate([unit_rows(target * per + a) for a in range(per)], axis=0)

    def moved(k, rows):
        pairs = [(c, c ^ k) for c in range(groups) if c >= pivot_devices]
        return lax.ppermute(rows, "col", pairs)

    near, far = list(range(1, ny)), list(reversed(range(ny, groups)))
    rows = {k: rows_for(col ^ k) for k in range(groups)}
    received = {0: rows[0]}
    for k in near:
        received[k] = moved(k, rows[k])

    z, y = col // ny, col % ny
    head = front[:P_SIZE]
    beside = [from_beside(head, "col", ny, j) for j in near]
    line, steps = line_gather(head, "col", ny, [(corner, [rows[k] for k in far])])
    corner = halve(corner, "col", gates=[head[:8]] + steps[2:])
    corner = join(corner, "col")

    def in_line(c, parts):
        return sum(jnp.where(z == (c // ny + k) % len(line), parts[k], 0.0) for k in range(len(line)))

    pivot_line = in_line(0, line)
    pivot_parts = [pivot_line] + [from_beside(pivot_line, "col", ny, j) for j in near]
    pivots = [
        sum(jnp.where(y == (c - j) % ny, pivot_parts[j], 0.0) for j in range(ny)) for c in range(pivot_devices)]
    pivots = jnp.concatenate(pivots, axis=1) if pivot_devices > 1 else pivots[0]

    for k in far[:EARLY]:
        row, _ = lax.optimization_barrier((rows[k], (steps[-1], corner)))
        received[k] = moved(k, row)
    others = lax.optimization_barrier((jnp.stack(line[1:]), corner))[0]
    others = [from_beside(others, "col", ny, j) for j in near]
    gathered = line + [x for j in range(ny - 1) for x in [beside[j]] + [others[j][k] for k in range(len(line) - 1)]]
    slots = (source % ny - y) % ny * len(line) + (z - source // ny) % len(line)

    inverse = inverse_factor(pivots)
    for k in far[EARLY:]:
        row, _ = lax.optimization_barrier((rows[k], inverse))
        received[k] = moved(k, row)
    places = col ^ source
    child_mine = product(inverse, front[:P_SIZE], 1, 0)

    early = [received[k] for k in far[:EARLY]]
    inverse, early = lax.optimization_barrier((inverse, early))
    received.update(zip(far[:EARLY], early))
    factor = jnp.stack([product(inverse, x, 1, 0) for x in gathered])

    def factor_columns(u):
        block = lax.dynamic_slice(factor, (slots[u], 0, parts[u] * width), (1, P_SIZE, width))
        return jnp.where(keeps[u] > 0, block[0], 0.0)

    mine = jnp.concatenate([factor_columns(col * per + a) for a in range(per)], axis=1)
    mine_keep = jnp.repeat(lax.dynamic_slice_in_dim(keeps, col * per, per), width)[:, None] > 0
    pieces = jnp.stack([jnp.where(mine_keep, received[k], 0.0) for k in range(groups)])
    left = three_part(mine)
    n = pivot_units
    first = spread_update(slots[:n], places[:n], parts[:n], keeps[:n], left, factor, pieces, width)
    first = jnp.concatenate([first[u] for u in range(n)], axis=1)
    steps = []
    first = first + jnp.where(branch == 0, parent_front[:PP].T, 0.0)
    first = join(halve(first, "branch", steps), "branch", steps)

    head = jnp.concatenate([factor_columns(u) for u in range(pivot_units)], axis=1)
    head, _ = lax.optimization_barrier((head, received[far[-2]]))
    corner = corner - halve(product(head, head, 0, 0), "branch")
    corner, _ = lax.optimization_barrier((corner, received[far[-1]]))
    corner = join(corner, "branch")

    owned = units_total // branches
    spread = [None] * branches
    for i, m in enumerate(reversed(range(branches))):
        table, _ = lax.optimization_barrier((slots, steps[min(i, len(steps) - 1)]))
        at = lambda table: lax.dynamic_slice_in_dim(table, (branch ^ m) * owned, owned)
        spread[m] = spread_update(at(table), at(places), at(parts), at(keeps), left, factor, pieces, width)
    terms, sent = scatter_sum(spread, "branch")
    corner, _ = lax.optimization_barrier((corner, sent))
    parent_inverse = inverse_factor(corner)

    parent_mine = product(parent_inverse, first, 1, 1)
    if groups // ny == branches:
        line, parent_inverse = lax.optimization_barrier((share_line(first, ny), parent_inverse))
        sides = jnp.concatenate(share_beside(line, ny), axis=0)
    else:
        sides = lax.dynamic_slice_in_dim(
            lax.all_gather(first, "col"), branch * groups // branches, groups // branches, 0).reshape(nrows, PP)
    result = finish(parent_front, terms, sides, parent_inverse, parent_mine)
    return (child_mine[None], parent_mine, result)


def solution(mesh):
    in_specs = (P("branch", None, "col"), P("branch", None), P("branch", "col"))
    out_specs = (P("branch", None, "col"), P(None, "col"), P("branch", "col"))
    return jax.shard_map(
        on_device, mesh=mesh, in_specs=in_specs, out_specs=out_specs, check_vma=False
    )
```

```python
import jax
import jax.numpy as jnp
from jax import lax
from jax.experimental import pallas as pl
from jax.experimental.pallas import tpu as pltpu
from jax.sharding import PartitionSpec as P

BS = 256
P_SIZE = 512
NP = 4096
PP = 512
EARLY = 3

SUB = 8
LANES = 128
F32 = jnp.float32


def mm(a, b, ca, cb):
    return lax.dot_general(
        a, b, (((ca,), (cb,)), ((), ())),
        precision=lax.Precision.HIGHEST, preferred_element_type=F32,
    )


def factor_tile(rows):
    sub = lax.broadcasted_iota(jnp.int32, (SUB, LANES), 0)
    lane = lax.broadcasted_iota(jnp.int32, (SUB, LANES), 1)
    rows = list(rows)
    count = len(rows)
    spread = lambda column: jnp.broadcast_to(column, (SUB, LANES))
    for g in range(count):
        base = g * SUB
        inside = (lane >= base) & (lane < base + SUB)
        cols = [spread(rows[g][:, base + j:base + j + 1]) for j in range(SUB)]
        panel = jnp.where(inside, jnp.where(lane - base == sub, 1.0, 0.0), rows[g])
        kept = panel
        pivots = cols[0]
        for j in range(SUB):
            here = sub == j
            pivot = spread(cols[j][j:j + 1, :])
            inverse = 1.0 / pivot
            scaled = cols[j] * inverse
            row = spread(panel[j:j + 1, :])
            kept = jnp.where(here, panel, kept)
            pivots = jnp.where(here, pivot, pivots)
            panel = jnp.where(here, row * inverse, panel - scaled * row)
            for m in range(j + 1, SUB):
                across = spread(cols[m][j:j + 1, :])
                cols[m] = jnp.where(here, across * inverse, cols[m] - scaled * across)
        rows[g] = kept * lax.rsqrt(pivots)
        panel_rows = [spread(panel[j:j + 1, :]) for j in range(SUB)]
        for i in range(g + 1, count):
            terms = [spread(rows[i][:, base + j:base + j + 1]) * panel_rows[j] for j in range(SUB)]
            while len(terms) > 1:
                terms = [terms[t] + terms[t + 1] for t in range(0, len(terms), 2)]
            rows[i] = jnp.where(inside, 0.0, rows[i]) - terms[0]
    return rows


def inverse_factor_kernel(a_ref, w_ref):
    n = a_ref.shape[0]
    steps = n // LANES
    tri = (lax.broadcasted_iota(jnp.int32, (LANES, LANES), 0)
           >= lax.broadcasted_iota(jnp.int32, (LANES, LANES), 1))
    work = [[a_ref[i * LANES:(i + 1) * LANES, j * LANES:(j + 1) * LANES]
             for j in range(steps)] for i in range(steps)]
    for k in range(steps):
        tile = work[k][k]
        done = factor_tile([tile[g * SUB:(g + 1) * SUB, :] for g in range(LANES // SUB)])
        inv = jnp.where(tri, jnp.concatenate(done, axis=0), 0.0)
        work[k] = [inv if j == k else mm(inv, work[k][j], 1, 0) for j in range(steps)]
        for i in range(k + 1, steps):
            left = work[k][i]
            for j in range(steps):
                product = mm(left, work[k][j], 0, 0)
                work[i][j] = -product if j == k else work[i][j] - product
    for i in range(steps):
        for j in range(steps):
            value = work[i][j] if j <= i else jnp.zeros((LANES, LANES), F32)
            w_ref[i * LANES:(i + 1) * LANES, j * LANES:(j + 1) * LANES] = value


def inverse_factor(a):
    n = a.shape[0]
    return pl.pallas_call(
        inverse_factor_kernel,
        out_shape=jax.ShapeDtypeStruct((n, n), F32),
        in_specs=[pl.BlockSpec(memory_space=pltpu.VMEM)],
        out_specs=pl.BlockSpec(memory_space=pltpu.VMEM),
        compiler_params=pltpu.CompilerParams(vmem_limit_bytes=32 * 1024 * 1024),
        cost_estimate=pl.CostEstimate(flops=n * n * n, bytes_accessed=8 * n * n, transcendentals=0),
    )(a)


def spread_kernel(slot_ref, place_ref, part_ref, keep_ref, left_ref, factor_ref, piece_ref, out_ref):
    t = pl.program_id(0)
    whole = factor_ref[0]
    high = whole.astype(jnp.bfloat16)
    low = (whole - high.astype(F32)).astype(jnp.bfloat16)
    right = jnp.concatenate([high, low, high], axis=0)
    value = lax.dot_general(left_ref[...], right, (((1,), (0,)), ((), ())), preferred_element_type=F32)
    out_ref[0] = jnp.where(keep_ref[t] > 0, piece_ref[0] - value, 0.0)


def three_part(x):
    turned = x.T
    rounded = lax.reduce_precision(turned, 8, 7)
    high = rounded.astype(jnp.bfloat16)
    low = (turned - rounded).astype(jnp.bfloat16)
    return jnp.concatenate([high, high, low], axis=1)


def spread_update(slots, places, parts, keeps, left, factor, pieces, width):
    count = slots.shape[0]
    q, depth = left.shape[0], left.shape[1] // 3
    return pl.pallas_call(
        spread_kernel,
        grid_spec=pltpu.PrefetchScalarGridSpec(
            num_scalar_prefetch=4,
            grid=(count,),
            in_specs=[
                pl.BlockSpec((q, 3 * depth), lambda t, *refs: (0, 0)),
                pl.BlockSpec((1, depth, width), lambda t, s, p, h, k: (s[t], 0, h[t])),
                pl.BlockSpec((1, q, width), lambda t, s, p, h, k: (p[t], 0, h[t])),
            ],
            out_specs=pl.BlockSpec((1, q, width), lambda t, *refs: (t, 0, 0)),
        ),
        out_shape=jax.ShapeDtypeStruct((count, q, width), F32),
        compiler_params=pltpu.CompilerParams(vmem_limit_bytes=56 * 1024 * 1024),
        cost_estimate=pl.CostEstimate(
            flops=6 * count * q * depth * width,
            bytes_accessed=4 * count * width * (2 * q + depth), transcendentals=0),
    )(slots, places, parts, keeps, left, factor, pieces)


def product(a, b, ca, cb, precision=lax.Precision.HIGH):
    return lax.dot_general(a, b, (((ca,), (cb,)), ((), ())), precision=precision)


def flip(x, axis, bit):
    n = lax.axis_size(axis)
    return lax.ppermute(x, axis, [(i, i ^ bit) for i in range(n)])


def axis_bits(axis):
    return [1 << i for i in range(lax.axis_size(axis).bit_length() - 1)]


def halve(x, axis, steps=None, gates=()):
    me = lax.axis_index(axis)
    for step, bit in enumerate(axis_bits(axis)):
        if step < len(gates):
            x, _ = lax.optimization_barrier((x, gates[step]))
        high = (me // bit) % 2
        half = x.shape[0] // 2
        away = lax.dynamic_slice_in_dim(x, (1 - high) * half, half, 0)
        x = lax.dynamic_slice_in_dim(x, high * half, half, 0) + flip(away, axis, bit)
        if steps is not None:
            steps.append(x)
    return x


def join(x, axis, steps=None):
    me = lax.axis_index(axis)
    for bit in reversed(axis_bits(axis)):
        high = (me // bit) % 2
        other = flip(x, axis, bit)
        x = jnp.concatenate([jnp.where(high == 0, x, other), jnp.where(high == 0, other, x)], axis=0)
        if steps is not None:
            steps.append(x)
    return x


def scatter_sum(parts, axis):
    parts = list(parts)
    terms = [parts[0]]
    for bit in axis_bits(axis):
        for m in reversed(range(len(parts))):
            if m & bit and not m & (bit - 1):
                sent = parts[m]
                other = flip(sent, axis, bit)
                if m == bit:
                    terms.append(other)
                else:
                    parts[m ^ bit] = parts[m ^ bit] + other
    return terms, sent


def three_rows(x):
    high = x.astype(jnp.bfloat16)
    return high, (x - high.astype(F32)).astype(jnp.bfloat16)


def finish_kernel(parent_ref, side_ref, inverse_ref, mine_ref, *rest):
    terms, out_ref = rest[:-1], rest[-1]
    total = terms[0][0]
    for term in terms[1:]:
        total = total + term[0]
    dot = lambda a, b, cb: lax.dot_general(a, b, (((1,), (cb,)), ((), ())), preferred_element_type=F32)
    high, low = three_rows(side_ref[0])
    ihigh, ilow = three_rows(inverse_ref[...])
    factor = dot(jnp.concatenate([high, high, low], axis=1), jnp.concatenate([ihigh, ilow, ihigh], axis=1), 1)
    high, low = three_rows(factor)
    mhigh, mlow = three_rows(mine_ref[...])
    outer = dot(jnp.concatenate([high, high, low], axis=1), jnp.concatenate([mhigh, mlow, mhigh], axis=0), 0)
    out_ref[...] = parent_ref[...] + total.T - outer


def finish(parent, terms, sides, inverse, mine):
    count, q, width = terms[0].shape
    depth = inverse.shape[0]
    sides = sides.reshape(count, width, depth)
    whole = lambda t: (0, 0)
    block = lambda t: (t, 0, 0)
    return pl.pallas_call(
        finish_kernel,
        grid=(count,),
        in_specs=[
            pl.BlockSpec((width, q), lambda t: (t, 0)),
            pl.BlockSpec((1, width, depth), block),
            pl.BlockSpec((depth, depth), whole),
            pl.BlockSpec((depth, q), whole),
        ] + [pl.BlockSpec((1, q, width), block)] * len(terms),
        out_specs=pl.BlockSpec((width, q), lambda t: (t, 0)),
        out_shape=jax.ShapeDtypeStruct(parent.shape, F32),
        compiler_params=pltpu.CompilerParams(vmem_limit_bytes=48 * 1024 * 1024),
        cost_estimate=pl.CostEstimate(
            flops=6 * count * width * depth * (q + depth), bytes_accessed=8 * parent.size * 4, transcendentals=0),
    )(parent, sides, inverse, mine, *terms)


def line_gather(x, axis, ny, gates):
    n = lax.axis_size(axis)
    nz = n // ny
    up, down = [x], [x]
    for step in range(1, nz):
        ends = (up[-1], down[-1])
        if 1 < step < len(gates) + 2:
            ends, _ = lax.optimization_barrier((ends, gates[step - 2]))
        up.append(lax.ppermute(ends[0], axis, [(c, c + ny) for c in range(n) if step - 1 <= c // ny < nz - 1]))
        down.append(lax.ppermute(ends[1], axis, [(c, c - ny) for c in range(n) if 0 < c // ny <= nz - step]))
    return [x] + [up[k] + down[nz - k] for k in range(1, nz)], list(zip(up, down))


def from_beside(x, axis, ny, j):
    n = lax.axis_size(axis)
    return lax.ppermute(x, axis, [(c, c // ny * ny + (c % ny - j) % ny) for c in range(n)])


def share_line(x, ny):
    branches = lax.axis_size("branch")
    groups = lax.axis_size("col")
    nz = groups // ny
    place = lambda b, z, y: b * groups + z * ny + y
    got = jnp.where(lax.axis_index("col") // ny == lax.axis_index("branch"), x, 0.0)
    for off in range(1, nz):
        pairs = [(place(b, b, y), place(b, (b + off) % nz, y)) for b in range(branches) for y in range(ny)]
        got = got + lax.ppermute(x, ("branch", "col"), pairs)
    return got


def share_beside(got, ny):
    groups = lax.axis_size("col")
    y = lax.axis_index("col") % ny
    shares = [got]
    for j in range(1, ny):
        pairs = [(c, c // ny * ny + (c % ny - j) % ny) for c in range(groups)]
        shares.append(lax.ppermute(got, "col", pairs))
    return [sum(jnp.where(y == (i - j) % ny, shares[j], 0.0) for j in range(ny)) for i in range(ny)]


def on_device(child_fronts, extend_map, parent_front):
    front = child_fronts[0]
    order, ncols = front.shape
    nrows, pcols = parent_front.shape
    groups = lax.axis_size("col")
    branches = lax.axis_size("branch")
    ny = 1
    while 4 * ny * ny <= groups:
        ny *= 2
    nz = groups // ny
    width = min(BS, ncols)
    per = ncols // width
    ratio = BS // width
    units_total = NP // width
    col = lax.axis_index("col")
    branch = lax.axis_index("branch")
    pivot_devices = P_SIZE // ncols

    blocks = extend_map[0]
    hit = blocks[:, None] == jnp.arange(NP // BS, dtype=jnp.int32)[None, :]
    present = jnp.any(hit, axis=0).astype(jnp.int32)
    child_block = jnp.sum(
        jnp.where(hit, jnp.arange(blocks.shape[0], dtype=jnp.int32)[:, None], 0), axis=0
    ).astype(jnp.int32)
    t = jnp.arange(units_total, dtype=jnp.int32)
    units = P_SIZE // width + child_block[t // ratio] * ratio + t % ratio
    keeps = present[t // ratio]
    source = units // per
    parts = units % per

    def unit_rows(u):
        return lax.dynamic_slice_in_dim(front, units[u] * width, width, 0)

    def placed(x):
        if pivot_devices == 1:
            return jnp.where(col == 0, x, 0.0)
        wide = jnp.zeros((x.shape[0], P_SIZE), F32)
        wide = lax.dynamic_update_slice_in_dim(wide, x, jnp.minimum(col, pivot_devices - 1) * ncols, 1)
        return jnp.where(col < pivot_devices, wide, 0.0)

    pivot_units = PP // width

    def pivot_column(b):
        local = units[b] - col * per
        ok = (local >= 0) & (local < per) & (keeps[b] > 0)
        column = lax.dynamic_slice_in_dim(front, jnp.clip(local, 0, per - 1) * width, width, 1)
        body = [
            jnp.where(ok & (keeps[a] > 0), lax.dynamic_slice_in_dim(column, units[a] * width, width, 0), 0.0)
            for a in range(pivot_units)
        ]
        return jnp.concatenate(body, axis=0)

    corner = jnp.concatenate([pivot_column(b) for b in range(pivot_units)], axis=1)
    corner = corner + jnp.where(branch == 0, placed(parent_front[:PP]), 0.0)
    corner = halve(corner, "branch")

    def rows_for(target):
        return jnp.concatenate([unit_rows(target * per + a) for a in range(per)], axis=0)

    def moved(k, rows):
        pairs = [(c, c ^ k) for c in range(groups) if c >= pivot_devices]
        return lax.ppermute(rows, "col", pairs)

    near, far = list(range(1, ny)), list(reversed(range(ny, groups)))
    rows = {k: rows_for(col ^ k) for k in range(groups)}
    received = {0: rows[0]}
    for k in near:
        received[k] = moved(k, rows[k])

    z, y = col // ny, col % ny
    head = front[:P_SIZE]
    beside = [from_beside(head, "col", ny, j) for j in near]
    line, steps = line_gather(head, "col", ny, [(corner, [rows[k] for k in far])])
    halved = halve(corner, "col", gates=[head[:8]] + steps[2:])
    corner = join(halved, "col")

    def in_line(c, parts):
        return sum(jnp.where(z == (c // ny + k) % len(line), parts[k], 0.0) for k in range(len(line)))

    pivot_line = in_line(0, line)
    pivot_parts = [pivot_line] + [from_beside(pivot_line, "col", ny, j) for j in near]
    pivots = [
        sum(jnp.where(y == (c - j) % ny, pivot_parts[j], 0.0) for j in range(ny)) for c in range(pivot_devices)]
    pivots = jnp.concatenate(pivots, axis=1) if pivot_devices > 1 else pivots[0]

    for k in far[:EARLY]:
        row, _ = lax.optimization_barrier((rows[k], (steps[-1], halved, beside)))
        received[k] = moved(k, row)
    others = lax.optimization_barrier((jnp.stack(line[1:]), pivots))[0]
    others = [from_beside(others, "col", ny, j) for j in near]
    gathered = line + [x for j in range(ny - 1) for x in [beside[j]] + [others[j][k] for k in range(len(line) - 1)]]
    slots = (source % ny - y) % ny * len(line) + (z - source // ny) % len(line)

    inverse = inverse_factor(pivots)
    for k in far[EARLY:]:
        row, _ = lax.optimization_barrier((rows[k], pivots if k == far[EARLY] else others))
        received[k] = moved(k, row)
    places = col ^ source
    child_mine = product(inverse, front[:P_SIZE], 1, 0)

    early = [received[k] for k in far[:EARLY]]
    inverse, early, corner = lax.optimization_barrier((inverse, early, corner))
    received.update(zip(far[:EARLY], early))
    factor = jnp.stack([product(inverse, x, 1, 0) for x in gathered])

    def factor_columns(u):
        block = lax.dynamic_slice(factor, (slots[u], 0, parts[u] * width), (1, P_SIZE, width))
        return jnp.where(keeps[u] > 0, block[0], 0.0)

    mine = jnp.concatenate([factor_columns(col * per + a) for a in range(per)], axis=1)
    mine_keep = jnp.repeat(lax.dynamic_slice_in_dim(keeps, col * per, per), width)[:, None] > 0
    pieces = jnp.stack([jnp.where(mine_keep, received[k], 0.0) for k in range(groups)])
    left = three_part(mine)
    n = pivot_units
    first = spread_update(slots[:n], places[:n], parts[:n], keeps[:n], left, factor, pieces, width)
    first = jnp.concatenate([first[u] for u in range(n)], axis=1)
    steps = []
    first = first + jnp.where(branch == 0, parent_front[:PP].T, 0.0)
    first = join(halve(first, "branch", steps), "branch", steps)

    head = jnp.concatenate([factor_columns(u) for u in range(pivot_units)], axis=1)
    corner = corner - halve(product(head, head, 0, 0), "branch")
    corner, _ = lax.optimization_barrier((corner, received[far[-2]]))
    corner = join(corner, "branch")

    owned = units_total // branches
    spread = [None] * branches
    for i, m in enumerate(reversed(range(branches))):
        table, _ = lax.optimization_barrier((slots, steps[min(i, len(steps) - 1)]))
        at = lambda table: lax.dynamic_slice_in_dim(table, (branch ^ m) * owned, owned)
        spread[m] = spread_update(at(table), at(places), at(parts), at(keeps), left, factor, pieces, width)
    terms, sent = scatter_sum(spread, "branch")
    corner, _ = lax.optimization_barrier((corner, sent))
    parent_inverse = inverse_factor(corner)

    parent_mine = product(parent_inverse, first, 1, 1)
    if groups // ny == branches:
        line, parent_inverse = lax.optimization_barrier((share_line(first, ny), parent_inverse))
        sides = jnp.concatenate(share_beside(line, ny), axis=0)
    else:
        sides = lax.dynamic_slice_in_dim(
            lax.all_gather(first, "col"), branch * groups // branches, groups // branches, 0).reshape(nrows, PP)
    result = finish(parent_front, terms, sides, parent_inverse, parent_mine)
    return (child_mine[None], parent_mine, result)


def solution(mesh):
    in_specs = (P("branch", None, "col"), P("branch", None), P("branch", "col"))
    out_specs = (P("branch", None, "col"), P(None, "col"), P("branch", "col"))
    return jax.shard_map(
        on_device, mesh=mesh, in_specs=in_specs, out_specs=out_specs, check_vma=False
    )
```

```python
import jax
import jax.numpy as jnp
from jax import lax
from jax.experimental import pallas as pl
from jax.experimental.pallas import tpu as pltpu
from jax.sharding import PartitionSpec as P

BS = 256
P_SIZE = 512
NP = 4096
PP = 512
EARLY = 3

SUB = 8
LANES = 128
F32 = jnp.float32


def mm(a, b, ca, cb):
    return lax.dot_general(
        a, b, (((ca,), (cb,)), ((), ())),
        precision=lax.Precision.HIGHEST, preferred_element_type=F32,
    )


def factor_tile(rows):
    sub = lax.broadcasted_iota(jnp.int32, (SUB, LANES), 0)
    lane = lax.broadcasted_iota(jnp.int32, (SUB, LANES), 1)
    rows = list(rows)
    count = len(rows)
    spread = lambda column: jnp.broadcast_to(column, (SUB, LANES))
    for g in range(count):
        base = g * SUB
        inside = (lane >= base) & (lane < base + SUB)
        cols = [spread(rows[g][:, base + j:base + j + 1]) for j in range(SUB)]
        panel = jnp.where(inside, jnp.where(lane - base == sub, 1.0, 0.0), rows[g])
        kept = panel
        pivots = cols[0]
        for j in range(SUB):
            here = sub == j
            pivot = spread(cols[j][j:j + 1, :])
            inverse = 1.0 / pivot
            scaled = cols[j] * inverse
            row = spread(panel[j:j + 1, :])
            kept = jnp.where(here, panel, kept)
            pivots = jnp.where(here, pivot, pivots)
            panel = jnp.where(here, row * inverse, panel - scaled * row)
            for m in range(j + 1, SUB):
                across = spread(cols[m][j:j + 1, :])
                cols[m] = jnp.where(here, across * inverse, cols[m] - scaled * across)
        rows[g] = kept * lax.rsqrt(pivots)
        panel_rows = [spread(panel[j:j + 1, :]) for j in range(SUB)]
        for i in range(g + 1, count):
            terms = [spread(rows[i][:, base + j:base + j + 1]) * panel_rows[j] for j in range(SUB)]
            while len(terms) > 1:
                terms = [terms[t] + terms[t + 1] for t in range(0, len(terms), 2)]
            rows[i] = jnp.where(inside, 0.0, rows[i]) - terms[0]
    return rows


def inverse_factor_kernel(a_ref, w_ref):
    n = a_ref.shape[0]
    steps = n // LANES
    tri = (lax.broadcasted_iota(jnp.int32, (LANES, LANES), 0)
           >= lax.broadcasted_iota(jnp.int32, (LANES, LANES), 1))
    work = [[a_ref[i * LANES:(i + 1) * LANES, j * LANES:(j + 1) * LANES]
             for j in range(steps)] for i in range(steps)]
    for k in range(steps):
        tile = work[k][k]
        done = factor_tile([tile[g * SUB:(g + 1) * SUB, :] for g in range(LANES // SUB)])
        inv = jnp.where(tri, jnp.concatenate(done, axis=0), 0.0)
        work[k] = [inv if j == k else mm(inv, work[k][j], 1, 0) for j in range(steps)]
        for i in range(k + 1, steps):
            left = work[k][i]
            for j in range(steps):
                product = mm(left, work[k][j], 0, 0)
                work[i][j] = -product if j == k else work[i][j] - product
    for i in range(steps):
        for j in range(steps):
            value = work[i][j] if j <= i else jnp.zeros((LANES, LANES), F32)
            w_ref[i * LANES:(i + 1) * LANES, j * LANES:(j + 1) * LANES] = value


def inverse_factor(a):
    n = a.shape[0]
    return pl.pallas_call(
        inverse_factor_kernel,
        out_shape=jax.ShapeDtypeStruct((n, n), F32),
        in_specs=[pl.BlockSpec(memory_space=pltpu.VMEM)],
        out_specs=pl.BlockSpec(memory_space=pltpu.VMEM),
        compiler_params=pltpu.CompilerParams(vmem_limit_bytes=32 * 1024 * 1024),
        cost_estimate=pl.CostEstimate(flops=n * n * n, bytes_accessed=8 * n * n, transcendentals=0),
    )(a)


def spread_kernel(slot_ref, place_ref, part_ref, keep_ref, left_ref, factor_ref, piece_ref, out_ref):
    t = pl.program_id(0)
    whole = factor_ref[0]
    high = whole.astype(jnp.bfloat16)
    low = (whole - high.astype(F32)).astype(jnp.bfloat16)
    right = jnp.concatenate([high, low, high], axis=0)
    value = lax.dot_general(left_ref[...], right, (((1,), (0,)), ((), ())), preferred_element_type=F32)
    out_ref[0] = jnp.where(keep_ref[t] > 0, piece_ref[0] - value, 0.0)


def three_part(x):
    turned = x.T
    rounded = lax.reduce_precision(turned, 8, 7)
    high = rounded.astype(jnp.bfloat16)
    low = (turned - rounded).astype(jnp.bfloat16)
    return jnp.concatenate([high, high, low], axis=1)


def spread_update(slots, places, parts, keeps, left, factor, pieces, width):
    count = slots.shape[0]
    q, depth = left.shape[0], left.shape[1] // 3
    return pl.pallas_call(
        spread_kernel,
        grid_spec=pltpu.PrefetchScalarGridSpec(
            num_scalar_prefetch=4,
            grid=(count,),
            in_specs=[
                pl.BlockSpec((q, 3 * depth), lambda t, *refs: (0, 0)),
                pl.BlockSpec((1, depth, width), lambda t, s, p, h, k: (s[t], 0, h[t])),
                pl.BlockSpec((1, q, width), lambda t, s, p, h, k: (p[t], 0, h[t])),
            ],
            out_specs=pl.BlockSpec((1, q, width), lambda t, *refs: (t, 0, 0)),
        ),
        out_shape=jax.ShapeDtypeStruct((count, q, width), F32),
        compiler_params=pltpu.CompilerParams(vmem_limit_bytes=56 * 1024 * 1024),
        cost_estimate=pl.CostEstimate(
            flops=6 * count * q * depth * width,
            bytes_accessed=4 * count * width * (2 * q + depth), transcendentals=0),
    )(slots, places, parts, keeps, left, factor, pieces)


def product(a, b, ca, cb, precision=lax.Precision.HIGH):
    return lax.dot_general(a, b, (((ca,), (cb,)), ((), ())), precision=precision)


def flip(x, axis, bit):
    n = lax.axis_size(axis)
    return lax.ppermute(x, axis, [(i, i ^ bit) for i in range(n)])


def axis_bits(axis):
    return [1 << i for i in range(lax.axis_size(axis).bit_length() - 1)]


def halve(x, axis, steps=None, gates=()):
    me = lax.axis_index(axis)
    for step, bit in enumerate(axis_bits(axis)):
        if step < len(gates):
            x, _ = lax.optimization_barrier((x, gates[step]))
        high = (me // bit) % 2
        half = x.shape[0] // 2
        away = lax.dynamic_slice_in_dim(x, (1 - high) * half, half, 0)
        x = lax.dynamic_slice_in_dim(x, high * half, half, 0) + flip(away, axis, bit)
        if steps is not None:
            steps.append(x)
    return x


def join(x, axis, steps=None):
    me = lax.axis_index(axis)
    for bit in reversed(axis_bits(axis)):
        high = (me // bit) % 2
        other = flip(x, axis, bit)
        x = jnp.concatenate([jnp.where(high == 0, x, other), jnp.where(high == 0, other, x)], axis=0)
        if steps is not None:
            steps.append(x)
    return x


def scatter_sum(parts, axis):
    parts = list(parts)
    terms = [parts[0]]
    for bit in axis_bits(axis):
        for m in reversed(range(len(parts))):
            if m & bit and not m & (bit - 1):
                sent = parts[m]
                other = flip(sent, axis, bit)
                if m == bit:
                    terms.append(other)
                else:
                    parts[m ^ bit] = parts[m ^ bit] + other
    return terms, sent


def three_rows(x):
    high = x.astype(jnp.bfloat16)
    return high, (x - high.astype(F32)).astype(jnp.bfloat16)


def finish_kernel(parent_ref, side_ref, inverse_ref, mine_ref, *rest):
    terms, out_ref = rest[:-1], rest[-1]
    total = terms[0][0]
    for term in terms[1:]:
        total = total + term[0]
    dot = lambda a, b, cb: lax.dot_general(a, b, (((1,), (cb,)), ((), ())), preferred_element_type=F32)
    high, low = three_rows(side_ref[0])
    ihigh, ilow = three_rows(inverse_ref[...])
    factor = dot(jnp.concatenate([high, high, low], axis=1), jnp.concatenate([ihigh, ilow, ihigh], axis=1), 1)
    high, low = three_rows(factor)
    mhigh, mlow = three_rows(mine_ref[...])
    outer = dot(jnp.concatenate([high, high, low], axis=1), jnp.concatenate([mhigh, mlow, mhigh], axis=0), 0)
    out_ref[...] = parent_ref[...] + total.T - outer


def finish(parent, terms, sides, inverse, mine):
    count, q, width = terms[0].shape
    depth = inverse.shape[0]
    sides = sides.reshape(count, width, depth)
    whole = lambda t: (0, 0)
    block = lambda t: (t, 0, 0)
    return pl.pallas_call(
        finish_kernel,
        grid=(count,),
        in_specs=[
            pl.BlockSpec((width, q), lambda t: (t, 0)),
            pl.BlockSpec((1, width, depth), block),
            pl.BlockSpec((depth, depth), whole),
            pl.BlockSpec((depth, q), whole),
        ] + [pl.BlockSpec((1, q, width), block)] * len(terms),
        out_specs=pl.BlockSpec((width, q), lambda t: (t, 0)),
        out_shape=jax.ShapeDtypeStruct(parent.shape, F32),
        compiler_params=pltpu.CompilerParams(vmem_limit_bytes=48 * 1024 * 1024),
        cost_estimate=pl.CostEstimate(
            flops=6 * count * width * depth * (q + depth), bytes_accessed=8 * parent.size * 4, transcendentals=0),
    )(parent, sides, inverse, mine, *terms)


def line_gather(x, axis, ny, gates):
    n = lax.axis_size(axis)
    nz = n // ny
    up, down = [x], [x]
    for step in range(1, nz):
        ends = (up[-1], down[-1])
        if 1 < step < len(gates) + 2:
            ends, _ = lax.optimization_barrier((ends, gates[step - 2]))
        up.append(lax.ppermute(ends[0], axis, [(c, c + ny) for c in range(n) if step - 1 <= c // ny < nz - 1]))
        down.append(lax.ppermute(ends[1], axis, [(c, c - ny) for c in range(n) if 0 < c // ny <= nz - step]))
    return [x] + [up[k] + down[nz - k] for k in range(1, nz)], list(zip(up, down))


def from_beside(x, axis, ny, j):
    n = lax.axis_size(axis)
    return lax.ppermute(x, axis, [(c, c // ny * ny + (c % ny - j) % ny) for c in range(n)])


def share_line(x, ny):
    branches = lax.axis_size("branch")
    groups = lax.axis_size("col")
    nz = groups // ny
    place = lambda b, z, y: b * groups + z * ny + y
    got = jnp.where(lax.axis_index("col") // ny == lax.axis_index("branch"), x, 0.0)
    for off in range(1, nz):
        pairs = [(place(b, b, y), place(b, (b + off) % nz, y)) for b in range(branches) for y in range(ny)]
        got = got + lax.ppermute(x, ("branch", "col"), pairs)
    return got


def share_beside(got, ny):
    groups = lax.axis_size("col")
    y = lax.axis_index("col") % ny
    shares = [got]
    for j in range(1, ny):
        pairs = [(c, c // ny * ny + (c % ny - j) % ny) for c in range(groups)]
        shares.append(lax.ppermute(got, "col", pairs))
    return [sum(jnp.where(y == (i - j) % ny, shares[j], 0.0) for j in range(ny)) for i in range(ny)]


def on_device(child_fronts, extend_map, parent_front):
    front = child_fronts[0]
    order, ncols = front.shape
    nrows, pcols = parent_front.shape
    groups = lax.axis_size("col")
    branches = lax.axis_size("branch")
    ny = 1
    while 4 * ny * ny <= groups:
        ny *= 2
    nz = groups // ny
    width = min(BS, ncols)
    per = ncols // width
    ratio = BS // width
    units_total = NP // width
    col = lax.axis_index("col")
    branch = lax.axis_index("branch")
    pivot_devices = P_SIZE // ncols

    blocks = extend_map[0]
    hit = blocks[:, None] == jnp.arange(NP // BS, dtype=jnp.int32)[None, :]
    present = jnp.any(hit, axis=0).astype(jnp.int32)
    child_block = jnp.sum(
        jnp.where(hit, jnp.arange(blocks.shape[0], dtype=jnp.int32)[:, None], 0), axis=0
    ).astype(jnp.int32)
    t = jnp.arange(units_total, dtype=jnp.int32)
    units = P_SIZE // width + child_block[t // ratio] * ratio + t % ratio
    keeps = present[t // ratio]
    source = units // per
    parts = units % per

    def unit_rows(u):
        return lax.dynamic_slice_in_dim(front, units[u] * width, width, 0)

    def placed(x):
        if pivot_devices == 1:
            return jnp.where(col == 0, x, 0.0)
        wide = jnp.zeros((x.shape[0], P_SIZE), F32)
        wide = lax.dynamic_update_slice_in_dim(wide, x, jnp.minimum(col, pivot_devices - 1) * ncols, 1)
        return jnp.where(col < pivot_devices, wide, 0.0)

    pivot_units = PP // width

    def pivot_column(b):
        local = units[b] - col * per
        ok = (local >= 0) & (local < per) & (keeps[b] > 0)
        column = lax.dynamic_slice_in_dim(front, jnp.clip(local, 0, per - 1) * width, width, 1)
        body = [
            jnp.where(ok & (keeps[a] > 0), lax.dynamic_slice_in_dim(column, units[a] * width, width, 0), 0.0)
            for a in range(pivot_units)
        ]
        return jnp.concatenate(body, axis=0)

    corner = jnp.concatenate([pivot_column(b) for b in range(pivot_units)], axis=1)
    corner = corner + jnp.where(branch == 0, placed(parent_front[:PP]), 0.0)
    corner = halve(corner, "branch")

    def rows_for(target):
        return jnp.concatenate([unit_rows(target * per + a) for a in range(per)], axis=0)

    def moved(k, rows):
        pairs = [(c, c ^ k) for c in range(groups) if c >= pivot_devices]
        return lax.ppermute(rows, "col", pairs)

    near, far = list(range(1, ny)), list(reversed(range(ny, groups)))
    rows = {k: rows_for(col ^ k) for k in range(groups)}
    received = {0: rows[0]}
    for k in near:
        received[k] = moved(k, rows[k])

    z, y = col // ny, col % ny
    head = front[:P_SIZE]
    beside = [from_beside(head, "col", ny, j) for j in near]
    line, steps = line_gather(head, "col", ny, [(corner, [rows[k] for k in far])])
    corner = halve(corner, "col", gates=[head[:8]] + steps[2:])
    corner = join(corner, "col")

    def in_line(c, parts):
        return sum(jnp.where(z == (c // ny + k) % len(line), parts[k], 0.0) for k in range(len(line)))

    pivot_line = in_line(0, line)
    pivot_parts = [pivot_line] + [from_beside(pivot_line, "col", ny, j) for j in near]
    pivots = [
        sum(jnp.where(y == (c - j) % ny, pivot_parts[j], 0.0) for j in range(ny)) for c in range(pivot_devices)]
    pivots = jnp.concatenate(pivots, axis=1) if pivot_devices > 1 else pivots[0]

    for k in far[:EARLY]:
        row, _ = lax.optimization_barrier((rows[k], (steps[-1], corner, beside)))
        received[k] = moved(k, row)
    others = lax.optimization_barrier((jnp.stack(line[1:]), corner))[0]
    others = [from_beside(others, "col", ny, j) for j in near]
    gathered = line + [x for j in range(ny - 1) for x in [beside[j]] + [others[j][k] for k in range(len(line) - 1)]]
    slots = (source % ny - y) % ny * len(line) + (z - source // ny) % len(line)

    inverse = inverse_factor(pivots)
    for k in far[EARLY:]:
        row, _ = lax.optimization_barrier((rows[k], inverse))
        received[k] = moved(k, row)
    places = col ^ source
    child_mine = product(inverse, front[:P_SIZE], 1, 0)

    early = [received[k] for k in far[:EARLY]]
    inverse, early = lax.optimization_barrier((inverse, early))
    received.update(zip(far[:EARLY], early))
    factor = jnp.stack([product(inverse, x, 1, 0) for x in gathered])

    def factor_columns(u):
        block = lax.dynamic_slice(factor, (slots[u], 0, parts[u] * width), (1, P_SIZE, width))
        return jnp.where(keeps[u] > 0, block[0], 0.0)

    mine = jnp.concatenate([factor_columns(col * per + a) for a in range(per)], axis=1)
    mine_keep = jnp.repeat(lax.dynamic_slice_in_dim(keeps, col * per, per), width)[:, None] > 0
    pieces = jnp.stack([jnp.where(mine_keep, received[k], 0.0) for k in range(groups)])
    left = three_part(mine)
    n = pivot_units
    first = spread_update(slots[:n], places[:n], parts[:n], keeps[:n], left, factor, pieces, width)
    first = jnp.concatenate([first[u] for u in range(n)], axis=1)
    steps = []
    first = first + jnp.where(branch == 0, parent_front[:PP].T, 0.0)
    first = join(halve(first, "branch", steps), "branch", steps)

    head = jnp.concatenate([factor_columns(u) for u in range(pivot_units)], axis=1)
    corner = corner - halve(product(head, head, 0, 0), "branch")
    corner, _ = lax.optimization_barrier((corner, received[far[-2]]))
    corner = join(corner, "branch")

    owned = units_total // branches
    spread = [None] * branches
    for i, m in enumerate(reversed(range(branches))):
        table, _ = lax.optimization_barrier((slots, steps[min(i, len(steps) - 1)]))
        at = lambda table: lax.dynamic_slice_in_dim(table, (branch ^ m) * owned, owned)
        spread[m] = spread_update(at(table), at(places), at(parts), at(keeps), left, factor, pieces, width)
    terms, sent = scatter_sum(spread, "branch")
    corner, _ = lax.optimization_barrier((corner, sent))
    parent_inverse = inverse_factor(corner)

    parent_mine = product(parent_inverse, first, 1, 1)
    if groups // ny == branches:
        line, parent_inverse = lax.optimization_barrier((share_line(first, ny), parent_inverse))
        sides = jnp.concatenate(share_beside(line, ny), axis=0)
    else:
        sides = lax.dynamic_slice_in_dim(
            lax.all_gather(first, "col"), branch * groups // branches, groups // branches, 0).reshape(nrows, PP)
    result = finish(parent_front, terms, sides, parent_inverse, parent_mine)
    return (child_mine[None], parent_mine, result)


def solution(mesh):
    in_specs = (P("branch", None, "col"), P("branch", None), P("branch", "col"))
    out_specs = (P("branch", None, "col"), P(None, "col"), P("branch", "col"))
    return jax.shard_map(
        on_device, mesh=mesh, in_specs=in_specs, out_specs=out_specs, check_vma=False
    )
```

```python
import jax
import jax.numpy as jnp
from jax import lax
from jax.experimental import pallas as pl
from jax.experimental.pallas import tpu as pltpu
from jax.sharding import PartitionSpec as P

BS = 256
P_SIZE = 512
NP = 4096
PP = 512
EARLY = 3

SUB = 8
LANES = 128
F32 = jnp.float32


def mm(a, b, ca, cb):
    return lax.dot_general(
        a, b, (((ca,), (cb,)), ((), ())),
        precision=lax.Precision.HIGHEST, preferred_element_type=F32,
    )


def factor_tile(rows):
    sub = lax.broadcasted_iota(jnp.int32, (SUB, LANES), 0)
    lane = lax.broadcasted_iota(jnp.int32, (SUB, LANES), 1)
    rows = list(rows)
    count = len(rows)
    spread = lambda column: jnp.broadcast_to(column, (SUB, LANES))
    for g in range(count):
        base = g * SUB
        inside = (lane >= base) & (lane < base + SUB)
        cols = [spread(rows[g][:, base + j:base + j + 1]) for j in range(SUB)]
        panel = jnp.where(inside, jnp.where(lane - base == sub, 1.0, 0.0), rows[g])
        kept = panel
        pivots = cols[0]
        for j in range(SUB):
            here = sub == j
            pivot = spread(cols[j][j:j + 1, :])
            inverse = 1.0 / pivot
            scaled = cols[j] * inverse
            row = spread(panel[j:j + 1, :])
            kept = jnp.where(here, panel, kept)
            pivots = jnp.where(here, pivot, pivots)
            panel = jnp.where(here, row * inverse, panel - scaled * row)
            for m in range(j + 1, SUB):
                across = spread(cols[m][j:j + 1, :])
                cols[m] = jnp.where(here, across * inverse, cols[m] - scaled * across)
        rows[g] = kept * lax.rsqrt(pivots)
        panel_rows = [spread(panel[j:j + 1, :]) for j in range(SUB)]
        for i in range(g + 1, count):
            terms = [spread(rows[i][:, base + j:base + j + 1]) * panel_rows[j] for j in range(SUB)]
            while len(terms) > 1:
                terms = [terms[t] + terms[t + 1] for t in range(0, len(terms), 2)]
            rows[i] = jnp.where(inside, 0.0, rows[i]) - terms[0]
    return rows


def inverse_factor_kernel(a_ref, w_ref):
    n = a_ref.shape[0]
    steps = n // LANES
    tri = (lax.broadcasted_iota(jnp.int32, (LANES, LANES), 0)
           >= lax.broadcasted_iota(jnp.int32, (LANES, LANES), 1))
    work = [[a_ref[i * LANES:(i + 1) * LANES, j * LANES:(j + 1) * LANES]
             for j in range(steps)] for i in range(steps)]
    for k in range(steps):
        tile = work[k][k]
        done = factor_tile([tile[g * SUB:(g + 1) * SUB, :] for g in range(LANES // SUB)])
        inv = jnp.where(tri, jnp.concatenate(done, axis=0), 0.0)
        work[k] = [inv if j == k else mm(inv, work[k][j], 1, 0) for j in range(steps)]
        for i in range(k + 1, steps):
            left = work[k][i]
            for j in range(steps):
                product = mm(left, work[k][j], 0, 0)
                work[i][j] = -product if j == k else work[i][j] - product
    for i in range(steps):
        for j in range(steps):
            value = work[i][j] if j <= i else jnp.zeros((LANES, LANES), F32)
            w_ref[i * LANES:(i + 1) * LANES, j * LANES:(j + 1) * LANES] = value


def inverse_factor(a):
    n = a.shape[0]
    return pl.pallas_call(
        inverse_factor_kernel,
        out_shape=jax.ShapeDtypeStruct((n, n), F32),
        in_specs=[pl.BlockSpec(memory_space=pltpu.VMEM)],
        out_specs=pl.BlockSpec(memory_space=pltpu.VMEM),
        compiler_params=pltpu.CompilerParams(vmem_limit_bytes=32 * 1024 * 1024),
        cost_estimate=pl.CostEstimate(flops=n * n * n, bytes_accessed=8 * n * n, transcendentals=0),
    )(a)


def spread_kernel(slot_ref, place_ref, part_ref, keep_ref, left_ref, factor_ref, piece_ref, out_ref):
    t = pl.program_id(0)
    whole = factor_ref[0]
    high = whole.astype(jnp.bfloat16)
    low = (whole - high.astype(F32)).astype(jnp.bfloat16)
    right = jnp.concatenate([high, low, high], axis=0)
    value = lax.dot_general(left_ref[...], right, (((1,), (0,)), ((), ())), preferred_element_type=F32)
    out_ref[0] = jnp.where(keep_ref[t] > 0, piece_ref[0] - value, 0.0)


def three_part(x):
    turned = x.T
    rounded = lax.reduce_precision(turned, 8, 7)
    high = rounded.astype(jnp.bfloat16)
    low = (turned - rounded).astype(jnp.bfloat16)
    return jnp.concatenate([high, high, low], axis=1)


def spread_update(slots, places, parts, keeps, left, factor, pieces, width):
    count = slots.shape[0]
    q, depth = left.shape[0], left.shape[1] // 3
    return pl.pallas_call(
        spread_kernel,
        grid_spec=pltpu.PrefetchScalarGridSpec(
            num_scalar_prefetch=4,
            grid=(count,),
            in_specs=[
                pl.BlockSpec((q, 3 * depth), lambda t, *refs: (0, 0)),
                pl.BlockSpec((1, depth, width), lambda t, s, p, h, k: (s[t], 0, h[t])),
                pl.BlockSpec((1, q, width), lambda t, s, p, h, k: (p[t], 0, h[t])),
            ],
            out_specs=pl.BlockSpec((1, q, width), lambda t, *refs: (t, 0, 0)),
        ),
        out_shape=jax.ShapeDtypeStruct((count, q, width), F32),
        compiler_params=pltpu.CompilerParams(vmem_limit_bytes=56 * 1024 * 1024),
        cost_estimate=pl.CostEstimate(
            flops=6 * count * q * depth * width,
            bytes_accessed=4 * count * width * (2 * q + depth), transcendentals=0),
    )(slots, places, parts, keeps, left, factor, pieces)


def product(a, b, ca, cb, precision=lax.Precision.HIGH):
    return lax.dot_general(a, b, (((ca,), (cb,)), ((), ())), precision=precision)


def flip(x, axis, bit):
    n = lax.axis_size(axis)
    return lax.ppermute(x, axis, [(i, i ^ bit) for i in range(n)])


def axis_bits(axis):
    return [1 << i for i in range(lax.axis_size(axis).bit_length() - 1)]


def halve(x, axis, steps=None, gates=()):
    me = lax.axis_index(axis)
    for step, bit in enumerate(axis_bits(axis)):
        if step < len(gates):
            x, _ = lax.optimization_barrier((x, gates[step]))
        high = (me // bit) % 2
        half = x.shape[0] // 2
        away = lax.dynamic_slice_in_dim(x, (1 - high) * half, half, 0)
        x = lax.dynamic_slice_in_dim(x, high * half, half, 0) + flip(away, axis, bit)
        if steps is not None:
            steps.append(x)
    return x


def join(x, axis, steps=None):
    me = lax.axis_index(axis)
    for bit in reversed(axis_bits(axis)):
        high = (me // bit) % 2
        other = flip(x, axis, bit)
        x = jnp.concatenate([jnp.where(high == 0, x, other), jnp.where(high == 0, other, x)], axis=0)
        if steps is not None:
            steps.append(x)
    return x


def scatter_sum(parts, axis):
    parts = list(parts)
    terms = [parts[0]]
    for bit in axis_bits(axis):
        for m in reversed(range(len(parts))):
            if m & bit and not m & (bit - 1):
                sent = parts[m]
                other = flip(sent, axis, bit)
                if m == bit:
                    terms.append(other)
                else:
                    parts[m ^ bit] = parts[m ^ bit] + other
    return terms, sent


def three_rows(x):
    high = x.astype(jnp.bfloat16)
    return high, (x - high.astype(F32)).astype(jnp.bfloat16)


def finish_kernel(parent_ref, side_ref, inverse_ref, mine_ref, *rest):
    terms, out_ref = rest[:-1], rest[-1]
    total = terms[0][0]
    for term in terms[1:]:
        total = total + term[0]
    dot = lambda a, b, cb: lax.dot_general(a, b, (((1,), (cb,)), ((), ())), preferred_element_type=F32)
    high, low = three_rows(side_ref[0])
    ihigh, ilow = three_rows(inverse_ref[...])
    factor = dot(jnp.concatenate([high, high, low], axis=1), jnp.concatenate([ihigh, ilow, ihigh], axis=1), 1)
    high, low = three_rows(factor)
    mhigh, mlow = three_rows(mine_ref[...])
    outer = dot(jnp.concatenate([high, high, low], axis=1), jnp.concatenate([mhigh, mlow, mhigh], axis=0), 0)
    out_ref[...] = parent_ref[...] + total.T - outer


def finish(parent, terms, sides, inverse, mine):
    count, q, width = terms[0].shape
    depth = inverse.shape[0]
    sides = sides.reshape(count, width, depth)
    whole = lambda t: (0, 0)
    block = lambda t: (t, 0, 0)
    return pl.pallas_call(
        finish_kernel,
        grid=(count,),
        in_specs=[
            pl.BlockSpec((width, q), lambda t: (t, 0)),
            pl.BlockSpec((1, width, depth), block),
            pl.BlockSpec((depth, depth), whole),
            pl.BlockSpec((depth, q), whole),
        ] + [pl.BlockSpec((1, q, width), block)] * len(terms),
        out_specs=pl.BlockSpec((width, q), lambda t: (t, 0)),
        out_shape=jax.ShapeDtypeStruct(parent.shape, F32),
        compiler_params=pltpu.CompilerParams(vmem_limit_bytes=48 * 1024 * 1024),
        cost_estimate=pl.CostEstimate(
            flops=6 * count * width * depth * (q + depth), bytes_accessed=8 * parent.size * 4, transcendentals=0),
    )(parent, sides, inverse, mine, *terms)


def line_gather(x, axis, ny, gates):
    n = lax.axis_size(axis)
    nz = n // ny
    up, down = [x], [x]
    for step in range(1, nz):
        ends = (up[-1], down[-1])
        if 1 < step < len(gates) + 2:
            ends, _ = lax.optimization_barrier((ends, gates[step - 2]))
        up.append(lax.ppermute(ends[0], axis, [(c, c + ny) for c in range(n) if step - 1 <= c // ny < nz - 1]))
        down.append(lax.ppermute(ends[1], axis, [(c, c - ny) for c in range(n) if 0 < c // ny <= nz - step]))
    return [x] + [up[k] + down[nz - k] for k in range(1, nz)], list(zip(up, down))


def from_beside(x, axis, ny, j):
    n = lax.axis_size(axis)
    return lax.ppermute(x, axis, [(c, c // ny * ny + (c % ny - j) % ny) for c in range(n)])


def share_line(x, ny):
    branches = lax.axis_size("branch")
    groups = lax.axis_size("col")
    nz = groups // ny
    place = lambda b, z, y: b * groups + z * ny + y
    got = jnp.where(lax.axis_index("col") // ny == lax.axis_index("branch"), x, 0.0)
    for off in range(1, nz):
        pairs = [(place(b, b, y), place(b, (b + off) % nz, y)) for b in range(branches) for y in range(ny)]
        got = got + lax.ppermute(x, ("branch", "col"), pairs)
    return got


def share_beside(got, ny):
    groups = lax.axis_size("col")
    y = lax.axis_index("col") % ny
    shares = [got]
    for j in range(1, ny):
        pairs = [(c, c // ny * ny + (c % ny - j) % ny) for c in range(groups)]
        shares.append(lax.ppermute(got, "col", pairs))
    return [sum(jnp.where(y == (i - j) % ny, shares[j], 0.0) for j in range(ny)) for i in range(ny)]


def on_device(child_fronts, extend_map, parent_front):
    front = child_fronts[0]
    order, ncols = front.shape
    nrows, pcols = parent_front.shape
    groups = lax.axis_size("col")
    branches = lax.axis_size("branch")
    ny = 1
    while 4 * ny * ny <= groups:
        ny *= 2
    nz = groups // ny
    width = min(BS, ncols)
    per = ncols // width
    ratio = BS // width
    units_total = NP // width
    col = lax.axis_index("col")
    branch = lax.axis_index("branch")
    pivot_devices = P_SIZE // ncols

    blocks = extend_map[0]
    hit = blocks[:, None] == jnp.arange(NP // BS, dtype=jnp.int32)[None, :]
    present = jnp.any(hit, axis=0).astype(jnp.int32)
    child_block = jnp.sum(
        jnp.where(hit, jnp.arange(blocks.shape[0], dtype=jnp.int32)[:, None], 0), axis=0
    ).astype(jnp.int32)
    t = jnp.arange(units_total, dtype=jnp.int32)
    units = P_SIZE // width + child_block[t // ratio] * ratio + t % ratio
    keeps = present[t // ratio]
    source = units // per
    parts = units % per

    def unit_rows(u):
        return lax.dynamic_slice_in_dim(front, units[u] * width, width, 0)

    def placed(x):
        if pivot_devices == 1:
            return jnp.where(col == 0, x, 0.0)
        wide = jnp.zeros((x.shape[0], P_SIZE), F32)
        wide = lax.dynamic_update_slice_in_dim(wide, x, jnp.minimum(col, pivot_devices - 1) * ncols, 1)
        return jnp.where(col < pivot_devices, wide, 0.0)

    pivot_units = PP // width

    def pivot_column(b):
        local = units[b] - col * per
        ok = (local >= 0) & (local < per) & (keeps[b] > 0)
        column = lax.dynamic_slice_in_dim(front, jnp.clip(local, 0, per - 1) * width, width, 1)
        body = [
            jnp.where(ok & (keeps[a] > 0), lax.dynamic_slice_in_dim(column, units[a] * width, width, 0), 0.0)
            for a in range(pivot_units)
        ]
        return jnp.concatenate(body, axis=0)

    corner = jnp.concatenate([pivot_column(b) for b in range(pivot_units)], axis=1)
    corner = corner + jnp.where(branch == 0, placed(parent_front[:PP]), 0.0)
    corner = halve(corner, "branch")

    def rows_for(target):
        return jnp.concatenate([unit_rows(target * per + a) for a in range(per)], axis=0)

    def moved(k, rows):
        pairs = [(c, c ^ k) for c in range(groups) if c >= pivot_devices]
        return lax.ppermute(rows, "col", pairs)

    near, far = list(range(1, ny)), list(reversed(range(ny, groups)))
    rows = {k: rows_for(col ^ k) for k in range(groups)}
    received = {0: rows[0]}
    for k in near:
        received[k] = moved(k, rows[k])

    z, y = col // ny, col % ny
    head = front[:P_SIZE]
    beside = [from_beside(head, "col", ny, j) for j in near]
    line, steps = line_gather(head, "col", ny, [(corner, [rows[k] for k in far])])
    corner = halve(corner, "col", gates=[head[:8]] + steps[2:])
    corner = join(corner, "col")

    def in_line(c, parts):
        return sum(jnp.where(z == (c // ny + k) % len(line), parts[k], 0.0) for k in range(len(line)))

    pivot_line = in_line(0, line)
    pivot_parts = [pivot_line] + [from_beside(pivot_line, "col", ny, j) for j in near]
    pivots = [
        sum(jnp.where(y == (c - j) % ny, pivot_parts[j], 0.0) for j in range(ny)) for c in range(pivot_devices)]
    pivots = jnp.concatenate(pivots, axis=1) if pivot_devices > 1 else pivots[0]

    for k in far[:EARLY]:
        row, _ = lax.optimization_barrier((rows[k], (steps[-1], corner, beside)))
        received[k] = moved(k, row)
    others = lax.optimization_barrier((jnp.stack(line[1:]), corner))[0]
    others = [from_beside(others, "col", ny, j) for j in near]
    gathered = line + [x for j in range(ny - 1) for x in [beside[j]] + [others[j][k] for k in range(len(line) - 1)]]
    slots = (source % ny - y) % ny * len(line) + (z - source // ny) % len(line)

    inverse = inverse_factor(pivots)
    for k in far[EARLY:]:
        row, _ = lax.optimization_barrier((rows[k], inverse))
        received[k] = moved(k, row)
    places = col ^ source
    child_mine = product(inverse, front[:P_SIZE], 1, 0)

    early = [received[k] for k in far[:EARLY - 1]]
    inverse, early = lax.optimization_barrier((inverse, early))
    received.update(zip(far, early))
    factor = jnp.stack([product(inverse, x, 1, 0) for x in gathered])

    def factor_columns(u):
        block = lax.dynamic_slice(factor, (slots[u], 0, parts[u] * width), (1, P_SIZE, width))
        return jnp.where(keeps[u] > 0, block[0], 0.0)

    mine = jnp.concatenate([factor_columns(col * per + a) for a in range(per)], axis=1)
    mine_keep = jnp.repeat(lax.dynamic_slice_in_dim(keeps, col * per, per), width)[:, None] > 0
    pieces = jnp.stack([jnp.where(mine_keep, received[k], 0.0) for k in range(groups)])
    left = three_part(mine)
    head = jnp.concatenate([factor_columns(u) for u in range(pivot_units)], axis=1)
    corner = corner - halve(product(head, head, 0, 0), "branch")
    left, _ = lax.optimization_barrier((left, corner))
    corner = join(corner, "branch")
    n = pivot_units
    first = spread_update(slots[:n], places[:n], parts[:n], keeps[:n], left, factor, pieces, width)
    first = jnp.concatenate([first[u] for u in range(n)], axis=1)
    steps = []
    first = first + jnp.where(branch == 0, parent_front[:PP].T, 0.0)
    first = join(halve(first, "branch", steps), "branch", steps)

    owned = units_total // branches
    spread = [None] * branches
    for i, m in enumerate(reversed(range(branches))):
        table, _ = lax.optimization_barrier((slots, steps[min(i, len(steps) - 1)]))
        at = lambda table: lax.dynamic_slice_in_dim(table, (branch ^ m) * owned, owned)
        spread[m] = spread_update(at(table), at(places), at(parts), at(keeps), left, factor, pieces, width)
    terms, sent = scatter_sum(spread, "branch")
    corner, _ = lax.optimization_barrier((corner, sent))
    parent_inverse = inverse_factor(corner)

    parent_mine = product(parent_inverse, first, 1, 1)
    if groups // ny == branches:
        line, parent_inverse = lax.optimization_barrier((share_line(first, ny), parent_inverse))
        sides = jnp.concatenate(share_beside(line, ny), axis=0)
    else:
        sides = lax.dynamic_slice_in_dim(
            lax.all_gather(first, "col"), branch * groups // branches, groups // branches, 0).reshape(nrows, PP)
    result = finish(parent_front, terms, sides, parent_inverse, parent_mine)
    return (child_mine[None], parent_mine, result)


def solution(mesh):
    in_specs = (P("branch", None, "col"), P("branch", None), P("branch", "col"))
    out_specs = (P("branch", None, "col"), P(None, "col"), P("branch", "col"))
    return jax.shard_map(
        on_device, mesh=mesh, in_specs=in_specs, out_specs=out_specs, check_vma=False
    )
```

```python
import jax
import jax.numpy as jnp
from jax import lax
from jax.experimental import pallas as pl
from jax.experimental.pallas import tpu as pltpu
from jax.sharding import PartitionSpec as P

BS = 256
P_SIZE = 512
NP = 4096
PP = 512
EARLY = 4

SUB = 8
LANES = 128
F32 = jnp.float32


def mm(a, b, ca, cb):
    return lax.dot_general(
        a, b, (((ca,), (cb,)), ((), ())),
        precision=lax.Precision.HIGHEST, preferred_element_type=F32,
    )


def factor_tile(rows):
    sub = lax.broadcasted_iota(jnp.int32, (SUB, LANES), 0)
    lane = lax.broadcasted_iota(jnp.int32, (SUB, LANES), 1)
    rows = list(rows)
    count = len(rows)
    spread = lambda column: jnp.broadcast_to(column, (SUB, LANES))
    for g in range(count):
        base = g * SUB
        inside = (lane >= base) & (lane < base + SUB)
        cols = [spread(rows[g][:, base + j:base + j + 1]) for j in range(SUB)]
        panel = jnp.where(inside, jnp.where(lane - base == sub, 1.0, 0.0), rows[g])
        kept = panel
        pivots = cols[0]
        for j in range(SUB):
            here = sub == j
            pivot = spread(cols[j][j:j + 1, :])
            inverse = 1.0 / pivot
            scaled = cols[j] * inverse
            row = spread(panel[j:j + 1, :])
            kept = jnp.where(here, panel, kept)
            pivots = jnp.where(here, pivot, pivots)
            panel = jnp.where(here, row * inverse, panel - scaled * row)
            for m in range(j + 1, SUB):
                across = spread(cols[m][j:j + 1, :])
                cols[m] = jnp.where(here, across * inverse, cols[m] - scaled * across)
        rows[g] = kept * lax.rsqrt(pivots)
        panel_rows = [spread(panel[j:j + 1, :]) for j in range(SUB)]
        for i in range(g + 1, count):
            terms = [spread(rows[i][:, base + j:base + j + 1]) * panel_rows[j] for j in range(SUB)]
            while len(terms) > 1:
                terms = [terms[t] + terms[t + 1] for t in range(0, len(terms), 2)]
            rows[i] = jnp.where(inside, 0.0, rows[i]) - terms[0]
    return rows


def inverse_factor_kernel(a_ref, w_ref):
    n = a_ref.shape[0]
    steps = n // LANES
    tri = (lax.broadcasted_iota(jnp.int32, (LANES, LANES), 0)
           >= lax.broadcasted_iota(jnp.int32, (LANES, LANES), 1))
    work = [[a_ref[i * LANES:(i + 1) * LANES, j * LANES:(j + 1) * LANES]
             for j in range(steps)] for i in range(steps)]
    for k in range(steps):
        tile = work[k][k]
        done = factor_tile([tile[g * SUB:(g + 1) * SUB, :] for g in range(LANES // SUB)])
        inv = jnp.where(tri, jnp.concatenate(done, axis=0), 0.0)
        work[k] = [inv if j == k else mm(inv, work[k][j], 1, 0) for j in range(steps)]
        for i in range(k + 1, steps):
            left = work[k][i]
            for j in range(steps):
                product = mm(left, work[k][j], 0, 0)
                work[i][j] = -product if j == k else work[i][j] - product
    for i in range(steps):
        for j in range(steps):
            value = work[i][j] if j <= i else jnp.zeros((LANES, LANES), F32)
            w_ref[i * LANES:(i + 1) * LANES, j * LANES:(j + 1) * LANES] = value


def inverse_factor(a):
    n = a.shape[0]
    return pl.pallas_call(
        inverse_factor_kernel,
        out_shape=jax.ShapeDtypeStruct((n, n), F32),
        in_specs=[pl.BlockSpec(memory_space=pltpu.VMEM)],
        out_specs=pl.BlockSpec(memory_space=pltpu.VMEM),
        compiler_params=pltpu.CompilerParams(vmem_limit_bytes=32 * 1024 * 1024),
        cost_estimate=pl.CostEstimate(flops=n * n * n, bytes_accessed=8 * n * n, transcendentals=0),
    )(a)


def spread_kernel(slot_ref, place_ref, part_ref, keep_ref, left_ref, factor_ref, piece_ref, out_ref):
    t = pl.program_id(0)
    whole = factor_ref[0]
    high = whole.astype(jnp.bfloat16)
    low = (whole - high.astype(F32)).astype(jnp.bfloat16)
    right = jnp.concatenate([high, low, high], axis=0)
    value = lax.dot_general(left_ref[...], right, (((1,), (0,)), ((), ())), preferred_element_type=F32)
    out_ref[0] = jnp.where(keep_ref[t] > 0, piece_ref[0] - value, 0.0)


def three_part(x):
    turned = x.T
    rounded = lax.reduce_precision(turned, 8, 7)
    high = rounded.astype(jnp.bfloat16)
    low = (turned - rounded).astype(jnp.bfloat16)
    return jnp.concatenate([high, high, low], axis=1)


def spread_update(slots, places, parts, keeps, left, factor, pieces, width):
    count = slots.shape[0]
    q, depth = left.shape[0], left.shape[1] // 3
    return pl.pallas_call(
        spread_kernel,
        grid_spec=pltpu.PrefetchScalarGridSpec(
            num_scalar_prefetch=4,
            grid=(count,),
            in_specs=[
                pl.BlockSpec((q, 3 * depth), lambda t, *refs: (0, 0)),
                pl.BlockSpec((1, depth, width), lambda t, s, p, h, k: (s[t], 0, h[t])),
                pl.BlockSpec((1, q, width), lambda t, s, p, h, k: (p[t], 0, h[t])),
            ],
            out_specs=pl.BlockSpec((1, q, width), lambda t, *refs: (t, 0, 0)),
        ),
        out_shape=jax.ShapeDtypeStruct((count, q, width), F32),
        compiler_params=pltpu.CompilerParams(vmem_limit_bytes=56 * 1024 * 1024),
        cost_estimate=pl.CostEstimate(
            flops=6 * count * q * depth * width,
            bytes_accessed=4 * count * width * (2 * q + depth), transcendentals=0),
    )(slots, places, parts, keeps, left, factor, pieces)


def product(a, b, ca, cb, precision=lax.Precision.HIGH):
    return lax.dot_general(a, b, (((ca,), (cb,)), ((), ())), precision=precision)


def flip(x, axis, bit):
    n = lax.axis_size(axis)
    return lax.ppermute(x, axis, [(i, i ^ bit) for i in range(n)])


def axis_bits(axis):
    return [1 << i for i in range(lax.axis_size(axis).bit_length() - 1)]


def halve(x, axis, steps=None, gates=()):
    me = lax.axis_index(axis)
    for step, bit in enumerate(axis_bits(axis)):
        if step < len(gates):
            x, _ = lax.optimization_barrier((x, gates[step]))
        high = (me // bit) % 2
        half = x.shape[0] // 2
        away = lax.dynamic_slice_in_dim(x, (1 - high) * half, half, 0)
        x = lax.dynamic_slice_in_dim(x, high * half, half, 0) + flip(away, axis, bit)
        if steps is not None:
            steps.append(x)
    return x


def join(x, axis, steps=None):
    me = lax.axis_index(axis)
    for bit in reversed(axis_bits(axis)):
        high = (me // bit) % 2
        other = flip(x, axis, bit)
        x = jnp.concatenate([jnp.where(high == 0, x, other), jnp.where(high == 0, other, x)], axis=0)
        if steps is not None:
            steps.append(x)
    return x


def scatter_sum(parts, axis):
    parts = list(parts)
    terms = [parts[0]]
    for bit in axis_bits(axis):
        for m in reversed(range(len(parts))):
            if m & bit and not m & (bit - 1):
                sent = parts[m]
                other = flip(sent, axis, bit)
                if m == bit:
                    terms.append(other)
                else:
                    parts[m ^ bit] = parts[m ^ bit] + other
    return terms, sent


def three_rows(x):
    high = x.astype(jnp.bfloat16)
    return high, (x - high.astype(F32)).astype(jnp.bfloat16)


def finish_kernel(parent_ref, side_ref, inverse_ref, mine_ref, *rest):
    terms, out_ref = rest[:-1], rest[-1]
    total = terms[0][0]
    for term in terms[1:]:
        total = total + term[0]
    dot = lambda a, b, cb: lax.dot_general(a, b, (((1,), (cb,)), ((), ())), preferred_element_type=F32)
    high, low = three_rows(side_ref[0])
    ihigh, ilow = three_rows(inverse_ref[...])
    factor = dot(jnp.concatenate([high, high, low], axis=1), jnp.concatenate([ihigh, ilow, ihigh], axis=1), 1)
    high, low = three_rows(factor)
    mhigh, mlow = three_rows(mine_ref[...])
    outer = dot(jnp.concatenate([high, high, low], axis=1), jnp.concatenate([mhigh, mlow, mhigh], axis=0), 0)
    out_ref[...] = parent_ref[...] + total.T - outer


def finish(parent, terms, sides, inverse, mine):
    count, q, width = terms[0].shape
    depth = inverse.shape[0]
    sides = sides.reshape(count, width, depth)
    whole = lambda t: (0, 0)
    block = lambda t: (t, 0, 0)
    return pl.pallas_call(
        finish_kernel,
        grid=(count,),
        in_specs=[
            pl.BlockSpec((width, q), lambda t: (t, 0)),
            pl.BlockSpec((1, width, depth), block),
            pl.BlockSpec((depth, depth), whole),
            pl.BlockSpec((depth, q), whole),
        ] + [pl.BlockSpec((1, q, width), block)] * len(terms),
        out_specs=pl.BlockSpec((width, q), lambda t: (t, 0)),
        out_shape=jax.ShapeDtypeStruct(parent.shape, F32),
        compiler_params=pltpu.CompilerParams(vmem_limit_bytes=48 * 1024 * 1024),
        cost_estimate=pl.CostEstimate(
            flops=6 * count * width * depth * (q + depth), bytes_accessed=8 * parent.size * 4, transcendentals=0),
    )(parent, sides, inverse, mine, *terms)


def line_gather(x, axis, ny, gates):
    n = lax.axis_size(axis)
    nz = n // ny
    up, down = [x], [x]
    for step in range(1, nz):
        ends = (up[-1], down[-1])
        if 1 < step < len(gates) + 2:
            ends, _ = lax.optimization_barrier((ends, gates[step - 2]))
        up.append(lax.ppermute(ends[0], axis, [(c, c + ny) for c in range(n) if step - 1 <= c // ny < nz - 1]))
        down.append(lax.ppermute(ends[1], axis, [(c, c - ny) for c in range(n) if 0 < c // ny <= nz - step]))
    return [x] + [up[k] + down[nz - k] for k in range(1, nz)], list(zip(up, down))


def from_beside(x, axis, ny, j):
    n = lax.axis_size(axis)
    return lax.ppermute(x, axis, [(c, c // ny * ny + (c % ny - j) % ny) for c in range(n)])


def share_line(x, ny):
    branches = lax.axis_size("branch")
    groups = lax.axis_size("col")
    nz = groups // ny
    place = lambda b, z, y: b * groups + z * ny + y
    got = jnp.where(lax.axis_index("col") // ny == lax.axis_index("branch"), x, 0.0)
    for off in range(1, nz):
        pairs = [(place(b, b, y), place(b, (b + off) % nz, y)) for b in range(branches) for y in range(ny)]
        got = got + lax.ppermute(x, ("branch", "col"), pairs)
    return got


def share_beside(got, ny):
    groups = lax.axis_size("col")
    y = lax.axis_index("col") % ny
    shares = [got]
    for j in range(1, ny):
        pairs = [(c, c // ny * ny + (c % ny - j) % ny) for c in range(groups)]
        shares.append(lax.ppermute(got, "col", pairs))
    return [sum(jnp.where(y == (i - j) % ny, shares[j], 0.0) for j in range(ny)) for i in range(ny)]


def on_device(child_fronts, extend_map, parent_front):
    front = child_fronts[0]
    order, ncols = front.shape
    nrows, pcols = parent_front.shape
    groups = lax.axis_size("col")
    branches = lax.axis_size("branch")
    ny = 1
    while 4 * ny * ny <= groups:
        ny *= 2
    nz = groups // ny
    width = min(BS, ncols)
    per = ncols // width
    ratio = BS // width
    units_total = NP // width
    col = lax.axis_index("col")
    branch = lax.axis_index("branch")
    pivot_devices = P_SIZE // ncols

    blocks = extend_map[0]
    hit = blocks[:, None] == jnp.arange(NP // BS, dtype=jnp.int32)[None, :]
    present = jnp.any(hit, axis=0).astype(jnp.int32)
    child_block = jnp.sum(
        jnp.where(hit, jnp.arange(blocks.shape[0], dtype=jnp.int32)[:, None], 0), axis=0
    ).astype(jnp.int32)
    t = jnp.arange(units_total, dtype=jnp.int32)
    units = P_SIZE // width + child_block[t // ratio] * ratio + t % ratio
    keeps = present[t // ratio]
    source = units // per
    parts = units % per

    def unit_rows(u):
        return lax.dynamic_slice_in_dim(front, units[u] * width, width, 0)

    def placed(x):
        if pivot_devices == 1:
            return jnp.where(col == 0, x, 0.0)
        wide = jnp.zeros((x.shape[0], P_SIZE), F32)
        wide = lax.dynamic_update_slice_in_dim(wide, x, jnp.minimum(col, pivot_devices - 1) * ncols, 1)
        return jnp.where(col < pivot_devices, wide, 0.0)

    pivot_units = PP // width

    def pivot_column(b):
        local = units[b] - col * per
        ok = (local >= 0) & (local < per) & (keeps[b] > 0)
        column = lax.dynamic_slice_in_dim(front, jnp.clip(local, 0, per - 1) * width, width, 1)
        body = [
            jnp.where(ok & (keeps[a] > 0), lax.dynamic_slice_in_dim(column, units[a] * width, width, 0), 0.0)
            for a in range(pivot_units)
        ]
        return jnp.concatenate(body, axis=0)

    corner = jnp.concatenate([pivot_column(b) for b in range(pivot_units)], axis=1)
    corner = corner + jnp.where(branch == 0, placed(parent_front[:PP]), 0.0)
    corner = halve(corner, "branch")

    def rows_for(target):
        return jnp.concatenate([unit_rows(target * per + a) for a in range(per)], axis=0)

    def moved(k, rows):
        pairs = [(c, c ^ k) for c in range(groups) if c >= pivot_devices]
        return lax.ppermute(rows, "col", pairs)

    near, far = list(range(1, ny)), list(reversed(range(ny, groups)))
    rows = {k: rows_for(col ^ k) for k in range(groups)}
    received = {0: rows[0]}
    for k in near:
        received[k] = moved(k, rows[k])

    z, y = col // ny, col % ny
    head = front[:P_SIZE]
    beside = [from_beside(head, "col", ny, j) for j in near]
    line, steps = line_gather(head, "col", ny, [(corner, [rows[k] for k in far])])
    corner = halve(corner, "col", gates=[head[:8]] + steps[2:])
    corner = join(corner, "col")

    def in_line(c, parts):
        return sum(jnp.where(z == (c // ny + k) % len(line), parts[k], 0.0) for k in range(len(line)))

    pivot_line = in_line(0, line)
    pivot_parts = [pivot_line] + [from_beside(pivot_line, "col", ny, j) for j in near]
    pivots = [
        sum(jnp.where(y == (c - j) % ny, pivot_parts[j], 0.0) for j in range(ny)) for c in range(pivot_devices)]
    pivots = jnp.concatenate(pivots, axis=1) if pivot_devices > 1 else pivots[0]

    for k in far[:EARLY]:
        row, _ = lax.optimization_barrier((rows[k], (steps[-1], corner, beside)))
        received[k] = moved(k, row)
    others = lax.optimization_barrier((jnp.stack(line[1:]), corner))[0]
    others = [from_beside(others, "col", ny, j) for j in near]
    gathered = line + [x for j in range(ny - 1) for x in [beside[j]] + [others[j][k] for k in range(len(line) - 1)]]
    slots = (source % ny - y) % ny * len(line) + (z - source // ny) % len(line)

    inverse = inverse_factor(pivots)
    for k in far[EARLY:]:
        row, _ = lax.optimization_barrier((rows[k], inverse))
        received[k] = moved(k, row)
    places = col ^ source
    child_mine = product(inverse, front[:P_SIZE], 1, 0)

    early = [received[k] for k in far[:EARLY - 1]]
    inverse, early = lax.optimization_barrier((inverse, early))
    received.update(zip(far, early))
    factor = jnp.stack([product(inverse, x, 1, 0) for x in gathered])

    def factor_columns(u):
        block = lax.dynamic_slice(factor, (slots[u], 0, parts[u] * width), (1, P_SIZE, width))
        return jnp.where(keeps[u] > 0, block[0], 0.0)

    mine = jnp.concatenate([factor_columns(col * per + a) for a in range(per)], axis=1)
    mine_keep = jnp.repeat(lax.dynamic_slice_in_dim(keeps, col * per, per), width)[:, None] > 0
    pieces = jnp.stack([jnp.where(mine_keep, received[k], 0.0) for k in range(groups)])
    left = three_part(mine)
    n = pivot_units
    first = spread_update(slots[:n], places[:n], parts[:n], keeps[:n], left, factor, pieces, width)
    first = jnp.concatenate([first[u] for u in range(n)], axis=1)
    steps = []
    first = first + jnp.where(branch == 0, parent_front[:PP].T, 0.0)
    first = join(halve(first, "branch", steps), "branch", steps)

    head = jnp.concatenate([factor_columns(u) for u in range(pivot_units)], axis=1)
    corner = corner - halve(product(head, head, 0, 0), "branch")
    corner, _ = lax.optimization_barrier((corner, received[far[-2]]))
    corner = join(corner, "branch")

    owned = units_total // branches
    spread = [None] * branches
    for i, m in enumerate(reversed(range(branches))):
        table, _ = lax.optimization_barrier((slots, steps[min(i, len(steps) - 1)]))
        at = lambda table: lax.dynamic_slice_in_dim(table, (branch ^ m) * owned, owned)
        spread[m] = spread_update(at(table), at(places), at(parts), at(keeps), left, factor, pieces, width)
    terms, sent = scatter_sum(spread, "branch")
    corner, _ = lax.optimization_barrier((corner, sent))
    parent_inverse = inverse_factor(corner)

    parent_mine = product(parent_inverse, first, 1, 1)
    if groups // ny == branches:
        line, parent_inverse = lax.optimization_barrier((share_line(first, ny), parent_inverse))
        sides = jnp.concatenate(share_beside(line, ny), axis=0)
    else:
        sides = lax.dynamic_slice_in_dim(
            lax.all_gather(first, "col"), branch * groups // branches, groups // branches, 0).reshape(nrows, PP)
    result = finish(parent_front, terms, sides, parent_inverse, parent_mine)
    return (child_mine[None], parent_mine, result)


def solution(mesh):
    in_specs = (P("branch", None, "col"), P("branch", None), P("branch", "col"))
    out_specs = (P("branch", None, "col"), P(None, "col"), P("branch", "col"))
    return jax.shard_map(
        on_device, mesh=mesh, in_specs=in_specs, out_specs=out_specs, check_vma=False
    )
```

```python
import jax
import jax.numpy as jnp
from jax import lax
from jax.experimental import pallas as pl
from jax.experimental.pallas import tpu as pltpu
from jax.sharding import PartitionSpec as P

BS = 256
P_SIZE = 512
NP = 4096
PP = 512
EARLY = 3

SUB = 8
LANES = 128
F32 = jnp.float32


def mm(a, b, ca, cb):
    return lax.dot_general(
        a, b, (((ca,), (cb,)), ((), ())),
        precision=lax.Precision.HIGHEST, preferred_element_type=F32,
    )


def factor_tile(rows):
    sub = lax.broadcasted_iota(jnp.int32, (SUB, LANES), 0)
    lane = lax.broadcasted_iota(jnp.int32, (SUB, LANES), 1)
    rows = list(rows)
    count = len(rows)
    spread = lambda column: jnp.broadcast_to(column, (SUB, LANES))
    for g in range(count):
        base = g * SUB
        inside = (lane >= base) & (lane < base + SUB)
        cols = [spread(rows[g][:, base + j:base + j + 1]) for j in range(SUB)]
        panel = jnp.where(inside, jnp.where(lane - base == sub, 1.0, 0.0), rows[g])
        kept = panel
        pivots = cols[0]
        for j in range(SUB):
            here = sub == j
            pivot = spread(cols[j][j:j + 1, :])
            inverse = 1.0 / pivot
            scaled = cols[j] * inverse
            row = spread(panel[j:j + 1, :])
            kept = jnp.where(here, panel, kept)
            pivots = jnp.where(here, pivot, pivots)
            panel = jnp.where(here, row * inverse, panel - scaled * row)
            for m in range(j + 1, SUB):
                across = spread(cols[m][j:j + 1, :])
                cols[m] = jnp.where(here, across * inverse, cols[m] - scaled * across)
        rows[g] = kept * lax.rsqrt(pivots)
        panel_rows = [spread(panel[j:j + 1, :]) for j in range(SUB)]
        for i in range(g + 1, count):
            terms = [spread(rows[i][:, base + j:base + j + 1]) * panel_rows[j] for j in range(SUB)]
            while len(terms) > 1:
                terms = [terms[t] + terms[t + 1] for t in range(0, len(terms), 2)]
            rows[i] = jnp.where(inside, 0.0, rows[i]) - terms[0]
    return rows


def inverse_factor_kernel(a_ref, w_ref):
    n = a_ref.shape[0]
    steps = n // LANES
    tri = (lax.broadcasted_iota(jnp.int32, (LANES, LANES), 0)
           >= lax.broadcasted_iota(jnp.int32, (LANES, LANES), 1))
    work = [[a_ref[i * LANES:(i + 1) * LANES, j * LANES:(j + 1) * LANES]
             for j in range(steps)] for i in range(steps)]
    for k in range(steps):
        tile = work[k][k]
        done = factor_tile([tile[g * SUB:(g + 1) * SUB, :] for g in range(LANES // SUB)])
        inv = jnp.where(tri, jnp.concatenate(done, axis=0), 0.0)
        work[k] = [inv if j == k else mm(inv, work[k][j], 1, 0) for j in range(steps)]
        for i in range(k + 1, steps):
            left = work[k][i]
            for j in range(steps):
                product = mm(left, work[k][j], 0, 0)
                work[i][j] = -product if j == k else work[i][j] - product
    for i in range(steps):
        for j in range(steps):
            value = work[i][j] if j <= i else jnp.zeros((LANES, LANES), F32)
            w_ref[i * LANES:(i + 1) * LANES, j * LANES:(j + 1) * LANES] = value


def inverse_factor(a):
    n = a.shape[0]
    return pl.pallas_call(
        inverse_factor_kernel,
        out_shape=jax.ShapeDtypeStruct((n, n), F32),
        in_specs=[pl.BlockSpec(memory_space=pltpu.VMEM)],
        out_specs=pl.BlockSpec(memory_space=pltpu.VMEM),
        compiler_params=pltpu.CompilerParams(vmem_limit_bytes=32 * 1024 * 1024),
        cost_estimate=pl.CostEstimate(flops=n * n * n, bytes_accessed=8 * n * n, transcendentals=0),
    )(a)


def spread_kernel(slot_ref, place_ref, part_ref, keep_ref, left_ref, factor_ref, piece_ref, out_ref):
    t = pl.program_id(0)
    whole = factor_ref[0]
    high = whole.astype(jnp.bfloat16)
    low = (whole - high.astype(F32)).astype(jnp.bfloat16)
    right = jnp.concatenate([high, low, high], axis=0)
    value = lax.dot_general(left_ref[...], right, (((1,), (0,)), ((), ())), preferred_element_type=F32)
    out_ref[0] = jnp.where(keep_ref[t] > 0, piece_ref[0] - value, 0.0)


def three_part(x):
    turned = x.T
    rounded = lax.reduce_precision(turned, 8, 7)
    high = rounded.astype(jnp.bfloat16)
    low = (turned - rounded).astype(jnp.bfloat16)
    return jnp.concatenate([high, high, low], axis=1)


def spread_update(slots, places, parts, keeps, left, factor, pieces, width):
    count = slots.shape[0]
    q, depth = left.shape[0], left.shape[1] // 3
    return pl.pallas_call(
        spread_kernel,
        grid_spec=pltpu.PrefetchScalarGridSpec(
            num_scalar_prefetch=4,
            grid=(count,),
            in_specs=[
                pl.BlockSpec((q, 3 * depth), lambda t, *refs: (0, 0)),
                pl.BlockSpec((1, depth, width), lambda t, s, p, h, k: (s[t], 0, h[t])),
                pl.BlockSpec((1, q, width), lambda t, s, p, h, k: (p[t], 0, h[t])),
            ],
            out_specs=pl.BlockSpec((1, q, width), lambda t, *refs: (t, 0, 0)),
        ),
        out_shape=jax.ShapeDtypeStruct((count, q, width), F32),
        compiler_params=pltpu.CompilerParams(vmem_limit_bytes=56 * 1024 * 1024),
        cost_estimate=pl.CostEstimate(
            flops=6 * count * q * depth * width,
            bytes_accessed=4 * count * width * (2 * q + depth), transcendentals=0),
    )(slots, places, parts, keeps, left, factor, pieces)


def product(a, b, ca, cb, precision=lax.Precision.HIGH):
    return lax.dot_general(a, b, (((ca,), (cb,)), ((), ())), precision=precision)


def flip(x, axis, bit):
    n = lax.axis_size(axis)
    return lax.ppermute(x, axis, [(i, i ^ bit) for i in range(n)])


def axis_bits(axis):
    return [1 << i for i in range(lax.axis_size(axis).bit_length() - 1)]


def halve(x, axis, steps=None, gates=()):
    me = lax.axis_index(axis)
    for step, bit in enumerate(axis_bits(axis)):
        if step < len(gates):
            x, _ = lax.optimization_barrier((x, gates[step]))
        high = (me // bit) % 2
        half = x.shape[0] // 2
        away = lax.dynamic_slice_in_dim(x, (1 - high) * half, half, 0)
        x = lax.dynamic_slice_in_dim(x, high * half, half, 0) + flip(away, axis, bit)
        if steps is not None:
            steps.append(x)
    return x


def join(x, axis, steps=None):
    me = lax.axis_index(axis)
    for bit in reversed(axis_bits(axis)):
        high = (me // bit) % 2
        other = flip(x, axis, bit)
        x = jnp.concatenate([jnp.where(high == 0, x, other), jnp.where(high == 0, other, x)], axis=0)
        if steps is not None:
            steps.append(x)
    return x


def scatter_sum(parts, axis):
    parts = list(parts)
    terms = [parts[0]]
    for bit in axis_bits(axis):
        for m in reversed(range(len(parts))):
            if m & bit and not m & (bit - 1):
                sent = parts[m]
                other = flip(sent, axis, bit)
                if m == bit:
                    terms.append(other)
                else:
                    parts[m ^ bit] = parts[m ^ bit] + other
    return terms, sent


def three_rows(x):
    high = x.astype(jnp.bfloat16)
    return high, (x - high.astype(F32)).astype(jnp.bfloat16)


def finish_kernel(parent_ref, side_ref, inverse_ref, mine_ref, *rest):
    terms, out_ref = rest[:-1], rest[-1]
    total = terms[0][0]
    for term in terms[1:]:
        total = total + term[0]
    dot = lambda a, b, cb: lax.dot_general(a, b, (((1,), (cb,)), ((), ())), preferred_element_type=F32)
    high, low = three_rows(side_ref[0])
    ihigh, ilow = three_rows(inverse_ref[...])
    factor = dot(jnp.concatenate([high, high, low], axis=1), jnp.concatenate([ihigh, ilow, ihigh], axis=1), 1)
    high, low = three_rows(factor)
    mhigh, mlow = three_rows(mine_ref[...])
    outer = dot(jnp.concatenate([high, high, low], axis=1), jnp.concatenate([mhigh, mlow, mhigh], axis=0), 0)
    out_ref[...] = parent_ref[...] + total.T - outer


def finish(parent, terms, sides, inverse, mine):
    count, q, width = terms[0].shape
    depth = inverse.shape[0]
    sides = sides.reshape(count, width, depth)
    whole = lambda t: (0, 0)
    block = lambda t: (t, 0, 0)
    return pl.pallas_call(
        finish_kernel,
        grid=(count,),
        in_specs=[
            pl.BlockSpec((width, q), lambda t: (t, 0)),
            pl.BlockSpec((1, width, depth), block),
            pl.BlockSpec((depth, depth), whole),
            pl.BlockSpec((depth, q), whole),
        ] + [pl.BlockSpec((1, q, width), block)] * len(terms),
        out_specs=pl.BlockSpec((width, q), lambda t: (t, 0)),
        out_shape=jax.ShapeDtypeStruct(parent.shape, F32),
        compiler_params=pltpu.CompilerParams(vmem_limit_bytes=48 * 1024 * 1024),
        cost_estimate=pl.CostEstimate(
            flops=6 * count * width * depth * (q + depth), bytes_accessed=8 * parent.size * 4, transcendentals=0),
    )(parent, sides, inverse, mine, *terms)


def line_gather(x, axis, ny, gates):
    n = lax.axis_size(axis)
    nz = n // ny
    up, down = [x], [x]
    for step in range(1, nz):
        ends = (up[-1], down[-1])
        if 1 < step < len(gates) + 2:
            ends, _ = lax.optimization_barrier((ends, gates[step - 2]))
        up.append(lax.ppermute(ends[0], axis, [(c, c + ny) for c in range(n) if step - 1 <= c // ny < nz - 1]))
        down.append(lax.ppermute(ends[1], axis, [(c, c - ny) for c in range(n) if 0 < c // ny <= nz - step]))
    return [x] + [up[k] + down[nz - k] for k in range(1, nz)], list(zip(up, down))


def from_beside(x, axis, ny, j):
    n = lax.axis_size(axis)
    return lax.ppermute(x, axis, [(c, c // ny * ny + (c % ny - j) % ny) for c in range(n)])


def share_line(x, ny):
    branches = lax.axis_size("branch")
    groups = lax.axis_size("col")
    nz = groups // ny
    place = lambda b, z, y: b * groups + z * ny + y
    got = jnp.where(lax.axis_index("col") // ny == lax.axis_index("branch"), x, 0.0)
    for off in range(1, nz):
        pairs = [(place(b, b, y), place(b, (b + off) % nz, y)) for b in range(branches) for y in range(ny)]
        got = got + lax.ppermute(x, ("branch", "col"), pairs)
    return got


def share_beside(got, ny):
    groups = lax.axis_size("col")
    y = lax.axis_index("col") % ny
    shares = [got]
    for j in range(1, ny):
        pairs = [(c, c // ny * ny + (c % ny - j) % ny) for c in range(groups)]
        shares.append(lax.ppermute(got, "col", pairs))
    return [sum(jnp.where(y == (i - j) % ny, shares[j], 0.0) for j in range(ny)) for i in range(ny)]


def on_device(child_fronts, extend_map, parent_front):
    front = child_fronts[0]
    order, ncols = front.shape
    nrows, pcols = parent_front.shape
    groups = lax.axis_size("col")
    branches = lax.axis_size("branch")
    ny = 1
    while 4 * ny * ny <= groups:
        ny *= 2
    nz = groups // ny
    width = min(BS, ncols)
    per = ncols // width
    ratio = BS // width
    units_total = NP // width
    col = lax.axis_index("col")
    branch = lax.axis_index("branch")
    pivot_devices = P_SIZE // ncols

    blocks = extend_map[0]
    hit = blocks[:, None] == jnp.arange(NP // BS, dtype=jnp.int32)[None, :]
    present = jnp.any(hit, axis=0).astype(jnp.int32)
    child_block = jnp.sum(
        jnp.where(hit, jnp.arange(blocks.shape[0], dtype=jnp.int32)[:, None], 0), axis=0
    ).astype(jnp.int32)
    t = jnp.arange(units_total, dtype=jnp.int32)
    units = P_SIZE // width + child_block[t // ratio] * ratio + t % ratio
    keeps = present[t // ratio]
    source = units // per
    parts = units % per

    def unit_rows(u):
        return lax.dynamic_slice_in_dim(front, units[u] * width, width, 0)

    def placed(x):
        if pivot_devices == 1:
            return jnp.where(col == 0, x, 0.0)
        wide = jnp.zeros((x.shape[0], P_SIZE), F32)
        wide = lax.dynamic_update_slice_in_dim(wide, x, jnp.minimum(col, pivot_devices - 1) * ncols, 1)
        return jnp.where(col < pivot_devices, wide, 0.0)

    pivot_units = PP // width

    def pivot_column(b):
        local = units[b] - col * per
        ok = (local >= 0) & (local < per) & (keeps[b] > 0)
        column = lax.dynamic_slice_in_dim(front, jnp.clip(local, 0, per - 1) * width, width, 1)
        body = [
            jnp.where(ok & (keeps[a] > 0), lax.dynamic_slice_in_dim(column, units[a] * width, width, 0), 0.0)
            for a in range(pivot_units)
        ]
        return jnp.concatenate(body, axis=0)

    corner = jnp.concatenate([pivot_column(b) for b in range(pivot_units)], axis=1)
    corner = corner + jnp.where(branch == 0, placed(parent_front[:PP]), 0.0)
    corner = halve(corner, "branch")

    def rows_for(target):
        return jnp.concatenate([unit_rows(target * per + a) for a in range(per)], axis=0)

    def moved(k, rows):
        pairs = [(c, c ^ k) for c in range(groups) if c >= pivot_devices]
        return lax.ppermute(rows, "col", pairs)

    near, far = list(range(1, ny)), list(reversed(range(ny, groups)))
    rows = {k: rows_for(col ^ k) for k in range(groups)}
    received = {0: rows[0]}
    for k in near:
        received[k] = moved(k, rows[k])

    z, y = col // ny, col % ny
    head = front[:P_SIZE]
    beside = [from_beside(head, "col", ny, j) for j in near]
    line, steps = line_gather(head, "col", ny, [(corner, [rows[k] for k in far])])
    halved = halve(corner, "col", gates=[head[:8]] + steps[2:])
    corner = join(halved, "col")

    def in_line(c, parts):
        return sum(jnp.where(z == (c // ny + k) % len(line), parts[k], 0.0) for k in range(len(line)))

    pivot_line = in_line(0, line)
    pivot_parts = [pivot_line] + [from_beside(pivot_line, "col", ny, j) for j in near]
    pivots = [
        sum(jnp.where(y == (c - j) % ny, pivot_parts[j], 0.0) for j in range(ny)) for c in range(pivot_devices)]
    pivots = jnp.concatenate(pivots, axis=1) if pivot_devices > 1 else pivots[0]

    for k in far[:EARLY]:
        row, _ = lax.optimization_barrier((rows[k], (steps[-1], halved, beside)))
        received[k] = moved(k, row)
    others, corner = lax.optimization_barrier((jnp.stack(line[1:]), corner))
    pivots, corner = lax.optimization_barrier((pivots, corner))
    others = [from_beside(others, "col", ny, j) for j in near]
    gathered = line + [x for j in range(ny - 1) for x in [beside[j]] + [others[j][k] for k in range(len(line) - 1)]]
    slots = (source % ny - y) % ny * len(line) + (z - source // ny) % len(line)

    inverse = inverse_factor(pivots)
    for k in far[EARLY:]:
        row, _ = lax.optimization_barrier((rows[k], inverse))
        received[k] = moved(k, row)
    places = col ^ source
    child_mine = product(inverse, front[:P_SIZE], 1, 0)

    early = [received[k] for k in far[:EARLY]]
    inverse, early = lax.optimization_barrier((inverse, early))
    received.update(zip(far[:EARLY], early))
    factor = jnp.stack([product(inverse, x, 1, 0) for x in gathered])

    def factor_columns(u):
        block = lax.dynamic_slice(factor, (slots[u], 0, parts[u] * width), (1, P_SIZE, width))
        return jnp.where(keeps[u] > 0, block[0], 0.0)

    mine = jnp.concatenate([factor_columns(col * per + a) for a in range(per)], axis=1)
    mine_keep = jnp.repeat(lax.dynamic_slice_in_dim(keeps, col * per, per), width)[:, None] > 0
    pieces = jnp.stack([jnp.where(mine_keep, received[k], 0.0) for k in range(groups)])
    left = three_part(mine)
    n = pivot_units
    first = spread_update(slots[:n], places[:n], parts[:n], keeps[:n], left, factor, pieces, width)
    first = jnp.concatenate([first[u] for u in range(n)], axis=1)
    steps = []
    first = first + jnp.where(branch == 0, parent_front[:PP].T, 0.0)
    first = join(halve(first, "branch", steps), "branch", steps)

    head = jnp.concatenate([factor_columns(u) for u in range(pivot_units)], axis=1)
    corner = corner - halve(product(head, head, 0, 0), "branch")
    corner, _ = lax.optimization_barrier((corner, received[far[-2]]))
    corner = join(corner, "branch")

    owned = units_total // branches
    spread = [None] * branches
    for i, m in enumerate(reversed(range(branches))):
        table, _ = lax.optimization_barrier((slots, steps[min(i, len(steps) - 1)]))
        at = lambda table: lax.dynamic_slice_in_dim(table, (branch ^ m) * owned, owned)
        spread[m] = spread_update(at(table), at(places), at(parts), at(keeps), left, factor, pieces, width)
    terms, sent = scatter_sum(spread, "branch")
    corner, _ = lax.optimization_barrier((corner, sent))
    parent_inverse = inverse_factor(corner)

    parent_mine = product(parent_inverse, first, 1, 1)
    if groups // ny == branches:
        line, parent_inverse = lax.optimization_barrier((share_line(first, ny), parent_inverse))
        sides = jnp.concatenate(share_beside(line, ny), axis=0)
    else:
        sides = lax.dynamic_slice_in_dim(
            lax.all_gather(first, "col"), branch * groups // branches, groups // branches, 0).reshape(nrows, PP)
    result = finish(parent_front, terms, sides, parent_inverse, parent_mine)
    return (child_mine[None], parent_mine, result)


def solution(mesh):
    in_specs = (P("branch", None, "col"), P("branch", None), P("branch", "col"))
    out_specs = (P("branch", None, "col"), P(None, "col"), P("branch", "col"))
    return jax.shard_map(
        on_device, mesh=mesh, in_specs=in_specs, out_specs=out_specs, check_vma=False
    )
```

```python
import jax
import jax.numpy as jnp
from jax import lax
from jax.experimental import pallas as pl
from jax.experimental.pallas import tpu as pltpu
from jax.sharding import PartitionSpec as P

BS = 256
P_SIZE = 512
NP = 4096
PP = 512
EARLY = 3

SUB = 8
LANES = 128
F32 = jnp.float32


def mm(a, b, ca, cb):
    return lax.dot_general(
        a, b, (((ca,), (cb,)), ((), ())),
        precision=lax.Precision.HIGHEST, preferred_element_type=F32,
    )


def factor_tile(rows):
    sub = lax.broadcasted_iota(jnp.int32, (SUB, LANES), 0)
    lane = lax.broadcasted_iota(jnp.int32, (SUB, LANES), 1)
    rows = list(rows)
    count = len(rows)
    spread = lambda column: jnp.broadcast_to(column, (SUB, LANES))
    for g in range(count):
        base = g * SUB
        inside = (lane >= base) & (lane < base + SUB)
        cols = [spread(rows[g][:, base + j:base + j + 1]) for j in range(SUB)]
        panel = jnp.where(inside, jnp.where(lane - base == sub, 1.0, 0.0), rows[g])
        kept = panel
        pivots = cols[0]
        for j in range(SUB):
            here = sub == j
            pivot = spread(cols[j][j:j + 1, :])
            inverse = 1.0 / pivot
            scaled = cols[j] * inverse
            row = spread(panel[j:j + 1, :])
            kept = jnp.where(here, panel, kept)
            pivots = jnp.where(here, pivot, pivots)
            panel = jnp.where(here, row * inverse, panel - scaled * row)
            for m in range(j + 1, SUB):
                across = spread(cols[m][j:j + 1, :])
                cols[m] = jnp.where(here, across * inverse, cols[m] - scaled * across)
        rows[g] = kept * lax.rsqrt(pivots)
        panel_rows = [spread(panel[j:j + 1, :]) for j in range(SUB)]
        for i in range(g + 1, count):
            terms = [spread(rows[i][:, base + j:base + j + 1]) * panel_rows[j] for j in range(SUB)]
            while len(terms) > 1:
                terms = [terms[t] + terms[t + 1] for t in range(0, len(terms), 2)]
            rows[i] = jnp.where(inside, 0.0, rows[i]) - terms[0]
    return rows


def inverse_factor_kernel(a_ref, w_ref):
    n = a_ref.shape[0]
    steps = n // LANES
    tri = (lax.broadcasted_iota(jnp.int32, (LANES, LANES), 0)
           >= lax.broadcasted_iota(jnp.int32, (LANES, LANES), 1))
    work = [[a_ref[i * LANES:(i + 1) * LANES, j * LANES:(j + 1) * LANES]
             for j in range(steps)] for i in range(steps)]
    for k in range(steps):
        tile = work[k][k]
        done = factor_tile([tile[g * SUB:(g + 1) * SUB, :] for g in range(LANES // SUB)])
        inv = jnp.where(tri, jnp.concatenate(done, axis=0), 0.0)
        work[k] = [inv if j == k else mm(inv, work[k][j], 1, 0) for j in range(steps)]
        for i in range(k + 1, steps):
            left = work[k][i]
            for j in range(steps):
                product = mm(left, work[k][j], 0, 0)
                work[i][j] = -product if j == k else work[i][j] - product
    for i in range(steps):
        for j in range(steps):
            value = work[i][j] if j <= i else jnp.zeros((LANES, LANES), F32)
            w_ref[i * LANES:(i + 1) * LANES, j * LANES:(j + 1) * LANES] = value


def inverse_factor(a):
    n = a.shape[0]
    return pl.pallas_call(
        inverse_factor_kernel,
        out_shape=jax.ShapeDtypeStruct((n, n), F32),
        in_specs=[pl.BlockSpec(memory_space=pltpu.VMEM)],
        out_specs=pl.BlockSpec(memory_space=pltpu.VMEM),
        compiler_params=pltpu.CompilerParams(vmem_limit_bytes=32 * 1024 * 1024),
        cost_estimate=pl.CostEstimate(flops=n * n * n, bytes_accessed=8 * n * n, transcendentals=0),
    )(a)


def spread_kernel(slot_ref, place_ref, part_ref, keep_ref, left_ref, factor_ref, piece_ref, out_ref):
    t = pl.program_id(0)
    whole = factor_ref[0]
    high = whole.astype(jnp.bfloat16)
    low = (whole - high.astype(F32)).astype(jnp.bfloat16)
    right = jnp.concatenate([high, low, high], axis=0)
    value = lax.dot_general(left_ref[...], right, (((1,), (0,)), ((), ())), preferred_element_type=F32)
    out_ref[0] = jnp.where(keep_ref[t] > 0, piece_ref[0] - value, 0.0)


def three_part(x):
    turned = x.T
    rounded = lax.reduce_precision(turned, 8, 7)
    high = rounded.astype(jnp.bfloat16)
    low = (turned - rounded).astype(jnp.bfloat16)
    return jnp.concatenate([high, high, low], axis=1)


def spread_update(slots, places, parts, keeps, left, factor, pieces, width):
    count = slots.shape[0]
    q, depth = left.shape[0], left.shape[1] // 3
    return pl.pallas_call(
        spread_kernel,
        grid_spec=pltpu.PrefetchScalarGridSpec(
            num_scalar_prefetch=4,
            grid=(count,),
            in_specs=[
                pl.BlockSpec((q, 3 * depth), lambda t, *refs: (0, 0)),
                pl.BlockSpec((1, depth, width), lambda t, s, p, h, k: (s[t], 0, h[t])),
                pl.BlockSpec((1, q, width), lambda t, s, p, h, k: (p[t], 0, h[t])),
            ],
            out_specs=pl.BlockSpec((1, q, width), lambda t, *refs: (t, 0, 0)),
        ),
        out_shape=jax.ShapeDtypeStruct((count, q, width), F32),
        compiler_params=pltpu.CompilerParams(vmem_limit_bytes=56 * 1024 * 1024),
        cost_estimate=pl.CostEstimate(
            flops=6 * count * q * depth * width,
            bytes_accessed=4 * count * width * (2 * q + depth), transcendentals=0),
    )(slots, places, parts, keeps, left, factor, pieces)


def product(a, b, ca, cb, precision=lax.Precision.HIGH):
    return lax.dot_general(a, b, (((ca,), (cb,)), ((), ())), precision=precision)


def flip(x, axis, bit):
    n = lax.axis_size(axis)
    return lax.ppermute(x, axis, [(i, i ^ bit) for i in range(n)])


def axis_bits(axis):
    return [1 << i for i in range(lax.axis_size(axis).bit_length() - 1)]


def halve(x, axis, steps=None, gates=()):
    me = lax.axis_index(axis)
    for step, bit in enumerate(axis_bits(axis)):
        if step < len(gates):
            x, _ = lax.optimization_barrier((x, gates[step]))
        high = (me // bit) % 2
        half = x.shape[0] // 2
        away = lax.dynamic_slice_in_dim(x, (1 - high) * half, half, 0)
        x = lax.dynamic_slice_in_dim(x, high * half, half, 0) + flip(away, axis, bit)
        if steps is not None:
            steps.append(x)
    return x


def join(x, axis, steps=None):
    me = lax.axis_index(axis)
    for bit in reversed(axis_bits(axis)):
        high = (me // bit) % 2
        other = flip(x, axis, bit)
        x = jnp.concatenate([jnp.where(high == 0, x, other), jnp.where(high == 0, other, x)], axis=0)
        if steps is not None:
            steps.append(x)
    return x


def scatter_sum(parts, axis):
    parts = list(parts)
    terms = [parts[0]]
    for bit in axis_bits(axis):
        for m in reversed(range(len(parts))):
            if m & bit and not m & (bit - 1):
                sent = parts[m]
                other = flip(sent, axis, bit)
                if m == bit:
                    terms.append(other)
                else:
                    parts[m ^ bit] = parts[m ^ bit] + other
    return terms, sent


def three_rows(x):
    high = x.astype(jnp.bfloat16)
    return high, (x - high.astype(F32)).astype(jnp.bfloat16)


def finish_kernel(parent_ref, side_ref, inverse_ref, mine_ref, *rest):
    terms, out_ref = rest[:-1], rest[-1]
    total = terms[0][0]
    for term in terms[1:]:
        total = total + term[0]
    dot = lambda a, b, cb: lax.dot_general(a, b, (((1,), (cb,)), ((), ())), preferred_element_type=F32)
    high, low = three_rows(side_ref[0])
    ihigh, ilow = three_rows(inverse_ref[...])
    factor = dot(jnp.concatenate([high, high, low], axis=1), jnp.concatenate([ihigh, ilow, ihigh], axis=1), 1)
    high, low = three_rows(factor)
    mhigh, mlow = three_rows(mine_ref[...])
    outer = dot(jnp.concatenate([high, high, low], axis=1), jnp.concatenate([mhigh, mlow, mhigh], axis=0), 0)
    out_ref[...] = parent_ref[...] + total.T - outer


def finish(parent, terms, sides, inverse, mine):
    count, q, width = terms[0].shape
    depth = inverse.shape[0]
    sides = sides.reshape(count, width, depth)
    whole = lambda t: (0, 0)
    block = lambda t: (t, 0, 0)
    return pl.pallas_call(
        finish_kernel,
        grid=(count,),
        in_specs=[
            pl.BlockSpec((width, q), lambda t: (t, 0)),
            pl.BlockSpec((1, width, depth), block),
            pl.BlockSpec((depth, depth), whole),
            pl.BlockSpec((depth, q), whole),
        ] + [pl.BlockSpec((1, q, width), block)] * len(terms),
        out_specs=pl.BlockSpec((width, q), lambda t: (t, 0)),
        out_shape=jax.ShapeDtypeStruct(parent.shape, F32),
        compiler_params=pltpu.CompilerParams(vmem_limit_bytes=48 * 1024 * 1024),
        cost_estimate=pl.CostEstimate(
            flops=6 * count * width * depth * (q + depth), bytes_accessed=8 * parent.size * 4, transcendentals=0),
    )(parent, sides, inverse, mine, *terms)


def line_gather(x, axis, ny, gates):
    n = lax.axis_size(axis)
    nz = n // ny
    up, down = [x], [x]
    for step in range(1, nz):
        ends = (up[-1], down[-1])
        if 1 < step < len(gates) + 2:
            ends, _ = lax.optimization_barrier((ends, gates[step - 2]))
        up.append(lax.ppermute(ends[0], axis, [(c, c + ny) for c in range(n) if step - 1 <= c // ny < nz - 1]))
        down.append(lax.ppermute(ends[1], axis, [(c, c - ny) for c in range(n) if 0 < c // ny <= nz - step]))
    return [x] + [up[k] + down[nz - k] for k in range(1, nz)], list(zip(up, down))


def from_beside(x, axis, ny, j):
    n = lax.axis_size(axis)
    return lax.ppermute(x, axis, [(c, c // ny * ny + (c % ny - j) % ny) for c in range(n)])


def share_line(x, ny):
    branches = lax.axis_size("branch")
    groups = lax.axis_size("col")
    nz = groups // ny
    place = lambda b, z, y: b * groups + z * ny + y
    got = jnp.where(lax.axis_index("col") // ny == lax.axis_index("branch"), x, 0.0)
    for off in range(1, nz):
        pairs = [(place(b, b, y), place(b, (b + off) % nz, y)) for b in range(branches) for y in range(ny)]
        got = got + lax.ppermute(x, ("branch", "col"), pairs)
    return got


def share_beside(got, ny):
    groups = lax.axis_size("col")
    y = lax.axis_index("col") % ny
    shares = [got]
    for j in range(1, ny):
        pairs = [(c, c // ny * ny + (c % ny - j) % ny) for c in range(groups)]
        shares.append(lax.ppermute(got, "col", pairs))
    return [sum(jnp.where(y == (i - j) % ny, shares[j], 0.0) for j in range(ny)) for i in range(ny)]


def on_device(child_fronts, extend_map, parent_front):
    front = child_fronts[0]
    order, ncols = front.shape
    nrows, pcols = parent_front.shape
    groups = lax.axis_size("col")
    branches = lax.axis_size("branch")
    ny = 1
    while 4 * ny * ny <= groups:
        ny *= 2
    nz = groups // ny
    width = min(BS, ncols)
    per = ncols // width
    ratio = BS // width
    units_total = NP // width
    col = lax.axis_index("col")
    branch = lax.axis_index("branch")
    pivot_devices = P_SIZE // ncols

    blocks = extend_map[0]
    hit = blocks[:, None] == jnp.arange(NP // BS, dtype=jnp.int32)[None, :]
    present = jnp.any(hit, axis=0).astype(jnp.int32)
    child_block = jnp.sum(
        jnp.where(hit, jnp.arange(blocks.shape[0], dtype=jnp.int32)[:, None], 0), axis=0
    ).astype(jnp.int32)
    t = jnp.arange(units_total, dtype=jnp.int32)
    units = P_SIZE // width + child_block[t // ratio] * ratio + t % ratio
    keeps = present[t // ratio]
    source = units // per
    parts = units % per

    def unit_rows(u):
        return lax.dynamic_slice_in_dim(front, units[u] * width, width, 0)

    def placed(x):
        if pivot_devices == 1:
            return jnp.where(col == 0, x, 0.0)
        wide = jnp.zeros((x.shape[0], P_SIZE), F32)
        wide = lax.dynamic_update_slice_in_dim(wide, x, jnp.minimum(col, pivot_devices - 1) * ncols, 1)
        return jnp.where(col < pivot_devices, wide, 0.0)

    pivot_units = PP // width

    def pivot_column(b):
        local = units[b] - col * per
        ok = (local >= 0) & (local < per) & (keeps[b] > 0)
        column = lax.dynamic_slice_in_dim(front, jnp.clip(local, 0, per - 1) * width, width, 1)
        body = [
            jnp.where(ok & (keeps[a] > 0), lax.dynamic_slice_in_dim(column, units[a] * width, width, 0), 0.0)
            for a in range(pivot_units)
        ]
        return jnp.concatenate(body, axis=0)

    corner = jnp.concatenate([pivot_column(b) for b in range(pivot_units)], axis=1)
    corner = corner + jnp.where(branch == 0, placed(parent_front[:PP]), 0.0)
    corner = halve(corner, "branch")

    def rows_for(target):
        return jnp.concatenate([unit_rows(target * per + a) for a in range(per)], axis=0)

    def moved(k, rows):
        pairs = [(c, c ^ k) for c in range(groups) if c >= pivot_devices]
        return lax.ppermute(rows, "col", pairs)

    near, far = list(range(1, ny)), list(reversed(range(ny, groups)))
    rows = {k: rows_for(col ^ k) for k in range(groups)}
    received = {0: rows[0]}
    for k in near:
        received[k] = moved(k, rows[k])

    z, y = col // ny, col % ny
    head = front[:P_SIZE]
    beside = [from_beside(head, "col", ny, j) for j in near]
    line, steps = line_gather(head, "col", ny, [(corner, [rows[k] for k in far])])
    corner = halve(corner, "col", gates=[head[:8]] + steps[2:])
    corner = join(corner, "col")

    def in_line(c, parts):
        return sum(jnp.where(z == (c // ny + k) % len(line), parts[k], 0.0) for k in range(len(line)))

    pivot_line = in_line(0, line)
    pivot_parts = [pivot_line] + [from_beside(pivot_line, "col", ny, j) for j in near]
    pivots = [
        sum(jnp.where(y == (c - j) % ny, pivot_parts[j], 0.0) for j in range(ny)) for c in range(pivot_devices)]
    pivots = jnp.concatenate(pivots, axis=1) if pivot_devices > 1 else pivots[0]

    for k in far[:EARLY]:
        row, _ = lax.optimization_barrier((rows[k], (steps[-1], corner, beside)))
        received[k] = moved(k, row)
    others = lax.optimization_barrier((jnp.stack(line[1:]), corner))[0]
    others = [from_beside(others, "col", ny, j) for j in near]
    gathered = line + [x for j in range(ny - 1) for x in [beside[j]] + [others[j][k] for k in range(len(line) - 1)]]
    slots = (source % ny - y) % ny * len(line) + (z - source // ny) % len(line)

    inverse = inverse_factor(pivots)
    for k in far[EARLY:]:
        row, _ = lax.optimization_barrier((rows[k], inverse))
        received[k] = moved(k, row)
    places = col ^ source
    child_mine = product(inverse, front[:P_SIZE], 1, 0)

    early = [received[k] for k in far[:EARLY]]
    inverse, early = lax.optimization_barrier((inverse, early))
    received.update(zip(far[:EARLY], early))
    factor = jnp.stack([product(inverse, x, 1, 0) for x in gathered])

    def factor_columns(u):
        block = lax.dynamic_slice(factor, (slots[u], 0, parts[u] * width), (1, P_SIZE, width))
        return jnp.where(keeps[u] > 0, block[0], 0.0)

    mine = jnp.concatenate([factor_columns(col * per + a) for a in range(per)], axis=1)
    mine_keep = jnp.repeat(lax.dynamic_slice_in_dim(keeps, col * per, per), width)[:, None] > 0
    pieces = jnp.stack([jnp.where(mine_keep, received[k], 0.0) for k in range(groups)])
    left = three_part(mine)
    n = pivot_units
    first = spread_update(slots[:n], places[:n], parts[:n], keeps[:n], left, factor, pieces, width)
    first = jnp.concatenate([first[u] for u in range(n)], axis=1)
    steps = []
    first = first + jnp.where(branch == 0, parent_front[:PP].T, 0.0)
    first = join(halve(first, "branch", steps), "branch", steps)

    head = jnp.concatenate([factor_columns(u) for u in range(pivot_units)], axis=1)
    corner = corner - halve(product(head, head, 0, 0), "branch")
    corner, _ = lax.optimization_barrier((corner, received[far[-2]]))
    corner = join(corner, "branch")

    owned = units_total // branches
    spread = [None] * branches
    for i, m in enumerate(reversed(range(branches))):
        table, _ = lax.optimization_barrier((slots, steps[min(i, len(steps) - 1)]))
        at = lambda table: lax.dynamic_slice_in_dim(table, (branch ^ m) * owned, owned)
        spread[m] = spread_update(at(table), at(places), at(parts), at(keeps), left, factor, pieces, width)
    terms, sent = scatter_sum(spread, "branch")
    corner, _ = lax.optimization_barrier((corner, sent))
    parent_inverse = inverse_factor(corner)

    parent_mine = product(parent_inverse, first, 1, 1)
    if groups // ny == branches:
        sides = jnp.concatenate(share_beside(share_line(first, ny), ny), axis=0)
    else:
        sides = lax.dynamic_slice_in_dim(
            lax.all_gather(first, "col"), branch * groups // branches, groups // branches, 0).reshape(nrows, PP)
    result = finish(parent_front, terms, sides, parent_inverse, parent_mine)
    return (child_mine[None], parent_mine, result)


def solution(mesh):
    in_specs = (P("branch", None, "col"), P("branch", None), P("branch", "col"))
    out_specs = (P("branch", None, "col"), P(None, "col"), P("branch", "col"))
    return jax.shard_map(
        on_device, mesh=mesh, in_specs=in_specs, out_specs=out_specs, check_vma=False
    )
```
